32 devices in a mesh: rows: 16 (over z, y, core), sub: 2 (over x).
Axes of the slice: x: 2, y: 2, z: 4, core: 2. Of those that a mesh axis runs over, the one named last changes fastest.
Arguments:
- features: bfloat16 [131072, 512], P(('rows', 'sub')), may hold values from -16 to 16
- residual: float32 [131072, 128], P(('rows', 'sub')), may hold values from -6 to 6
- coefficients: float32 [131072, 128], P(('rows', 'sub')), may hold values from -6 to 6
- block_owner: int32 [2], replicated, may hold values from 0 to 31
- block_tiles: int32 [2, 4], replicated, may hold values from 0 to 31, as said below
Outputs:
- residual_out: float32 [131072, 128], P(('rows', 'sub'))
- coefficients_out: float32 [131072, 128], P(('rows', 'sub'))
The draws below stay inside these ranges and needn't reach their ends.
Inputs may be any that keep to these rules, and one draw needn't show every extreme that they name: `block_tiles`: in each step the tile numbers are distinct, and tiles 0 and 31 are among them.
All inputs are finite; a program needn't handle non-finite values.
Results may differ from the reference program's by a relative error of at most 0.0012.
Values may be sent and summed in bfloat16 or wider, within the bound.
No kernel may reach another device: no remote copies, remote signals or barrier semaphores. Data moves between devices by JAX's collectives and lax.ppermute only.
A program may use at most 128 MiB of HBM per device.

```python
import math
import jax
import jax.numpy as jnp
from jax import lax

F = 512
C = 128
BLOCK = 512
TILE = 128
STEPS = 2
ROWS_DEV = 4096
NROWS = 131072
DEVICES = 32


def draw_features(key, part):
    key = jax.random.fold_in(key, 11)
    latent_key, scale_key, random_key = jax.random.split(key, 3)
    latent_dims = 16
    latent = jax.random.normal(latent_key, (NROWS, latent_dims), jnp.float32)
    column_scale = jax.random.uniform(scale_key, (F,), jnp.float32, 0.8, 1.2)
    spread = 0.45
    random_part = jax.random.normal(random_key, (NROWS, F), jnp.float32)
    shared = jnp.tile(latent, (1, F // latent_dims))
    values = 1.1 * shared * column_scale[None, :] + spread * random_part
    return jnp.clip(values, -16.0, 16.0).astype(jnp.bfloat16)


def draw_block_tiles(key, part):
    key = jax.random.fold_in(key, 7)
    step_keys = jax.random.split(key, STEPS)
    tiles_dev = ROWS_DEV // TILE
    block_tiles = BLOCK // TILE

    def pick_tiles(one_key):
        first_key, second_key = jax.random.split(one_key)
        middle = jax.random.permutation(first_key, tiles_dev - 2)[:block_tiles - 2].astype(jnp.int32) + 1
        ends = jnp.array([0, tiles_dev - 1], dtype=jnp.int32)
        chosen = jnp.concatenate([ends, middle])
        order = jax.random.permutation(second_key, block_tiles)
        return chosen[order].astype(jnp.int32)
    return jax.vmap(pick_tiles)(step_keys)


def level_of(own_key, shape, pieces, least, largest):
    def one(dim, shards_of):
        draws = jax.random.uniform(jax.random.fold_in(jax.random.fold_in(own_key, 6), dim), (shards_of,), jnp.float32, least / len(pieces), largest / len(pieces))
        return jnp.repeat(jnp.exp(draws), shape[dim] // shards_of).reshape((-1,) + (1,) * (len(shape) - dim - 1))

    gain = one(*pieces[0])
    for cut in pieces[1:]:
        gain = gain * one(*cut)
    return gain


def normal_values(stream_key, shape, deviation, most, pieces=(), kind=jnp.bfloat16):
    loudness = level_of(stream_key, shape, pieces, -0.22, 0.18) if pieces else 1.0
    result = jax.random.normal(stream_key, shape, jnp.float32) * deviation * loudness
    return jnp.minimum(jnp.maximum(result, -most), most).astype(kind)


def setup_inputs(seed: int = 0) -> dict:
    key_of = jax.random.split(jax.random.key(seed), 6)
    features = draw_features(jax.random.fold_in(key_of[5], 71), 0)
    residual = normal_values(key_of[1], (NROWS, C), 1.0, 6.0, ((0, 32),), jnp.float32)
    coefficients = normal_values(key_of[2], (NROWS, C), 1.0, 6.0, ((0, 32),), jnp.float32)
    block_owner = jax.random.randint(key_of[3], (STEPS,), 0, DEVICES).astype(jnp.int32)
    block_tiles = draw_block_tiles(jax.random.fold_in(key_of[5], 71), 0)
    return {"features": features, "residual": residual, "coefficients": coefficients, "block_owner": block_owner, "block_tiles": block_tiles}


RIDGE = 0.5

def kernel_block(left_rows, right_rows, left_norm, right_norm, kernel_scale):
    cross_dot = jnp.dot(left_rows.astype(jnp.float32), right_rows.astype(jnp.float32).T)
    distance = left_norm[:, None] + right_norm[None, :] - 2.0 * cross_dot
    return jnp.exp(-kernel_scale * distance)

def block_solve(kernel_bb, gradient):
    size_now = kernel_bb.shape[0]
    system = kernel_bb + RIDGE * jnp.eye(size_now, dtype=jnp.float32)
    factor = jnp.linalg.cholesky(system)
    half_way = lax.linalg.triangular_solve(factor, gradient, left_side=True, lower=True)
    return lax.linalg.triangular_solve(factor, half_way, left_side=True, lower=True, transpose_a=True)

def reference(features, residual, coefficients, block_owner, block_tiles):
    devices = features.shape[0] // ROWS_DEV
    kernel_scale = 1.0 / F
    step_size = 1.0 / math.sqrt(ROWS_DEV * devices)
    shards = features.reshape(devices, ROWS_DEV, F)
    norms = lax.optimization_barrier(jnp.sum(jnp.square(features.astype(jnp.float32)), axis=1)).reshape(devices, ROWS_DEV)
    for step_index in range(STEPS):
        owner_now = block_owner[step_index]
        tile_ids = block_tiles[step_index]
        block_rows = shards[owner_now].reshape(ROWS_DEV // TILE, TILE, F)[tile_ids].reshape(BLOCK, F)
        block_norm = lax.optimization_barrier(jnp.sum(jnp.square(block_rows.astype(jnp.float32)), axis=1))
        weighted = (residual - RIDGE * coefficients).astype(jnp.bfloat16).reshape(devices, ROWS_DEV, C)

        def partial_term(inputs):
            shard_rows, shard_norm, shard_weight = inputs
            slab = kernel_block(shard_rows, block_rows, shard_norm, block_norm, kernel_scale).astype(jnp.bfloat16)
            return jnp.einsum('rb,rc->bc', slab.astype(jnp.float32), shard_weight.astype(jnp.float32))
        terms = lax.map(partial_term, (shards, norms, weighted))
        gradient = lax.optimization_barrier(jnp.sum(terms, axis=0))
        kernel_bb = kernel_block(block_rows, block_rows, block_norm, block_norm, kernel_scale)
        update = block_solve(kernel_bb, gradient) * step_size
        update_low = update.astype(jnp.bfloat16)

        def new_residual(inputs):
            shard_rows, shard_norm, shard_residual = inputs
            slab = kernel_block(shard_rows, block_rows, shard_norm, block_norm, kernel_scale).astype(jnp.bfloat16)
            return shard_residual - jnp.dot(slab.astype(jnp.float32), update_low.astype(jnp.float32))
        residual = lax.map(new_residual, (shards, norms, residual.reshape(devices, ROWS_DEV, C))).reshape(devices * ROWS_DEV, C)
        row_index = (owner_now * ROWS_DEV + tile_ids[:, None] * TILE + jnp.arange(TILE, dtype=jnp.int32)[None, :]).reshape(-1).astype(jnp.int32)
        coefficients = coefficients.at[row_index].add(update)
    return (residual, coefficients)
```

```python
import functools
import math

import jax
import jax.numpy as jnp
from jax import lax
from jax.experimental import pallas as pl
from jax.experimental.pallas import tpu as pltpu
from jax.sharding import PartitionSpec as P

BLOCK = 512
TILE = 128
STEPS = 2
RIDGE = 0.5
AXES = ("rows", "sub")
HIGH = lax.Precision.HIGHEST
NT = (((1,), (1,)), ((), ()))
LOG2E = math.log2(math.e)
VMEM_LIMIT = 24 * 1024 * 1024
SMALL_LIMIT = 12 * 1024 * 1024


def pick_kernel(tiles_ref, core_ref, feat_ref, keep_ref, send_ref, sems):
    per_half = keep_ref.shape[1] // TILE
    copies = []
    for turn, out in enumerate((keep_ref, send_ref)):
        half = core_ref[0] if turn == 0 else 1 - core_ref[0]
        for s in range(STEPS):
            for i in range(per_half):
                source = pl.multiple_of(tiles_ref[s, half * per_half + i] * TILE, TILE)
                copies.append(
                    pltpu.make_async_copy(
                        feat_ref.at[pl.ds(source, TILE), :],
                        out.at[s, pl.ds(i * TILE, TILE), :],
                        sems.at[turn, s, i],
                    )
                )
    for copy in copies:
        copy.start()
    for copy in copies:
        copy.wait()


def pick_halves(features, block_tiles, core):
    width = features.shape[1]
    half = jax.ShapeDtypeStruct((STEPS, BLOCK // 2, width), features.dtype)
    return pl.pallas_call(
        pick_kernel,
        grid_spec=pltpu.PrefetchScalarGridSpec(
            num_scalar_prefetch=2,
            grid=(1,),
            in_specs=[pl.BlockSpec(memory_space=pltpu.HBM)],
            out_specs=[pl.BlockSpec(half.shape, lambda i, *_: (0, 0, 0))] * 2,
            scratch_shapes=[pltpu.SemaphoreType.DMA((2, STEPS, BLOCK // 2 // TILE))],
        ),
        out_shape=(half, half),
        compiler_params=pltpu.CompilerParams(vmem_limit_bytes=SMALL_LIMIT),
        name="pick",
    )(block_tiles, core, pltpu.with_memory_space_constraint(features, pltpu.HBM))


def swap(value, axes, flip):
    return lax.ppermute(value, axes, [(i, i ^ flip) for i in range(lax.axis_size(axes))])


def bit_of(index, mask):
    return ((index & mask) != 0).astype(jnp.int32)


def swap_among(pick, me, axes, low, high):
    place = bit_of(me, low) + 2 * bit_of(me, high)
    flips = [0, low, high, low | high]
    return place, [swap(pick(place ^ c), axes, flips[c]) for c in (1, 2, 3)]


def ordered(parts, me, low, high, axis):
    one, two = (me & low) != 0, (me & high) != 0
    parts = [jnp.where(one, parts[c ^ 1], parts[c]) for c in range(4)]
    return jnp.stack([jnp.where(two, parts[c ^ 2], parts[c]) for c in range(4)], axis=axis)


def fetch_blocks(features, norms, block_owner, block_tiles, me, devices, core):
    width = features.shape[1]
    low, high = 1, 2 * core
    differs = lambda mask: (((block_owner ^ me) & mask) != 0)[:, None, None]
    on_core = (me & core) != 0

    keep, send = pick_halves(features, block_tiles, bit_of(me, core).reshape(1))
    half = jnp.where(differs(core), swap(send, AXES, core), keep)
    quarters = half.reshape(STEPS, 4, BLOCK // 8, width)
    pick = lambda place: lax.dynamic_index_in_dim(quarters, place, 1, False)
    place, got = swap_among(pick, me, AXES, low, high)
    part = jnp.where(
        differs(high),
        jnp.where(differs(low), got[2], got[1]),
        jnp.where(differs(low), got[0], pick(place)),
    )
    mask = 1
    while mask < devices:
        if mask not in (core, low, high):
            other = swap(part, AXES, mask)
            if mask == devices // 2:
                other, norms = lax.optimization_barrier((other, norms))
            part = jnp.where(differs(mask), other, part)
        mask *= 2
    _, got = swap_among(lambda place: part, me, AXES, low, high)
    half = ordered([part] + got, me, low, high, 1)
    other = swap(half, AXES, core)
    both = jnp.stack([jnp.where(on_core, other, half), jnp.where(on_core, half, other)], axis=1)
    return both.reshape(STEPS * BLOCK, width), norms


class Spread:
    def __init__(self, axes, core):
        self.axes, self.core = axes, core
        self.me = lax.axis_index(axes).astype(jnp.int32)
        self.near = [1 << b for b in range(3) if 1 << b != core]
        self.far = [1 << b for b in range(3, lax.axis_size(axes).bit_length() - 1)]
        self.count = 8
        self.core_axis = 2 - (core.bit_length() - 1)

    def core_sum(self, value):
        value = value.reshape((2,) * 3 + value.shape[1:])
        zero, one = (lax.index_in_dim(value, i, self.core_axis, False) for i in (0, 1))
        bit = (self.me & self.core) != 0
        value = jnp.where(bit, one, zero) + swap(jnp.where(bit, zero, one), self.axes, self.core)
        return value.reshape((4,) + value.shape[2:])

    def near_sum(self, value):
        pick = lambda place: lax.dynamic_index_in_dim(value, place, 0, False)
        place, got = swap_among(pick, self.me, self.axes, *self.near)
        return lambda got: pick(place) + got[0] + got[1] + got[2], got

    def far_sum(self, value, mask):
        return lambda got: value + got[0], [swap(value, self.axes, mask)]

    def near_gather(self, value):
        _, got = swap_among(lambda place: value, self.me, self.axes, *self.near)
        return lambda got: ordered([value] + got, self.me, *self.near, 0), got

    def core_gather(self, value):
        rest = value.shape[1:]
        value = value.reshape((2, 2) + rest)
        bit = (self.me & self.core) != 0
        got = swap(value, self.axes, self.core)
        value = jnp.stack([jnp.where(bit, got, value), jnp.where(bit, value, got)], axis=self.core_axis)
        return value.reshape((self.count,) + rest)


def scaled_norm(rows, scale):
    wide = rows.astype(jnp.float32)
    return jnp.sum(wide * wide, axis=1, keepdims=True) * scale


def gram_kernel(scale, core_ref, block_ref, own_ref, cross_ref):
    mine = block_ref[pl.ds(pl.multiple_of(core_ref[0] * BLOCK, BLOCK), BLOCK), :]
    eye = jnp.where(
        lax.broadcasted_iota(jnp.int32, (BLOCK, BLOCK), 0)
        == lax.broadcasted_iota(jnp.int32, (BLOCK, BLOCK), 1),
        RIDGE,
        0.0,
    )
    for left, right, shift, out in (
        (mine, mine, eye, own_ref),
        (block_ref[:BLOCK], block_ref[BLOCK:], 0.0, cross_ref),
    ):
        dots = lax.dot_general(left, right, NT, preferred_element_type=jnp.float32)
        right_norm = scaled_norm(right, scale)
        row = jnp.transpose(jnp.broadcast_to(right_norm, (BLOCK, 128)))[:1]
        value = jnp.exp(dots * (2.0 * scale) - scaled_norm(left, scale) - row)
        out[...] = (value + shift).astype(out.dtype)


def gram(block, core, scale):
    square = (BLOCK, BLOCK)
    whole = lambda shape: pl.BlockSpec(shape, lambda i, *_: (0, 0))
    return pl.pallas_call(
        functools.partial(gram_kernel, scale),
        grid_spec=pltpu.PrefetchScalarGridSpec(
            num_scalar_prefetch=1,
            grid=(1,),
            in_specs=[whole(block.shape)],
            out_specs=[whole(square)] * 2,
        ),
        out_shape=(jax.ShapeDtypeStruct(square, jnp.float32), jax.ShapeDtypeStruct(square, jnp.bfloat16)),
        compiler_params=pltpu.CompilerParams(vmem_limit_bytes=SMALL_LIMIT),
        cost_estimate=pl.CostEstimate(
            flops=2 * 2 * BLOCK**3, bytes_accessed=4 * BLOCK * BLOCK * 4, transcendentals=2 * BLOCK**2
        ),
        name="gram",
    )(core, block)


def slab_kernel(scale, chunk, block_ref, feat_ref, norm_ref, res_ref, coef_ref, slab_ref, piece_ref, bnorm, grad, cross):
    scale2 = scale * LOG2E
    norm = scaled_norm(block_ref[...], scale2)
    bnorm[...] = jnp.broadcast_to(norm, bnorm.shape)
    grad[...] = jnp.zeros_like(grad)
    cross[...] = jnp.zeros_like(cross)
    part = BLOCK // 2

    def body(i, _):
        rows = pl.ds(pl.multiple_of(i * chunk, chunk), chunk)
        weighted = (res_ref[rows, :] - RIDGE * coef_ref[rows, :]).astype(jnp.bfloat16)
        feat = feat_ref[rows, :]
        norm_row = norm_ref[:, rows] * LOG2E
        for p in range(STEPS * 2):
            at = slice(p * part, (p + 1) * part)
            dots = lax.dot_general(block_ref[at], feat, NT, preferred_element_type=jnp.float32)
            norm_wide = jnp.concatenate([bnorm[at]] * (chunk // bnorm.shape[1]), axis=1)
            slab = jnp.exp2(dots * (2.0 * scale2) - norm_wide - norm_row).astype(jnp.bfloat16)
            slab_ref[at, rows] = slab
            grad[at] += jnp.dot(slab, weighted, preferred_element_type=jnp.float32)
        cross[...] += lax.dot_general(
            slab_ref[:BLOCK, rows], slab_ref[BLOCK:, rows], NT, preferred_element_type=jnp.float32
        )
        return 0

    lax.fori_loop(0, feat_ref.shape[0] // chunk, body, 0)
    grads = jnp.transpose(grad[...])
    groups = piece_ref.shape[0]
    own, depth = grads.shape[0] // groups, BLOCK // groups
    for d in range(groups):
        for s in range(STEPS):
            piece_ref[d, s * own : (s + 1) * own] = grads[d * own : (d + 1) * own, s * BLOCK : (s + 1) * BLOCK]
        piece_ref[d, STEPS * own :] = cross[d * depth : (d + 1) * depth]


def in_vmem(value):
    return pltpu.with_memory_space_constraint(value, pltpu.VMEM)


def slabs(block, features, norms, residual, coefficients, scale, groups, chunk=512):
    rows, width = features.shape
    targets = residual.shape[1]
    both = STEPS * BLOCK
    piece = (groups, STEPS * targets // groups + BLOCK // groups, BLOCK)
    return pl.pallas_call(
        functools.partial(slab_kernel, scale, chunk),
        out_shape=(pltpu.VMEM((both, rows), jnp.bfloat16), jax.ShapeDtypeStruct(piece, jnp.float32)),
        scratch_shapes=[
            pltpu.VMEM((both, 128), jnp.float32),
            pltpu.VMEM((both, targets), jnp.float32),
            pltpu.VMEM((BLOCK, BLOCK), jnp.float32),
        ],
        compiler_params=pltpu.CompilerParams(vmem_limit_bytes=VMEM_LIMIT),
        cost_estimate=pl.CostEstimate(
            flops=2 * rows * both * (width + targets + BLOCK // 2),
            bytes_accessed=rows * (width * 2 + targets * 8 + both * 2),
            transcendentals=rows * both,
        ),
        name="slabs",
    )(block, in_vmem(features), norms, in_vmem(residual), in_vmem(coefficients))


def reciprocal(x):
    guess = pl.reciprocal(x, approx=True)
    return guess * (2.0 - x * guess)


def eliminate(tiles, t, lane, scaled_ref):
    start, shape = 8 * t, tiles[t].shape
    wide = lambda tile, k: jnp.broadcast_to(tile[:, start + k : start + k + 1], shape)
    rows = [jnp.broadcast_to(tiles[t][k : k + 1], shape) for k in range(8)]
    at = {(i, k): wide(rows[i], k) for i in range(8) for k in range(i, 8)}
    units = [jnp.where(lane == start + k, 1.0, 0.0) for k in range(8)]
    rows = [row + unit for row, unit in zip(rows, units)]
    total, lower = [None] * 8, {}
    for r in range(0, 8, 2):
        p, m, q = at[r, r], at[r, r + 1], at[r + 1, r + 1]
        inverse = reciprocal(p * q - m * m)
        p, m, q = p * inverse, m * inverse, q * inverse
        for k in range(r + 2, 8):
            first = q * at[r, k] - m * at[r + 1, k]
            second = p * at[r + 1, k] - m * at[r, k]
            lower[r, k], lower[r + 1, k] = first, second
            for i in range(r + 2, k + 1):
                at[i, k] = at[i, k] - (at[r, i] * first + at[r + 1, i] * second)
            rows[k] = rows[k] - (first * rows[r] + second * rows[r + 1])
        total[r] = q * rows[r] - m * rows[r + 1]
        total[r + 1] = p * rows[r + 1] - m * rows[r]
    for r in (4, 2, 0):
        for k in range(r + 2, 8):
            total[r] = total[r] - lower[r, k] * total[k]
            total[r + 1] = total[r + 1] - lower[r + 1, k] * total[k]
    for k in range(8):
        scaled_ref[start + k : start + k + 1] = total[k][:1] - units[k][:1]
    for u in range(t + 1, len(tiles)):
        parts = [wide(tiles[u], k) * total[k] for k in range(8)]
        while len(parts) > 1:
            parts = [x + y for x, y in zip(parts[::2], parts[1::2])]
        tiles[u] = tiles[u] - parts[0]


def factor_kernel(index, copies, *refs):
    refs = list(refs)
    rest_ref = refs.pop(0)
    if copies:
        source, scaled, sem = refs.pop(0), refs[-2], refs[-1]
        copy = pltpu.make_async_copy(source, refs[-3], sem)
        copy.start()
    else:
        scaled = refs[-1]
    last = rest_ref.shape[0] == TILE
    factor_ref = refs[0] if last else refs[1]
    here = slice(index * TILE, (index + 1) * TILE)
    row_ids = lax.broadcasted_iota(jnp.int32, (TILE, TILE), 0)
    col_ids = lax.broadcasted_iota(jnp.int32, (TILE, TILE), 1)
    lane = lax.broadcasted_iota(jnp.int32, (8, TILE), 1)
    tiles = [rest_ref[8 * t : 8 * t + 8, here] for t in range(TILE // 8)]
    for t in range(TILE // 8):
        eliminate(tiles, t, lane, scaled)
    start = row_ids - row_ids % 8
    dot = functools.partial(lax.dot_general, precision=HIGH, preferred_element_type=jnp.float32)
    lower = jnp.where(col_ids < start, jnp.concatenate(tiles, axis=0), 0.0)
    lower = lower + jnp.where(col_ids == row_ids, 1.0, 0.0)
    right = jnp.where(col_ids < start + 8, scaled[...], 0.0)
    inv = dot(lower, right, (((0,), (0,)), ((), ())))
    top = rest_ref[:TILE]
    panel = dot(inv, top, (((1,), (0,)), ((), ())))
    inside = lax.broadcasted_iota(jnp.int32, panel.shape, 1) // TILE == index
    panel = jnp.where(inside, jnp.concatenate([inv] * (BLOCK // TILE), axis=1), panel)
    factor_ref[:TILE] = top
    factor_ref[TILE:] = panel
    if not last:
        under = rest_ref[TILE:]
        change = dot(rest_ref[TILE:, here], panel, (((1,), (0,)), ((), ())))
        inside = lax.broadcasted_iota(jnp.int32, under.shape, 1) // TILE == index
        refs[0][...] = jnp.where(inside, 0.0, under) - change
    if copies:
        copy.wait()


def factor_step(rest, index, copied=None):
    left = rest.shape[0] - TILE
    vmem, hbm = pl.BlockSpec(memory_space=pltpu.VMEM), pl.BlockSpec(memory_space=pltpu.HBM)
    out = [jax.ShapeDtypeStruct((left, BLOCK), jnp.float32)] if left else []
    out.append(jax.ShapeDtypeStruct((2 * TILE, BLOCK), jnp.float32))
    inputs, in_specs, out_specs = [rest], [vmem], [vmem] * len(out)
    scratch = [pltpu.VMEM((TILE, TILE), jnp.float32)]
    if copied is not None:
        inputs.append(pltpu.with_memory_space_constraint(copied, pltpu.HBM))
        in_specs.append(hbm)
        out.append(pltpu.HBM(copied.shape, copied.dtype))
        out_specs.append(hbm)
        scratch.append(pltpu.SemaphoreType.DMA)
    out = pl.pallas_call(
        functools.partial(factor_kernel, index, copied is not None),
        in_specs=in_specs,
        out_specs=tuple(out_specs),
        out_shape=tuple(out),
        scratch_shapes=scratch,
        compiler_params=pltpu.CompilerParams(vmem_limit_bytes=SMALL_LIMIT),
        cost_estimate=pl.CostEstimate(flops=6 * 10**9, bytes_accessed=4 * 1024 * 1024, transcendentals=0),
        name="factor",
    )(*inputs)
    out = list(out)
    below = out.pop(0) if left else None
    return (below,) + tuple(out)


def apply_inverse(value, refs):
    ids = lambda axis: lax.broadcasted_iota(jnp.int32, (TILE, BLOCK), axis)
    lower, right = [], []
    for k in range(BLOCK // TILE):
        rest, panel = refs[k][:TILE], refs[k][TILE:]
        unit = jnp.where(ids(1) == ids(0) + k * TILE, 1.0, 0.0)
        lower.append(jnp.where(ids(1) < k * TILE, rest, unit))
        right.append(jnp.where(ids(1) < (k + 1) * TILE, panel, 0.0))
    lower, right = jnp.concatenate(lower, axis=0), jnp.concatenate(right, axis=0)
    middle = lax.dot_general(value, right, NT, precision=HIGH, preferred_element_type=jnp.float32)
    return jnp.dot(middle, lower, precision=HIGH, preferred_element_type=jnp.float32)


def first_kernel(step_size, grad_ref, *refs):
    refs[-1][...] = apply_inverse(grad_ref[: refs[-1].shape[0]], refs[:-1]) * step_size


def second_kernel(step_size, grad_ref, first_ref, cross_ref, gram_ref, *refs):
    out_ref = refs[-1]
    first = first_ref[...]
    own = first.shape[0]
    again = (
        grad_ref[own:]
        - jnp.dot(first.astype(jnp.bfloat16), cross_ref[...], preferred_element_type=jnp.float32)
        - RIDGE * jnp.dot(first, gram_ref[...].astype(jnp.float32), precision=HIGH, preferred_element_type=jnp.float32)
    )
    out_ref[:own] = first.astype(out_ref.dtype)
    out_ref[own:] = (apply_inverse(again, refs[:-1]) * step_size).astype(out_ref.dtype)


def solve(kernel, out, arrays, factors, step_size):
    whole = lambda value: pl.BlockSpec(value.shape, lambda i: (0,) * len(value.shape))
    return pl.pallas_call(
        functools.partial(kernel, step_size),
        grid=(1,),
        in_specs=[whole(value) for value in list(arrays) + list(factors)],
        out_specs=whole(out),
        out_shape=out,
        compiler_params=pltpu.CompilerParams(vmem_limit_bytes=SMALL_LIMIT),
        cost_estimate=pl.CostEstimate(flops=10**9, bytes_accessed=3 * 1024 * 1024, transcendentals=0),
        name=kernel.__name__[:-7],
    )(*arrays, *factors)


def final_kernel(chunk, owner_ref, tiles_ref, me_ref, gathered_ref, slab_ref, res_ref, coef_ref, base_ref, res_out, coef_out, upd_ref, res_buf, tile_buf, res_sems, tile_sems):
    rows, targets = res_ref.shape
    groups, own2 = gathered_ref.shape[0], gathered_ref.shape[1]
    own = own2 // STEPS
    count = BLOCK // TILE
    flat = gathered_ref[...].reshape(groups * own2, BLOCK)
    target = lax.broadcasted_iota(jnp.int32, (targets, groups * own2), 0)
    place = lax.broadcasted_iota(jnp.int32, (targets, groups * own2), 1)
    wanted = target // own * own2 + target % own
    for s in range(STEPS):
        pick = jnp.where(place == wanted + s * own, 1.0, 0.0).astype(jnp.bfloat16)
        chosen = jnp.dot(pick, flat, preferred_element_type=jnp.float32)
        upd_ref[:, s * BLOCK : (s + 1) * BLOCK] = chosen.astype(jnp.bfloat16)

    def change_of(s, k):
        at = s * BLOCK + k * TILE
        return jnp.transpose(upd_ref[:, at : at + TILE].astype(jnp.float32))

    def tile_rows(s, k):
        return pl.ds(pl.multiple_of(tiles_ref[s, k] * TILE, TILE), TILE)

    def tile_copy(s, k):
        return pltpu.make_async_copy(tile_buf.at[s, k], coef_out.at[tile_rows(s, k), :], tile_sems.at[s, k])

    owned = [owner_ref[s] == me_ref[0] for s in range(STEPS)]

    def writes(s, k):
        kept = owned[s]
        for later in range(s + 1, STEPS):
            for j in range(count):
                kept = kept & jnp.logical_not(owned[later] & (tiles_ref[later, j] == tiles_ref[s, k]))
        return kept

    for s in range(STEPS):
        for k in range(count):

            @pl.when(writes(s, k))
            def _():
                tile_buf[s, k] = coef_ref[tile_rows(s, k), :] + change_of(s, k)
                for earlier in range(s):
                    for j in range(count):

                        @pl.when(owned[earlier] & (tiles_ref[earlier, j] == tiles_ref[s, k]))
                        def _():
                            tile_buf[s, k] += change_of(earlier, j)

                tile_copy(s, k).start()

    def res_copy(i):
        at = pl.ds(pl.multiple_of(i * chunk, chunk), chunk)
        return pltpu.make_async_copy(res_buf.at[at, :], res_out.at[at, :], res_sems.at[i])

    def body(i, _):
        at = pl.ds(pl.multiple_of(i * chunk, chunk), chunk)
        change = jnp.dot(upd_ref[...], slab_ref[:, at], preferred_element_type=jnp.float32)
        res_buf[at, :] = res_ref[at, :] - jnp.transpose(change)
        res_copy(i).start()
        return 0

    lax.fori_loop(0, rows // chunk, body, 0)
    for i in range(rows // chunk):
        res_copy(i).wait()
    for s in range(STEPS):
        for k in range(count):

            @pl.when(writes(s, k))
            def _():
                tile_copy(s, k).wait()


def finish(owner, tiles, me, gathered, slab, residual, coefficients, base, chunk=512):
    rows, targets = residual.shape
    both = STEPS * BLOCK
    count = BLOCK // TILE
    smem, vmem, hbm = (pl.BlockSpec(memory_space=space) for space in (pltpu.SMEM, pltpu.VMEM, pltpu.HBM))
    return pl.pallas_call(
        functools.partial(final_kernel, chunk),
        in_specs=[smem] * 3 + [vmem] * 4 + [hbm],
        out_specs=(hbm, hbm),
        out_shape=(
            pltpu.HBM(residual.shape, jnp.float32),
            pltpu.HBM(residual.shape, jnp.float32),
        ),
        scratch_shapes=[
            pltpu.VMEM((targets, both), jnp.bfloat16),
            pltpu.VMEM((rows, targets), jnp.float32),
            pltpu.VMEM((STEPS, count, TILE, targets), jnp.float32),
            pltpu.SemaphoreType.DMA((rows // chunk,)),
            pltpu.SemaphoreType.DMA((STEPS, count)),
        ],
        input_output_aliases={7: 1},
        compiler_params=pltpu.CompilerParams(vmem_limit_bytes=VMEM_LIMIT),
        cost_estimate=pl.CostEstimate(
            flops=2 * rows * both * targets, bytes_accessed=rows * (both * 2 + targets * 16), transcendentals=0
        ),
        name="finish",
    )(owner, tiles, me, gathered, in_vmem(slab), in_vmem(residual), in_vmem(coefficients), base)


def local(features, residual, coefficients, block_owner, block_tiles):
    rows_dev, width = features.shape
    targets = residual.shape[1]
    sub_count = lax.axis_size("sub")
    devices = lax.axis_size("rows") * sub_count
    me = lax.axis_index(AXES).astype(jnp.int32)
    scale = 1.0 / width
    step_size = 1.0 / math.sqrt(rows_dev * devices)
    spread = Spread(AXES, sub_count) if devices <= 32 else Spread(("rows",), 1)
    groups = spread.count
    own = targets // groups

    wide = features.astype(jnp.float32)
    norms = (jnp.sum(wide * wide, axis=1) * scale).reshape(1, rows_dev)
    block, norms = fetch_blocks(features, norms, block_owner, block_tiles, me, devices, sub_count)
    slab, pieces = slabs(block, features, norms, residual, coefficients, scale, groups)
    if spread.axes != AXES:
        pieces = lax.psum(pieces, "sub")
    core = bit_of(me, sub_count)
    rest, gram12 = gram(block, core.reshape(1), scale)
    factors, base = ([], []), None

    def beside(hop, index, rest):
        then, got = hop
        below, mine, *copied = factor_step(rest, index, coefficients if index == 0 else None)
        got, below, mine = lax.optimization_barrier((got, below, mine))
        other = swap(mine, AXES, sub_count)
        factors[0].append(jnp.where(core != 0, other, mine))
        factors[1].append(jnp.where(core != 0, mine, other))
        return then(got), below, copied

    value = spread.core_sum(pieces)
    value, rest, (base,) = beside(spread.near_sum(value), 0, rest)
    for index, mask in enumerate(spread.far):
        value, rest, _ = beside(spread.far_sum(value, mask), 1 + index, rest)
    cross = value[STEPS * own :].astype(jnp.bfloat16)
    cross, rest, _ = beside(spread.near_gather(cross), 3, rest)
    cross = spread.core_gather(cross)
    grads = value[: STEPS * own]
    first = jax.ShapeDtypeStruct((own, BLOCK), jnp.float32)
    first = solve(first_kernel, first, [grads], factors[0], step_size)
    cross, first = lax.optimization_barrier((cross, first))
    update = jax.ShapeDtypeStruct(grads.shape, jnp.bfloat16)
    update = solve(
        second_kernel, update, [grads, first, cross.reshape(BLOCK, BLOCK), gram12], factors[1], step_size
    )
    then, got = spread.near_gather(update)
    gathered = spread.core_gather(then(got))
    return finish(block_owner, block_tiles, me.reshape(1), gathered, slab, residual, coefficients, base)


def solution(mesh):
    row_spec = P(AXES, None)
    return jax.shard_map(
        local,
        mesh=mesh,
        in_specs=(row_spec, row_spec, row_spec, P(), P()),
        out_specs=(row_spec, row_spec),
        check_vma=False,
    )
```

```python
import functools
import math

import jax
import jax.numpy as jnp
from jax import lax
from jax.experimental import pallas as pl
from jax.experimental.pallas import tpu as pltpu
from jax.sharding import PartitionSpec as P

BLOCK = 512
TILE = 128
STEPS = 2
RIDGE = 0.5
AXES = ("rows", "sub")
HIGH = lax.Precision.HIGHEST
NT = (((1,), (1,)), ((), ()))
LOG2E = math.log2(math.e)
VMEM_LIMIT = 16 * 1024 * 1024
SMALL_LIMIT = 12 * 1024 * 1024


def pick_kernel(tiles_ref, core_ref, feat_ref, keep_ref, send_ref, sems):
    per_half = keep_ref.shape[1] // TILE
    copies = []
    for turn, out in enumerate((keep_ref, send_ref)):
        half = core_ref[0] if turn == 0 else 1 - core_ref[0]
        for s in range(STEPS):
            for i in range(per_half):
                source = pl.multiple_of(tiles_ref[s, half * per_half + i] * TILE, TILE)
                copies.append(
                    pltpu.make_async_copy(
                        feat_ref.at[pl.ds(source, TILE), :],
                        out.at[s, pl.ds(i * TILE, TILE), :],
                        sems.at[turn, s, i],
                    )
                )
    for copy in copies:
        copy.start()
    for copy in copies:
        copy.wait()


def pick_halves(features, block_tiles, core):
    width = features.shape[1]
    half = jax.ShapeDtypeStruct((STEPS, BLOCK // 2, width), features.dtype)
    return pl.pallas_call(
        pick_kernel,
        grid_spec=pltpu.PrefetchScalarGridSpec(
            num_scalar_prefetch=2,
            grid=(1,),
            in_specs=[pl.BlockSpec(memory_space=pltpu.HBM)],
            out_specs=[pl.BlockSpec(half.shape, lambda i, *_: (0, 0, 0))] * 2,
            scratch_shapes=[pltpu.SemaphoreType.DMA((2, STEPS, BLOCK // 2 // TILE))],
        ),
        out_shape=(half, half),
        compiler_params=pltpu.CompilerParams(vmem_limit_bytes=SMALL_LIMIT),
        name="pick",
    )(block_tiles, core, pltpu.with_memory_space_constraint(features, pltpu.HBM))


def swap(value, axes, flip):
    return lax.ppermute(value, axes, [(i, i ^ flip) for i in range(lax.axis_size(axes))])


def bit_of(index, mask):
    return ((index & mask) != 0).astype(jnp.int32)


def swap_among(pick, me, axes, low, high):
    place = bit_of(me, low) + 2 * bit_of(me, high)
    flips = [0, low, high, low | high]
    return place, [swap(pick(place ^ c), axes, flips[c]) for c in (1, 2, 3)]


def ordered(parts, me, low, high, axis):
    one, two = (me & low) != 0, (me & high) != 0
    parts = [jnp.where(one, parts[c ^ 1], parts[c]) for c in range(4)]
    return jnp.stack([jnp.where(two, parts[c ^ 2], parts[c]) for c in range(4)], axis=axis)


def fetch_blocks(features, norms, block_owner, block_tiles, me, devices, core):
    width = features.shape[1]
    low, high = 1, 2 * core
    differs = lambda mask: (((block_owner ^ me) & mask) != 0)[:, None, None]
    on_core = (me & core) != 0

    keep, send = pick_halves(features, block_tiles, bit_of(me, core).reshape(1))
    half = jnp.where(differs(core), swap(send, AXES, core), keep)
    quarters = half.reshape(STEPS, 4, BLOCK // 8, width)
    pick = lambda place: lax.dynamic_index_in_dim(quarters, place, 1, False)
    place, got = swap_among(pick, me, AXES, low, high)
    part = jnp.where(
        differs(high),
        jnp.where(differs(low), got[2], got[1]),
        jnp.where(differs(low), got[0], pick(place)),
    )
    mask = 1
    while mask < devices:
        if mask not in (core, low, high):
            other = swap(part, AXES, mask)
            if mask == devices // 2:
                other, norms = lax.optimization_barrier((other, norms))
            part = jnp.where(differs(mask), other, part)
        mask *= 2
    _, got = swap_among(lambda place: part, me, AXES, low, high)
    half = ordered([part] + got, me, low, high, 1)
    other = swap(half, AXES, core)
    both = jnp.stack([jnp.where(on_core, other, half), jnp.where(on_core, half, other)], axis=1)
    return both.reshape(STEPS * BLOCK, width), norms


def pack(value, exact):
    high = lax.reduce_precision(value[..., :exact, :], 8, 7)
    low = value[..., :exact, :] - high
    return jnp.concatenate([part.astype(jnp.bfloat16) for part in (high, low, value[..., exact:, :])], axis=-2)


def unpack(value, exact):
    value = value.astype(jnp.float32)
    return jnp.concatenate([value[..., :exact, :] + value[..., exact : 2 * exact, :], value[..., 2 * exact :, :]], axis=-2)


class Spread:
    def __init__(self, axes, core):
        self.axes, self.core = axes, core
        self.me = lax.axis_index(axes).astype(jnp.int32)
        self.near = [1 << b for b in range(3) if 1 << b != core]
        self.far = [1 << b for b in range(3, lax.axis_size(axes).bit_length() - 1)]
        self.count = 8
        self.core_axis = 2 - (core.bit_length() - 1)

    def core_sum(self, value):
        value = value.reshape((2,) * 3 + value.shape[1:])
        zero, one = (lax.index_in_dim(value, i, self.core_axis, False) for i in (0, 1))
        bit = (self.me & self.core) != 0
        value = jnp.where(bit, one, zero) + swap(jnp.where(bit, zero, one), self.axes, self.core)
        return value.reshape((4,) + value.shape[2:])

    def near_sum(self, value, exact):
        packed = pack(value, exact)
        pick = lambda array, place: lax.dynamic_index_in_dim(array, place, 0, False)
        place, got = swap_among(lambda place: pick(packed, place), self.me, self.axes, *self.near)
        return lambda got: pick(value, place) + unpack(got[0], exact) + unpack(got[1], exact) + unpack(got[2], exact), got

    def far_sum(self, value, exact, mask):
        return lambda got: value + unpack(got[0], exact), [swap(pack(value, exact), self.axes, mask)]

    def near_gather(self, value):
        _, got = swap_among(lambda place: value, self.me, self.axes, *self.near)
        return lambda got: ordered([value] + got, self.me, *self.near, 0), got

    def core_gather(self, value):
        rest = value.shape[1:]
        value = value.reshape((2, 2) + rest)
        bit = (self.me & self.core) != 0
        got = swap(value, self.axes, self.core)
        value = jnp.stack([jnp.where(bit, got, value), jnp.where(bit, value, got)], axis=self.core_axis)
        return value.reshape((self.count,) + rest)


def scaled_norm(rows, scale):
    wide = rows.astype(jnp.float32)
    return jnp.sum(wide * wide, axis=1, keepdims=True) * scale


def gram_kernel(scale, core_ref, block_ref, own_ref, cross_ref):
    mine = block_ref[pl.ds(pl.multiple_of(core_ref[0] * BLOCK, BLOCK), BLOCK), :]
    eye = jnp.where(
        lax.broadcasted_iota(jnp.int32, (BLOCK, BLOCK), 0)
        == lax.broadcasted_iota(jnp.int32, (BLOCK, BLOCK), 1),
        RIDGE,
        0.0,
    )
    for left, right, shift, out in (
        (mine, mine, eye, own_ref),
        (block_ref[:BLOCK], block_ref[BLOCK:], 0.0, cross_ref),
    ):
        dots = lax.dot_general(left, right, NT, preferred_element_type=jnp.float32)
        right_norm = scaled_norm(right, scale)
        row = jnp.transpose(jnp.broadcast_to(right_norm, (BLOCK, 128)))[:1]
        value = jnp.exp(dots * (2.0 * scale) - scaled_norm(left, scale) - row)
        out[...] = (value + shift).astype(out.dtype)


def gram(block, core, scale):
    square = (BLOCK, BLOCK)
    whole = lambda shape: pl.BlockSpec(shape, lambda i, *_: (0, 0))
    return pl.pallas_call(
        functools.partial(gram_kernel, scale),
        grid_spec=pltpu.PrefetchScalarGridSpec(
            num_scalar_prefetch=1,
            grid=(1,),
            in_specs=[whole(block.shape)],
            out_specs=[whole(square)] * 2,
        ),
        out_shape=(jax.ShapeDtypeStruct(square, jnp.float32), jax.ShapeDtypeStruct(square, jnp.bfloat16)),
        compiler_params=pltpu.CompilerParams(vmem_limit_bytes=SMALL_LIMIT),
        cost_estimate=pl.CostEstimate(
            flops=2 * 2 * BLOCK**3, bytes_accessed=4 * BLOCK * BLOCK * 4, transcendentals=2 * BLOCK**2
        ),
        name="gram",
    )(core, block)


def slab_kernel(scale, chunk, block_ref, feat_ref, norm_ref, res_ref, coef_ref, slab_ref, piece_ref, bnorm, grad, cross):
    scale2 = scale * LOG2E
    norm = scaled_norm(block_ref[...], scale2)
    bnorm[...] = jnp.broadcast_to(norm, bnorm.shape)
    grad[...] = jnp.zeros_like(grad)
    cross[...] = jnp.zeros_like(cross)
    part = BLOCK // 2
    parts = STEPS * BLOCK // part
    total = feat_ref.shape[0] // chunk * parts

    def product(n):
        at, rows = slice(n % parts * part, (n % parts + 1) * part), slice(n // parts * chunk, (n // parts + 1) * chunk)
        return lax.dot_general(block_ref[at], feat_ref[rows], NT, preferred_element_type=jnp.float32)

    def finish_part(n, dots):
        at, rows = slice(n % parts * part, (n % parts + 1) * part), slice(n // parts * chunk, (n // parts + 1) * chunk)
        weighted = (res_ref[rows] - RIDGE * coef_ref[rows]).astype(jnp.bfloat16)
        norm_wide = jnp.concatenate([bnorm[at]] * (chunk // bnorm.shape[1]), axis=1)
        slab = jnp.exp2(dots * (2.0 * scale2) - norm_wide - norm_ref[:, rows] * LOG2E).astype(jnp.bfloat16)
        slab_ref[at, rows] = slab
        grad[at] += jnp.dot(slab, weighted, preferred_element_type=jnp.float32)

    def add_cross(c):
        rows = slice(c * chunk, (c + 1) * chunk)
        cross[...] += lax.dot_general(
            slab_ref[:BLOCK, rows], slab_ref[BLOCK:, rows], NT, preferred_element_type=jnp.float32
        )

    dots = product(0)
    for n in range(total):
        ahead = product(n + 1) if n + 1 < total else None
        finish_part(n, dots)
        dots = ahead
        if n % parts == 0 and n:
            add_cross(n // parts - 1)
    add_cross(total // parts - 1)
    grads = jnp.transpose(grad[...])
    groups = piece_ref.shape[0]
    own, depth = grads.shape[0] // groups, BLOCK // groups
    for d in range(groups):
        for s in range(STEPS):
            piece_ref[d, s * own : (s + 1) * own] = grads[d * own : (d + 1) * own, s * BLOCK : (s + 1) * BLOCK]
        piece_ref[d, STEPS * own :] = cross[d * depth : (d + 1) * depth]


def in_vmem(value):
    return pltpu.with_memory_space_constraint(value, pltpu.VMEM)


def slabs(block, features, norms, residual, coefficients, scale, groups, chunk=512):
    rows, width = features.shape
    targets = residual.shape[1]
    both = STEPS * BLOCK
    piece = (groups, STEPS * targets // groups + BLOCK // groups, BLOCK)
    return pl.pallas_call(
        functools.partial(slab_kernel, scale, chunk),
        out_shape=(pltpu.VMEM((both, rows), jnp.bfloat16), jax.ShapeDtypeStruct(piece, jnp.float32)),
        scratch_shapes=[
            pltpu.VMEM((both, 128), jnp.float32),
            pltpu.VMEM((both, targets), jnp.float32),
            pltpu.VMEM((BLOCK, BLOCK), jnp.float32),
        ],
        compiler_params=pltpu.CompilerParams(vmem_limit_bytes=VMEM_LIMIT),
        cost_estimate=pl.CostEstimate(
            flops=2 * rows * both * (width + targets + BLOCK // 2),
            bytes_accessed=rows * (width * 2 + targets * 8 + both * 2),
            transcendentals=rows * both,
        ),
        name="slabs",
    )(block, in_vmem(features), norms, in_vmem(residual), in_vmem(coefficients))


def reciprocal(x):
    guess = pl.reciprocal(x, approx=True)
    return guess * (2.0 - x * guess)


def eliminate(tiles, t, lane, scaled_ref):
    start, shape = 8 * t, tiles[t].shape
    wide = lambda tile, k: jnp.broadcast_to(tile[:, start + k : start + k + 1], shape)
    rows = [jnp.broadcast_to(tiles[t][k : k + 1], shape) for k in range(8)]
    at = {(i, k): wide(rows[i], k) for i in range(8) for k in range(i, 8)}
    units = [jnp.where(lane == start + k, 1.0, 0.0) for k in range(8)]
    rows = [row + unit for row, unit in zip(rows, units)]
    total, lower = [None] * 8, {}
    for r in range(0, 8, 2):
        p, m, q = at[r, r], at[r, r + 1], at[r + 1, r + 1]
        inverse = reciprocal(p * q - m * m)
        p, m, q = p * inverse, m * inverse, q * inverse
        for k in range(r + 2, 8):
            first = q * at[r, k] - m * at[r + 1, k]
            second = p * at[r + 1, k] - m * at[r, k]
            lower[r, k], lower[r + 1, k] = first, second
            for i in range(r + 2, k + 1):
                at[i, k] = at[i, k] - (at[r, i] * first + at[r + 1, i] * second)
            rows[k] = rows[k] - (first * rows[r] + second * rows[r + 1])
        total[r] = q * rows[r] - m * rows[r + 1]
        total[r + 1] = p * rows[r + 1] - m * rows[r]
    for r in (4, 2, 0):
        for k in range(r + 2, 8):
            total[r] = total[r] - lower[r, k] * total[k]
            total[r + 1] = total[r + 1] - lower[r + 1, k] * total[k]
    for k in range(8):
        scaled_ref[start + k : start + k + 1] = total[k][:1] - units[k][:1]
    for u in range(t + 1, len(tiles)):
        parts = [wide(tiles[u], k) * total[k] for k in range(8)]
        while len(parts) > 1:
            parts = [x + y for x, y in zip(parts[::2], parts[1::2])]
        tiles[u] = tiles[u] - parts[0]


def factor_kernel(index, copies, *refs):
    refs = list(refs)
    rest_ref = refs.pop(0)
    if copies:
        source, scaled, sem = refs.pop(0), refs[-2], refs[-1]
        copy = pltpu.make_async_copy(source, refs[-3], sem)
        copy.start()
    else:
        scaled = refs[-1]
    last = rest_ref.shape[0] == TILE
    factor_ref = refs[0] if last else refs[1]
    here = slice(index * TILE, (index + 1) * TILE)
    row_ids = lax.broadcasted_iota(jnp.int32, (TILE, TILE), 0)
    col_ids = lax.broadcasted_iota(jnp.int32, (TILE, TILE), 1)
    lane = lax.broadcasted_iota(jnp.int32, (8, TILE), 1)
    tiles = [rest_ref[8 * t : 8 * t + 8, here] for t in range(TILE // 8)]
    for t in range(TILE // 8):
        eliminate(tiles, t, lane, scaled)
    start = row_ids - row_ids % 8
    dot = functools.partial(lax.dot_general, precision=HIGH, preferred_element_type=jnp.float32)
    lower = jnp.where(col_ids < start, jnp.concatenate(tiles, axis=0), 0.0)
    lower = lower + jnp.where(col_ids == row_ids, 1.0, 0.0)
    right = jnp.where(col_ids < start + 8, scaled[...], 0.0)
    inv = dot(lower, right, (((0,), (0,)), ((), ())))
    top = rest_ref[:TILE]
    panel = dot(inv, top, (((1,), (0,)), ((), ())))
    inside = lax.broadcasted_iota(jnp.int32, panel.shape, 1) // TILE == index
    panel = jnp.where(inside, jnp.concatenate([inv] * (BLOCK // TILE), axis=1), panel)
    factor_ref[:TILE] = top
    factor_ref[TILE:] = panel
    if not last:
        under = rest_ref[TILE:]
        change = dot(rest_ref[TILE:, here], panel, (((1,), (0,)), ((), ())))
        inside = lax.broadcasted_iota(jnp.int32, under.shape, 1) // TILE == index
        refs[0][...] = jnp.where(inside, 0.0, under) - change
    if copies:
        copy.wait()


def factor_step(rest, index, copied=None):
    left = rest.shape[0] - TILE
    vmem, hbm = pl.BlockSpec(memory_space=pltpu.VMEM), pl.BlockSpec(memory_space=pltpu.HBM)
    out = [jax.ShapeDtypeStruct((left, BLOCK), jnp.float32)] if left else []
    out.append(jax.ShapeDtypeStruct((2 * TILE, BLOCK), jnp.float32))
    inputs, in_specs, out_specs = [rest], [vmem], [vmem] * len(out)
    scratch = [pltpu.VMEM((TILE, TILE), jnp.float32)]
    if copied is not None:
        inputs.append(in_vmem(copied))
        in_specs.append(vmem)
        out.append(pltpu.HBM(copied.shape, copied.dtype))
        out_specs.append(hbm)
        scratch.append(pltpu.SemaphoreType.DMA)
    out = pl.pallas_call(
        functools.partial(factor_kernel, index, copied is not None),
        in_specs=in_specs,
        out_specs=tuple(out_specs),
        out_shape=tuple(out),
        scratch_shapes=scratch,
        compiler_params=pltpu.CompilerParams(vmem_limit_bytes=SMALL_LIMIT),
        cost_estimate=pl.CostEstimate(flops=6 * 10**9, bytes_accessed=4 * 1024 * 1024, transcendentals=0),
        name="factor",
    )(*inputs)
    out = list(out)
    below = out.pop(0) if left else None
    return (below,) + tuple(out)


def apply_inverse(value, refs):
    ids = lambda axis: lax.broadcasted_iota(jnp.int32, (TILE, BLOCK), axis)
    lower, right = [], []
    for k in range(BLOCK // TILE):
        rest, panel = refs[k][:TILE], refs[k][TILE:]
        unit = jnp.where(ids(1) == ids(0) + k * TILE, 1.0, 0.0)
        lower.append(jnp.where(ids(1) < k * TILE, rest, unit))
        right.append(jnp.where(ids(1) < (k + 1) * TILE, panel, 0.0))
    lower, right = jnp.concatenate(lower, axis=0), jnp.concatenate(right, axis=0)
    middle = lax.dot_general(value, right, NT, precision=HIGH, preferred_element_type=jnp.float32)
    return jnp.dot(middle, lower, precision=HIGH, preferred_element_type=jnp.float32)


def first_kernel(step_size, grad_ref, *refs):
    refs[-1][...] = apply_inverse(grad_ref[: refs[-1].shape[0]], refs[:-1]) * step_size


def second_kernel(step_size, grad_ref, first_ref, cross_ref, gram_ref, *refs):
    out_ref = refs[-1]
    first = first_ref[...]
    own = first.shape[0]
    again = (
        grad_ref[own:]
        - jnp.dot(first.astype(jnp.bfloat16), cross_ref[...], preferred_element_type=jnp.float32)
        - RIDGE * jnp.dot(first, gram_ref[...].astype(jnp.float32), precision=HIGH, preferred_element_type=jnp.float32)
    )
    out_ref[:own] = first.astype(out_ref.dtype)
    out_ref[own:] = (apply_inverse(again, refs[:-1]) * step_size).astype(out_ref.dtype)


def solve(kernel, out, arrays, factors, step_size):
    whole = lambda value: pl.BlockSpec(value.shape, lambda i: (0,) * len(value.shape))
    return pl.pallas_call(
        functools.partial(kernel, step_size),
        grid=(1,),
        in_specs=[whole(value) for value in list(arrays) + list(factors)],
        out_specs=whole(out),
        out_shape=out,
        compiler_params=pltpu.CompilerParams(vmem_limit_bytes=SMALL_LIMIT),
        cost_estimate=pl.CostEstimate(flops=10**9, bytes_accessed=3 * 1024 * 1024, transcendentals=0),
        name=kernel.__name__[:-7],
    )(*arrays, *factors)


def final_kernel(chunk, owner_ref, tiles_ref, me_ref, gathered_ref, slab_ref, res_ref, coef_ref, base_ref, res_out, coef_out, upd_ref, res_buf, tile_buf, res_sems, tile_sems):
    rows, targets = res_ref.shape
    groups, own2 = gathered_ref.shape[0], gathered_ref.shape[1]
    own = own2 // STEPS
    count = BLOCK // TILE
    flat = gathered_ref[...].reshape(groups * own2, BLOCK)
    target = lax.broadcasted_iota(jnp.int32, (targets, groups * own2), 0)
    place = lax.broadcasted_iota(jnp.int32, (targets, groups * own2), 1)
    wanted = target // own * own2 + target % own
    for s in range(STEPS):
        pick = jnp.where(place == wanted + s * own, 1.0, 0.0).astype(jnp.bfloat16)
        chosen = jnp.dot(pick, flat, preferred_element_type=jnp.float32)
        upd_ref[:, s * BLOCK : (s + 1) * BLOCK] = chosen.astype(jnp.bfloat16)

    def change_of(s, k):
        at = s * BLOCK + k * TILE
        return jnp.transpose(upd_ref[:, at : at + TILE].astype(jnp.float32))

    def tile_rows(s, k):
        return pl.ds(pl.multiple_of(tiles_ref[s, k] * TILE, TILE), TILE)

    def tile_copy(s, k):
        return pltpu.make_async_copy(tile_buf.at[s, k], coef_out.at[tile_rows(s, k), :], tile_sems.at[s, k])

    owned = [owner_ref[s] == me_ref[0] for s in range(STEPS)]

    def writes(s, k):
        kept = owned[s]
        for later in range(s + 1, STEPS):
            for j in range(count):
                kept = kept & jnp.logical_not(owned[later] & (tiles_ref[later, j] == tiles_ref[s, k]))
        return kept

    for s in range(STEPS):
        for k in range(count):

            @pl.when(writes(s, k))
            def _():
                tile_buf[s, k] = coef_ref[tile_rows(s, k), :] + change_of(s, k)
                for earlier in range(s):
                    for j in range(count):

                        @pl.when(owned[earlier] & (tiles_ref[earlier, j] == tiles_ref[s, k]))
                        def _():
                            tile_buf[s, k] += change_of(earlier, j)

                tile_copy(s, k).start()

    def res_copy(i):
        at = pl.ds(pl.multiple_of(i * chunk, chunk), chunk)
        return pltpu.make_async_copy(res_buf.at[at, :], res_out.at[at, :], res_sems.at[i])

    def body(i, _):
        at = pl.ds(pl.multiple_of(i * chunk, chunk), chunk)
        change = jnp.dot(upd_ref[...], slab_ref[:, at], preferred_element_type=jnp.float32)
        res_buf[at, :] = res_ref[at, :] - jnp.transpose(change)
        res_copy(i).start()
        return 0

    lax.fori_loop(0, rows // chunk, body, 0)
    for i in range(rows // chunk):
        res_copy(i).wait()
    for s in range(STEPS):
        for k in range(count):

            @pl.when(writes(s, k))
            def _():
                tile_copy(s, k).wait()


def finish(owner, tiles, me, gathered, slab, residual, coefficients, base, chunk=512):
    rows, targets = residual.shape
    both = STEPS * BLOCK
    count = BLOCK // TILE
    smem, vmem, hbm = (pl.BlockSpec(memory_space=space) for space in (pltpu.SMEM, pltpu.VMEM, pltpu.HBM))
    return pl.pallas_call(
        functools.partial(final_kernel, chunk),
        in_specs=[smem] * 3 + [vmem] * 4 + [hbm],
        out_specs=(hbm, hbm),
        out_shape=(
            pltpu.HBM(residual.shape, jnp.float32),
            pltpu.HBM(residual.shape, jnp.float32),
        ),
        scratch_shapes=[
            pltpu.VMEM((targets, both), jnp.bfloat16),
            pltpu.VMEM((rows, targets), jnp.float32),
            pltpu.VMEM((STEPS, count, TILE, targets), jnp.float32),
            pltpu.SemaphoreType.DMA((rows // chunk,)),
            pltpu.SemaphoreType.DMA((STEPS, count)),
        ],
        input_output_aliases={7: 1},
        compiler_params=pltpu.CompilerParams(vmem_limit_bytes=SMALL_LIMIT),
        cost_estimate=pl.CostEstimate(
            flops=2 * rows * both * targets, bytes_accessed=rows * (both * 2 + targets * 16), transcendentals=0
        ),
        name="finish",
    )(owner, tiles, me, gathered, in_vmem(slab), in_vmem(residual), in_vmem(coefficients), base)


def local(features, residual, coefficients, block_owner, block_tiles):
    rows_dev, width = features.shape
    targets = residual.shape[1]
    sub_count = lax.axis_size("sub")
    devices = lax.axis_size("rows") * sub_count
    me = lax.axis_index(AXES).astype(jnp.int32)
    scale = 1.0 / width
    step_size = 1.0 / math.sqrt(rows_dev * devices)
    spread = Spread(AXES, sub_count) if devices <= 32 else Spread(("rows",), 1)
    groups = spread.count
    own = targets // groups

    wide = features.astype(jnp.float32)
    norms = (jnp.sum(wide * wide, axis=1) * scale).reshape(1, rows_dev)
    block, norms = fetch_blocks(features, norms, block_owner, block_tiles, me, devices, sub_count)
    slab, pieces = slabs(block, features, norms, residual, coefficients, scale, groups)
    if spread.axes != AXES:
        pieces = lax.psum(pieces, "sub")
    core = bit_of(me, sub_count)
    rest, gram12 = gram(block, core.reshape(1), scale)
    factors, base = ([], []), None

    def beside(hop, index, rest):
        then, got = hop
        below, mine, *copied = factor_step(rest, index, coefficients if index == 0 else None)
        got, below, mine = lax.optimization_barrier((got, below, mine))
        other = swap(mine, AXES, sub_count)
        factors[0].append(jnp.where(core != 0, other, mine))
        factors[1].append(jnp.where(core != 0, mine, other))
        return then(got), below, copied

    value = spread.core_sum(pieces)
    value, rest, (base,) = beside(spread.near_sum(value, STEPS * own), 0, rest)
    for index, mask in enumerate(spread.far):
        value, rest, _ = beside(spread.far_sum(value, STEPS * own, mask), 1 + index, rest)
    cross = value[STEPS * own :].astype(jnp.bfloat16)
    cross, rest, _ = beside(spread.near_gather(cross), 3, rest)
    cross = spread.core_gather(cross)
    grads = value[: STEPS * own]
    first = jax.ShapeDtypeStruct((own, BLOCK), jnp.float32)
    first = solve(first_kernel, first, [grads], factors[0], step_size)
    cross, first = lax.optimization_barrier((cross, first))
    update = jax.ShapeDtypeStruct(grads.shape, jnp.bfloat16)
    update = solve(
        second_kernel, update, [grads, first, cross.reshape(BLOCK, BLOCK), gram12], factors[1], step_size
    )
    then, got = spread.near_gather(update)
    gathered = spread.core_gather(then(got))
    return finish(block_owner, block_tiles, me.reshape(1), gathered, slab, residual, coefficients, base)


def solution(mesh):
    row_spec = P(AXES, None)
    return jax.shard_map(
        local,
        mesh=mesh,
        in_specs=(row_spec, row_spec, row_spec, P(), P()),
        out_specs=(row_spec, row_spec),
        check_vma=False,
    )
```

```python
import functools
import math

import jax
import jax.numpy as jnp
from jax import lax
from jax.experimental import pallas as pl
from jax.experimental.pallas import tpu as pltpu
from jax.sharding import PartitionSpec as P

BLOCK = 512
TILE = 128
STEPS = 2
RIDGE = 0.5
AXES = ("rows", "sub")
HIGH = lax.Precision.HIGHEST
NT = (((1,), (1,)), ((), ()))
LOG2E = math.log2(math.e)
VMEM_LIMIT = 16 * 1024 * 1024
SMALL_LIMIT = 12 * 1024 * 1024


def pick_kernel(tiles_ref, core_ref, feat_ref, keep_ref, send_ref, sems):
    per_half = keep_ref.shape[1] // TILE
    copies = []
    for turn, out in enumerate((keep_ref, send_ref)):
        half = core_ref[0] if turn == 0 else 1 - core_ref[0]
        for s in range(STEPS):
            for i in range(per_half):
                source = pl.multiple_of(tiles_ref[s, half * per_half + i] * TILE, TILE)
                copies.append(
                    pltpu.make_async_copy(
                        feat_ref.at[pl.ds(source, TILE), :],
                        out.at[s, pl.ds(i * TILE, TILE), :],
                        sems.at[turn, s, i],
                    )
                )
    for copy in copies:
        copy.start()
    for copy in copies:
        copy.wait()


def pick_halves(features, block_tiles, core):
    width = features.shape[1]
    half = jax.ShapeDtypeStruct((STEPS, BLOCK // 2, width), features.dtype)
    return pl.pallas_call(
        pick_kernel,
        grid_spec=pltpu.PrefetchScalarGridSpec(
            num_scalar_prefetch=2,
            grid=(1,),
            in_specs=[pl.BlockSpec(memory_space=pltpu.HBM)],
            out_specs=[pl.BlockSpec(half.shape, lambda i, *_: (0, 0, 0))] * 2,
            scratch_shapes=[pltpu.SemaphoreType.DMA((2, STEPS, BLOCK // 2 // TILE))],
        ),
        out_shape=(half, half),
        compiler_params=pltpu.CompilerParams(vmem_limit_bytes=SMALL_LIMIT),
        name="pick",
    )(pltpu.with_memory_space_constraint(block_tiles, pltpu.HBM), core, pltpu.with_memory_space_constraint(features, pltpu.HBM))


def swap(value, axes, flip):
    flip_of = flip if callable(flip) else lambda i: flip
    return lax.ppermute(value, axes, [(i, i ^ flip_of(i)) for i in range(lax.axis_size(axes))])


def bit_of(index, mask):
    return ((index & mask) != 0).astype(jnp.int32)


def swap_among(pick, me, axes, low, high):
    place = bit_of(me, low) + 2 * bit_of(me, high)
    flips = [0, low, high, low | high]
    return place, [swap(pick(place ^ c), axes, flips[c]) for c in (1, 2, 3)]


def ordered(parts, me, low, high, axis):
    one, two = (me & low) != 0, (me & high) != 0
    parts = [jnp.where(one, parts[c ^ 1], parts[c]) for c in range(4)]
    return jnp.stack([jnp.where(two, parts[c ^ 2], parts[c]) for c in range(4)], axis=axis)


def fetch_blocks(features, norms, block_owner, block_tiles, me, devices, core):
    width = features.shape[1]
    low, high = 1, 2 * core
    differs = lambda mask: (((block_owner ^ me) & mask) != 0)[:, None, None]
    on_core = (me & core) != 0

    keep, send = pick_halves(features, block_tiles, bit_of(me, core).reshape(1))
    half = jnp.where(differs(core), swap(send, AXES, core), keep)
    quarters = half.reshape(STEPS, 4, BLOCK // 8, width)
    pick = lambda place: lax.dynamic_index_in_dim(quarters, place, 1, False)
    place, got = swap_among(pick, me, AXES, low, high)
    part = jnp.where(
        differs(high),
        jnp.where(differs(low), got[2], got[1]),
        jnp.where(differs(low), got[0], pick(place)),
    )
    far = [1 << b for b in range(devices.bit_length() - 1) if 1 << b not in (core, low, high)]
    hops = []
    for one, two in zip(far[::2], far[1::2]):
        for first, second in ((one, two), (two, one)):
            flip = lambda i, first=first, second=second: second if i & core else first
            hops.append((flip, jnp.where(on_core, second, first)))
    if len(far) % 2:
        hops.append((far[-1], far[-1]))
    for hop, (flip, mask) in enumerate(hops):
        other = swap(part, AXES, flip)
        if hop == len(hops) - 2:
            other, norms = lax.optimization_barrier((other, norms))
        part = jnp.where(differs(mask), other, part)
    _, got = swap_among(lambda place: part, me, AXES, low, high)
    half = ordered([part] + got, me, low, high, 1)
    other = swap(half, AXES, core)
    both = jnp.stack([jnp.where(on_core, other, half), jnp.where(on_core, half, other)], axis=1)
    return both.reshape(STEPS * BLOCK, width), norms


def pack(value, exact):
    high = lax.reduce_precision(value[..., :exact, :], 8, 7)
    low = value[..., :exact, :] - high
    return jnp.concatenate([part.astype(jnp.bfloat16) for part in (high, low, value[..., exact:, :])], axis=-2)


def unpack(value, exact):
    value = value.astype(jnp.float32)
    return jnp.concatenate([value[..., :exact, :] + value[..., exact : 2 * exact, :], value[..., 2 * exact :, :]], axis=-2)


class Spread:
    def __init__(self, axes, core):
        self.axes, self.core = axes, core
        self.me = lax.axis_index(axes).astype(jnp.int32)
        self.near = [1 << b for b in range(3) if 1 << b != core]
        self.far = [1 << b for b in range(3, lax.axis_size(axes).bit_length() - 1)]
        self.count = 8
        self.core_axis = 2 - (core.bit_length() - 1)

    def core_sum(self, value):
        value = value.reshape((2,) * 3 + value.shape[1:])
        zero, one = (lax.index_in_dim(value, i, self.core_axis, False) for i in (0, 1))
        bit = (self.me & self.core) != 0
        value = jnp.where(bit, one, zero) + swap(jnp.where(bit, zero, one), self.axes, self.core)
        return value.reshape((4,) + value.shape[2:])

    def near_sum(self, value, exact):
        packed = pack(value, exact)
        pick = lambda array, place: lax.dynamic_index_in_dim(array, place, 0, False)
        place, got = swap_among(lambda place: pick(packed, place), self.me, self.axes, *self.near)
        return lambda got: pick(value, place) + unpack(got[0], exact) + unpack(got[1], exact) + unpack(got[2], exact), got

    def far_sum(self, value, exact, mask):
        return lambda got: value + unpack(got[0], exact), [swap(pack(value, exact), self.axes, mask)]

    def near_gather(self, value):
        _, got = swap_among(lambda place: value, self.me, self.axes, *self.near)
        return lambda got: ordered([value] + got, self.me, *self.near, 0), got

    def core_gather(self, value):
        rest = value.shape[1:]
        value = value.reshape((2, 2) + rest)
        bit = (self.me & self.core) != 0
        got = swap(value, self.axes, self.core)
        value = jnp.stack([jnp.where(bit, got, value), jnp.where(bit, value, got)], axis=self.core_axis)
        return value.reshape((self.count,) + rest)


def scaled_norm(rows, scale):
    wide = rows.astype(jnp.float32)
    return jnp.sum(wide * wide, axis=1, keepdims=True) * scale


def gram_kernel(scale, core_ref, block_ref, slab_ref, own_ref, cross_ref):
    mine = block_ref[pl.ds(pl.multiple_of(core_ref[0] * BLOCK, BLOCK), BLOCK), :]
    eye = jnp.where(
        lax.broadcasted_iota(jnp.int32, (BLOCK, BLOCK), 0)
        == lax.broadcasted_iota(jnp.int32, (BLOCK, BLOCK), 1),
        RIDGE,
        0.0,
    )
    for left, right, shift, out in (
        (mine, mine, eye, own_ref),
        (block_ref[:BLOCK], block_ref[BLOCK:], 0.0, cross_ref),
    ):
        dots = lax.dot_general(left, right, NT, preferred_element_type=jnp.float32)
        right_norm = scaled_norm(right, scale)
        row = jnp.transpose(jnp.broadcast_to(right_norm, (BLOCK, 128)))[:1]
        value = jnp.exp(dots * (2.0 * scale) - scaled_norm(left, scale) - row)
        out[...] = (value + shift).astype(out.dtype)


def gram(block, core, scale, slab):
    square = (BLOCK, BLOCK)
    vmem = pl.BlockSpec(memory_space=pltpu.VMEM)
    return pl.pallas_call(
        functools.partial(gram_kernel, scale),
        in_specs=[pl.BlockSpec(memory_space=pltpu.SMEM), vmem, vmem],
        out_shape=(jax.ShapeDtypeStruct(square, jnp.float32), jax.ShapeDtypeStruct(square, jnp.bfloat16)),
        compiler_params=pltpu.CompilerParams(vmem_limit_bytes=SMALL_LIMIT),
        cost_estimate=pl.CostEstimate(
            flops=2 * 2 * BLOCK**3, bytes_accessed=4 * BLOCK * BLOCK * 4, transcendentals=2 * BLOCK**2
        ),
        name="gram",
    )(core, block, in_vmem(slab))


def slab_kernel(scale, chunk, block_ref, feat_ref, norm_ref, res_ref, coef_ref, slab_ref, piece_ref, bnorm, grad, cross, ahead_ref):
    scale2 = scale * LOG2E
    norm = scaled_norm(block_ref[...], scale2)
    bnorm[...] = jnp.broadcast_to(norm, bnorm.shape)
    grad[...] = jnp.zeros_like(grad)
    cross[...] = jnp.zeros_like(cross)
    part = BLOCK // 2
    parts = STEPS * BLOCK // part
    chunks = feat_ref.shape[0] // chunk
    rows_of = lambda i: pl.ds(pl.multiple_of(i * chunk, chunk), chunk)
    at_of = lambda p: slice(p * part, (p + 1) * part)

    def product(i, p):
        return lax.dot_general(block_ref[at_of(p)], feat_ref[rows_of(i), :], NT, preferred_element_type=jnp.float32)

    ahead_ref[...] = product(0, 0)

    def body(i, _):
        rows = rows_of(i)
        weighted = (res_ref[rows, :] - RIDGE * coef_ref[rows, :]).astype(jnp.bfloat16)
        norm_row = norm_ref[:, rows] * LOG2E
        dots = ahead_ref[...]
        for p in range(parts):
            ahead = product(i, p + 1) if p + 1 < parts else product(jnp.minimum(i + 1, chunks - 1), 0)
            norm_wide = jnp.concatenate([bnorm[at_of(p)]] * (chunk // bnorm.shape[1]), axis=1)
            slab = jnp.exp2(dots * (2.0 * scale2) - norm_wide - norm_row).astype(jnp.bfloat16)
            slab_ref[at_of(p), rows] = slab
            grad[at_of(p)] += jnp.dot(slab, weighted, preferred_element_type=jnp.float32)
            dots = ahead
        ahead_ref[...] = dots
        cross[...] += lax.dot_general(
            slab_ref[:BLOCK, rows], slab_ref[BLOCK:, rows], NT, preferred_element_type=jnp.float32
        )
        return 0

    lax.fori_loop(0, chunks, body, 0, unroll=2)
    grads = jnp.transpose(grad[...])
    groups = piece_ref.shape[0]
    own, depth = grads.shape[0] // groups, BLOCK // groups
    for d in range(groups):
        for s in range(STEPS):
            piece_ref[d, s * own : (s + 1) * own] = grads[d * own : (d + 1) * own, s * BLOCK : (s + 1) * BLOCK]
        piece_ref[d, STEPS * own :] = cross[d * depth : (d + 1) * depth]


def in_vmem(value):
    return pltpu.with_memory_space_constraint(value, pltpu.VMEM)


def slabs(block, features, norms, residual, coefficients, scale, groups, chunk=512):
    rows, width = features.shape
    targets = residual.shape[1]
    both = STEPS * BLOCK
    piece = (groups, STEPS * targets // groups + BLOCK // groups, BLOCK)
    return pl.pallas_call(
        functools.partial(slab_kernel, scale, chunk),
        out_shape=(pltpu.VMEM((both, rows), jnp.bfloat16), jax.ShapeDtypeStruct(piece, jnp.float32)),
        scratch_shapes=[
            pltpu.VMEM((both, 128), jnp.float32),
            pltpu.VMEM((both, targets), jnp.float32),
            pltpu.VMEM((BLOCK, BLOCK), jnp.float32),
            pltpu.VMEM((BLOCK // 2, chunk), jnp.float32),
        ],
        compiler_params=pltpu.CompilerParams(vmem_limit_bytes=VMEM_LIMIT),
        cost_estimate=pl.CostEstimate(
            flops=2 * rows * both * (width + targets + BLOCK // 2),
            bytes_accessed=rows * (width * 2 + targets * 8 + both * 2),
            transcendentals=rows * both,
        ),
        name="slabs",
    )(block, in_vmem(features), norms, in_vmem(residual), in_vmem(coefficients))


def reciprocal(x):
    guess = pl.reciprocal(x, approx=True)
    return guess * (2.0 - x * guess)


def eliminate(tiles, t, lane, scaled_ref):
    start, shape = 8 * t, tiles[t].shape
    wide = lambda tile, k: jnp.broadcast_to(tile[:, start + k : start + k + 1], shape)
    rows = [jnp.broadcast_to(tiles[t][k : k + 1], shape) for k in range(8)]
    at = {(i, k): wide(rows[i], k) for i in range(8) for k in range(i, 8)}
    units = [jnp.where(lane == start + k, 1.0, 0.0) for k in range(8)]
    rows = [row + unit for row, unit in zip(rows, units)]
    total, lower = [None] * 8, {}
    for r in range(0, 8, 2):
        p, m, q = at[r, r], at[r, r + 1], at[r + 1, r + 1]
        inverse = reciprocal(p * q - m * m)
        p, m, q = p * inverse, m * inverse, q * inverse
        for k in range(r + 2, 8):
            first = q * at[r, k] - m * at[r + 1, k]
            second = p * at[r + 1, k] - m * at[r, k]
            lower[r, k], lower[r + 1, k] = first, second
            for i in range(r + 2, k + 1):
                at[i, k] = at[i, k] - (at[r, i] * first + at[r + 1, i] * second)
            rows[k] = rows[k] - (first * rows[r] + second * rows[r + 1])
        total[r] = q * rows[r] - m * rows[r + 1]
        total[r + 1] = p * rows[r + 1] - m * rows[r]
    for r in (4, 2, 0):
        for k in range(r + 2, 8):
            total[r] = total[r] - lower[r, k] * total[k]
            total[r + 1] = total[r + 1] - lower[r + 1, k] * total[k]
    for k in range(8):
        scaled_ref[start + k : start + k + 1] = total[k][:1] - units[k][:1]
    for u in range(t + 1, len(tiles)):
        parts = [wide(tiles[u], k) * total[k] for k in range(8)]
        while len(parts) > 1:
            parts = [x + y for x, y in zip(parts[::2], parts[1::2])]
        tiles[u] = tiles[u] - parts[0]


def factor_kernel(index, copies, *refs):
    refs = list(refs)
    rest_ref, _ = refs.pop(0), refs.pop(0)
    if copies:
        source, scaled, sem = refs.pop(0), *refs[-2:]
        copy = pltpu.make_async_copy(source, refs[-3], sem)
        copy.start()
    else:
        scaled = refs[-1]
    last = rest_ref.shape[0] == TILE
    factor_ref = refs[0] if last else refs[1]
    here = slice(index * TILE, (index + 1) * TILE)
    row_ids = lax.broadcasted_iota(jnp.int32, (TILE, TILE), 0)
    col_ids = lax.broadcasted_iota(jnp.int32, (TILE, TILE), 1)
    lane = lax.broadcasted_iota(jnp.int32, (8, TILE), 1)
    tiles = [rest_ref[8 * t : 8 * t + 8, here] for t in range(TILE // 8)]
    for t in range(TILE // 8):
        eliminate(tiles, t, lane, scaled)
    start = row_ids - row_ids % 8
    dot = functools.partial(lax.dot_general, precision=HIGH, preferred_element_type=jnp.float32)
    lower = jnp.where(col_ids < start, jnp.concatenate(tiles, axis=0), 0.0)
    lower = lower + jnp.where(col_ids == row_ids, 1.0, 0.0)
    right = jnp.where(col_ids < start + 8, scaled[...], 0.0)
    inv = dot(lower, right, (((0,), (0,)), ((), ())))
    top = rest_ref[:TILE]
    panel = dot(inv, top, (((1,), (0,)), ((), ())))
    inside = lax.broadcasted_iota(jnp.int32, panel.shape, 1) // TILE == index
    panel = jnp.where(inside, jnp.concatenate([inv] * (BLOCK // TILE), axis=1), panel)
    factor_ref[:TILE] = top
    factor_ref[TILE:] = panel
    if not last:
        under = rest_ref[TILE:]
        change = dot(rest_ref[TILE:, here], panel, (((1,), (0,)), ((), ())))
        inside = lax.broadcasted_iota(jnp.int32, under.shape, 1) // TILE == index
        refs[0][...] = jnp.where(inside, 0.0, under) - change
    if copies:
        copy.wait()


def factor_step(rest, index, slab, copied=None):
    left = rest.shape[0] - TILE
    vmem, hbm = pl.BlockSpec(memory_space=pltpu.VMEM), pl.BlockSpec(memory_space=pltpu.HBM)
    out = [jax.ShapeDtypeStruct((left, BLOCK), jnp.float32)] if left else []
    out.append(jax.ShapeDtypeStruct((2 * TILE, BLOCK), jnp.float32))
    inputs, in_specs, out_specs = [rest, in_vmem(slab)], [vmem] * 2, [vmem] * len(out)
    scratch = [pltpu.VMEM((TILE, TILE), jnp.float32)]
    if copied is not None:
        inputs.append(in_vmem(copied))
        in_specs.append(vmem)
        out.append(pltpu.HBM(copied.shape, copied.dtype))
        out_specs.append(hbm)
        scratch.append(pltpu.SemaphoreType.DMA)
    out = pl.pallas_call(
        functools.partial(factor_kernel, index, copied is not None),
        in_specs=in_specs,
        out_specs=tuple(out_specs),
        out_shape=tuple(out),
        scratch_shapes=scratch,
        compiler_params=pltpu.CompilerParams(vmem_limit_bytes=SMALL_LIMIT),
        cost_estimate=pl.CostEstimate(flops=6 * 10**9, bytes_accessed=4 * 1024 * 1024, transcendentals=0),
        name="factor",
    )(*inputs)
    out = list(out)
    below = out.pop(0) if left else None
    return (below,) + tuple(out)


def apply_inverse(value, refs):
    ids = lambda axis: lax.broadcasted_iota(jnp.int32, (TILE, BLOCK), axis)
    lower, right = [], []
    for k in range(BLOCK // TILE):
        rest, panel = refs[k][:TILE], refs[k][TILE:]
        unit = jnp.where(ids(1) == ids(0) + k * TILE, 1.0, 0.0)
        lower.append(jnp.where(ids(1) < k * TILE, rest, unit))
        right.append(jnp.where(ids(1) < (k + 1) * TILE, panel, 0.0))
    lower, right = jnp.concatenate(lower, axis=0), jnp.concatenate(right, axis=0)
    middle = lax.dot_general(value, right, NT, precision=HIGH, preferred_element_type=jnp.float32)
    return jnp.dot(middle, lower, precision=HIGH, preferred_element_type=jnp.float32)


def final_kernel(step_size, chunk, owner_ref, tiles_ref, me_ref, packed_ref, gram_ref, slab_ref, res_ref, coef_ref, base_ref, *refs):
    factors, refs = refs[: 2 * (BLOCK // TILE)], refs[2 * (BLOCK // TILE) :]
    res_out, coef_out, upd_ref, wide_ref, ahead_ref, res_buf, tile_buf, res_sems, tile_sems = refs
    rows, targets = res_ref.shape
    own = targets // packed_ref.shape[0]
    exact = STEPS * own
    count = BLOCK // TILE

    def gradient(s):
        high = packed_ref[:, s * own : (s + 1) * own].astype(jnp.float32)
        low = packed_ref[:, exact + s * own : exact + (s + 1) * own].astype(jnp.float32)
        return (high + low).reshape(targets, BLOCK)

    dot = functools.partial(jnp.dot, preferred_element_type=jnp.float32)
    first = apply_inverse(gradient(0), factors[:count]) * step_size
    high = first.astype(jnp.bfloat16)
    low = (first - high.astype(jnp.float32)).astype(jnp.bfloat16)
    cross = packed_ref[:, 2 * exact :].reshape(BLOCK, BLOCK)
    block_part = dot(high, gram_ref[...]) + dot(low, gram_ref[...])
    again = gradient(1) - dot(high, cross) - RIDGE * block_part
    second = apply_inverse(again, factors[count:]) * step_size
    wide_ref[:, :BLOCK] = first
    wide_ref[:, BLOCK:] = second
    upd_ref[:, :BLOCK] = high
    upd_ref[:, BLOCK:] = second.astype(jnp.bfloat16)

    def change_of(s, k):
        at = s * BLOCK + k * TILE
        return jnp.transpose(wide_ref[:, at : at + TILE])

    def tile_rows(s, k):
        return pl.ds(pl.multiple_of(tiles_ref[s, k] * TILE, TILE), TILE)

    def tile_copy(s, k):
        return pltpu.make_async_copy(tile_buf.at[s, k], coef_out.at[tile_rows(s, k), :], tile_sems.at[s, k])

    owned = [owner_ref[s] == me_ref[0] for s in range(STEPS)]

    def writes(s, k):
        kept = owned[s]
        for later in range(s + 1, STEPS):
            for j in range(count):
                kept = kept & jnp.logical_not(owned[later] & (tiles_ref[later, j] == tiles_ref[s, k]))
        return kept

    for s in range(STEPS):
        for k in range(count):

            @pl.when(writes(s, k))
            def _():
                tile_buf[s, k] = coef_ref[tile_rows(s, k), :] + change_of(s, k)
                for earlier in range(s):
                    for j in range(count):

                        @pl.when(owned[earlier] & (tiles_ref[earlier, j] == tiles_ref[s, k]))
                        def _():
                            tile_buf[s, k] += change_of(earlier, j)

                tile_copy(s, k).start()

    chunks = rows // chunk
    rows_of = lambda i: pl.ds(pl.multiple_of(i * chunk, chunk), chunk)

    def res_copy(i):
        return pltpu.make_async_copy(res_buf.at[rows_of(i), :], res_out.at[rows_of(i), :], res_sems.at[i])

    def product(i):
        return jnp.dot(upd_ref[...], slab_ref[:, rows_of(i)], preferred_element_type=jnp.float32)

    ahead_ref[...] = product(0)

    def body(i, _):
        change = ahead_ref[...]
        ahead = product(jnp.minimum(i + 1, chunks - 1))
        res_buf[rows_of(i), :] = res_ref[rows_of(i), :] - jnp.transpose(change)
        ahead_ref[...] = ahead
        res_copy(i).start()
        return 0

    lax.fori_loop(0, chunks, body, 0)
    for i in range(rows // chunk):
        res_copy(i).wait()
    for s in range(STEPS):
        for k in range(count):

            @pl.when(writes(s, k))
            def _():
                tile_copy(s, k).wait()


def finish(owner, tiles, me, packed, gram12, slab, residual, coefficients, base, factors, step_size, chunk=512):
    rows, targets = residual.shape
    both = STEPS * BLOCK
    count = BLOCK // TILE
    smem, vmem, hbm = (pl.BlockSpec(memory_space=space) for space in (pltpu.SMEM, pltpu.VMEM, pltpu.HBM))
    return pl.pallas_call(
        functools.partial(final_kernel, step_size, chunk),
        in_specs=[smem] * 3 + [vmem] * 5 + [hbm] + [vmem] * len(factors),
        out_specs=(hbm, hbm),
        out_shape=(
            pltpu.HBM(residual.shape, jnp.float32),
            pltpu.HBM(residual.shape, jnp.float32),
        ),
        scratch_shapes=[
            pltpu.VMEM((targets, both), jnp.bfloat16),
            pltpu.VMEM((targets, both), jnp.float32),
            pltpu.VMEM((targets, chunk), jnp.float32),
            pltpu.VMEM((rows, targets), jnp.float32),
            pltpu.VMEM((STEPS, count, TILE, targets), jnp.float32),
            pltpu.SemaphoreType.DMA((rows // chunk,)),
            pltpu.SemaphoreType.DMA((STEPS, count)),
        ],
        input_output_aliases={8: 1},
        compiler_params=pltpu.CompilerParams(vmem_limit_bytes=VMEM_LIMIT),
        cost_estimate=pl.CostEstimate(
            flops=2 * rows * both * targets, bytes_accessed=rows * (both * 2 + targets * 16), transcendentals=0
        ),
        name="finish",
    )(owner, tiles, me, packed, gram12, in_vmem(slab), in_vmem(residual), in_vmem(coefficients), base, *factors)


def local(features, residual, coefficients, block_owner, block_tiles):
    rows_dev, width = features.shape
    targets = residual.shape[1]
    sub_count = lax.axis_size("sub")
    devices = lax.axis_size("rows") * sub_count
    me = lax.axis_index(AXES).astype(jnp.int32)
    scale = 1.0 / width
    step_size = 1.0 / math.sqrt(rows_dev * devices)
    spread = Spread(AXES, sub_count) if devices <= 32 else Spread(("rows",), 1)
    groups = spread.count
    own = targets // groups

    wide = features.astype(jnp.float32)
    norms = (jnp.sum(wide * wide, axis=1) * scale).reshape(1, rows_dev)
    block, norms = fetch_blocks(features, norms, block_owner, block_tiles, me, devices, sub_count)
    slab, pieces = slabs(block, features, norms, residual, coefficients, scale, groups)
    if spread.axes != AXES:
        pieces = lax.psum(pieces, "sub")
    core, on_core = bit_of(me, sub_count), (me & sub_count) != 0
    rest, gram12 = gram(block, core.reshape(1), scale, slab)
    factors, base = ([], []), None

    def beside(hop, index, rest):
        then, got = hop
        below, mine, *copied = factor_step(rest, index, slab, coefficients if index == 0 else None)
        got, below, mine = lax.optimization_barrier((got, below, mine))
        other = swap(mine, AXES, sub_count)
        factors[0].append(jnp.where(on_core, other, mine))
        factors[1].append(jnp.where(on_core, mine, other))
        return then(got), below, copied

    value = spread.core_sum(pieces)
    value, rest, (base,) = beside(spread.near_sum(value, STEPS * own), 0, rest)
    for index, mask in enumerate(spread.far):
        value, rest, _ = beside(spread.far_sum(value, STEPS * own, mask), 1 + index, rest)
    packed, rest, _ = beside(spread.near_gather(pack(value, STEPS * own)), 3, rest)
    packed = spread.core_gather(packed)
    return finish(
        block_owner, block_tiles, me.reshape(1), packed, gram12, slab, residual, coefficients, base,
        factors[0] + factors[1], step_size,
    )


def solution(mesh):
    row_spec = P(AXES, None)
    return jax.shard_map(
        local,
        mesh=mesh,
        in_specs=(row_spec, row_spec, row_spec, P(), P()),
        out_specs=(row_spec, row_spec),
        check_vma=False,
    )
```

```python
import functools
import math

import jax
import jax.numpy as jnp
from jax import lax
from jax.experimental import pallas as pl
from jax.experimental.pallas import tpu as pltpu
from jax.sharding import PartitionSpec as P

BLOCK = 512
TILE = 128
STEPS = 2
RIDGE = 0.5
AXES = ("rows", "sub")
HIGH = lax.Precision.HIGHEST
NT = (((1,), (1,)), ((), ()))
LOG2E = math.log2(math.e)
VMEM_LIMIT = 16 * 1024 * 1024
SMALL_LIMIT = 12 * 1024 * 1024


def pick_kernel(tiles_ref, core_ref, feat_ref, keep_ref, send_ref, sems):
    per_half = keep_ref.shape[1] // TILE
    copies = []
    for turn, out in enumerate((keep_ref, send_ref)):
        half = core_ref[0] if turn == 0 else 1 - core_ref[0]
        for s in range(STEPS):
            for i in range(per_half):
                source = pl.multiple_of(tiles_ref[s, half * per_half + i] * TILE, TILE)
                copies.append(
                    pltpu.make_async_copy(
                        feat_ref.at[pl.ds(source, TILE), :],
                        out.at[s, pl.ds(i * TILE, TILE), :],
                        sems.at[turn, s, i],
                    )
                )
    for copy in copies:
        copy.start()
    for copy in copies:
        copy.wait()


def pick_halves(features, block_tiles, core):
    width = features.shape[1]
    half = jax.ShapeDtypeStruct((STEPS, BLOCK // 2, width), features.dtype)
    return pl.pallas_call(
        pick_kernel,
        grid_spec=pltpu.PrefetchScalarGridSpec(
            num_scalar_prefetch=2,
            grid=(1,),
            in_specs=[pl.BlockSpec(memory_space=pltpu.HBM)],
            out_specs=[pl.BlockSpec(half.shape, lambda i, *_: (0, 0, 0))] * 2,
            scratch_shapes=[pltpu.SemaphoreType.DMA((2, STEPS, BLOCK // 2 // TILE))],
        ),
        out_shape=(half, half),
        compiler_params=pltpu.CompilerParams(vmem_limit_bytes=SMALL_LIMIT),
        name="pick",
    )(pltpu.with_memory_space_constraint(block_tiles, pltpu.HBM), core, pltpu.with_memory_space_constraint(features, pltpu.HBM))


def swap(value, axes, flip):
    flip_of = flip if callable(flip) else lambda i: flip
    return lax.ppermute(value, axes, [(i, i ^ flip_of(i)) for i in range(lax.axis_size(axes))])


def bit_of(index, mask):
    return ((index & mask) != 0).astype(jnp.int32)


def swap_among(pick, me, axes, low, high):
    place = bit_of(me, low) + 2 * bit_of(me, high)
    flips = [0, low, high, low | high]
    return place, [swap(pick(place ^ c), axes, flips[c]) for c in (1, 2, 3)]


def ordered(parts, me, low, high, axis):
    one, two = (me & low) != 0, (me & high) != 0
    parts = [jnp.where(one, parts[c ^ 1], parts[c]) for c in range(4)]
    return jnp.stack([jnp.where(two, parts[c ^ 2], parts[c]) for c in range(4)], axis=axis)


def fetch_blocks(features, norms, block_owner, block_tiles, me, devices, core):
    width = features.shape[1]
    low, high = 1, 2 * core
    differs = lambda mask: (((block_owner ^ me) & mask) != 0)[:, None, None]
    on_core = (me & core) != 0

    keep, send = pick_halves(features, block_tiles, bit_of(me, core).reshape(1))
    half = jnp.where(differs(core), swap(send, AXES, core), keep)
    quarters = half.reshape(STEPS, 4, BLOCK // 8, width)
    pick = lambda place: lax.dynamic_index_in_dim(quarters, place, 1, False)
    place, got = swap_among(pick, me, AXES, low, high)
    part = jnp.where(
        differs(high),
        jnp.where(differs(low), got[2], got[1]),
        jnp.where(differs(low), got[0], pick(place)),
    )
    far = [1 << b for b in range(devices.bit_length() - 1) if 1 << b not in (core, low, high)]
    hops = []
    for one, two in zip(far[::2], far[1::2]):
        for first, second in ((one, two), (two, one)):
            flip = lambda i, first=first, second=second: second if i & core else first
            hops.append((flip, jnp.where(on_core, second, first)))
    if len(far) % 2:
        hops.append((far[-1], far[-1]))
    for hop, (flip, mask) in enumerate(hops):
        other = swap(part, AXES, flip)
        if hop == len(hops) - 2:
            other, norms = lax.optimization_barrier((other, norms))
        part = jnp.where(differs(mask), other, part)
    _, got = swap_among(lambda place: part, me, AXES, low, high)
    half = ordered([part] + got, me, low, high, 1)
    other = swap(half, AXES, core)
    both = jnp.stack([jnp.where(on_core, other, half), jnp.where(on_core, half, other)], axis=1)
    return both.reshape(STEPS * BLOCK, width), norms


def pack(value, exact):
    high = lax.reduce_precision(value[..., :exact, :], 8, 7)
    low = value[..., :exact, :] - high
    return jnp.concatenate([part.astype(jnp.bfloat16) for part in (high, low, value[..., exact:, :])], axis=-2)


def unpack(value, exact):
    value = value.astype(jnp.float32)
    return jnp.concatenate([value[..., :exact, :] + value[..., exact : 2 * exact, :], value[..., 2 * exact :, :]], axis=-2)


class Spread:
    def __init__(self, axes, core):
        self.axes, self.core = axes, core
        self.me = lax.axis_index(axes).astype(jnp.int32)
        self.near = [1 << b for b in range(3) if 1 << b != core]
        self.far = [1 << b for b in range(3, lax.axis_size(axes).bit_length() - 1)]
        self.count = 8
        self.core_axis = 2 - (core.bit_length() - 1)

    def core_sum(self, value):
        value = value.reshape((2,) * 3 + value.shape[1:])
        zero, one = (lax.index_in_dim(value, i, self.core_axis, False) for i in (0, 1))
        bit = (self.me & self.core) != 0
        value = jnp.where(bit, one, zero) + swap(jnp.where(bit, zero, one), self.axes, self.core)
        return value.reshape((4,) + value.shape[2:])

    def near_sum(self, value, exact):
        packed = pack(value, exact)
        pick = lambda array, place: lax.dynamic_index_in_dim(array, place, 0, False)
        place, got = swap_among(lambda place: pick(packed, place), self.me, self.axes, *self.near)
        return lambda got: pick(value, place) + unpack(got[0], exact) + unpack(got[1], exact) + unpack(got[2], exact), got

    def far_sum(self, value, exact, mask):
        return lambda got: value + unpack(got[0], exact), [swap(pack(value, exact), self.axes, mask)]

    def near_gather(self, value):
        _, got = swap_among(lambda place: value, self.me, self.axes, *self.near)
        return lambda got: ordered([value] + got, self.me, *self.near, 0), got

    def core_gather(self, value):
        rest = value.shape[1:]
        value = value.reshape((2, 2) + rest)
        bit = (self.me & self.core) != 0
        got = swap(value, self.axes, self.core)
        value = jnp.stack([jnp.where(bit, got, value), jnp.where(bit, value, got)], axis=self.core_axis)
        return value.reshape((self.count,) + rest)


def scaled_norm(rows, scale):
    wide = rows.astype(jnp.float32)
    return jnp.sum(wide * wide, axis=1, keepdims=True) * scale


def gram_kernel(scale, core_ref, block_ref, slab_ref, own_ref, cross_ref):
    mine = block_ref[pl.ds(pl.multiple_of(core_ref[0] * BLOCK, BLOCK), BLOCK), :]
    eye = jnp.where(
        lax.broadcasted_iota(jnp.int32, (BLOCK, BLOCK), 0)
        == lax.broadcasted_iota(jnp.int32, (BLOCK, BLOCK), 1),
        RIDGE,
        0.0,
    )
    for left, right, shift, out in (
        (mine, mine, eye, own_ref),
        (block_ref[:BLOCK], block_ref[BLOCK:], 0.0, cross_ref),
    ):
        dots = lax.dot_general(left, right, NT, preferred_element_type=jnp.float32)
        right_norm = scaled_norm(right, scale)
        row = jnp.transpose(jnp.broadcast_to(right_norm, (BLOCK, 128)))[:1]
        value = jnp.exp(dots * (2.0 * scale) - scaled_norm(left, scale) - row)
        out[...] = (value + shift).astype(out.dtype)


def gram(block, core, scale, slab):
    square = (BLOCK, BLOCK)
    vmem = pl.BlockSpec(memory_space=pltpu.VMEM)
    return pl.pallas_call(
        functools.partial(gram_kernel, scale),
        in_specs=[pl.BlockSpec(memory_space=pltpu.SMEM), vmem, vmem],
        out_shape=(jax.ShapeDtypeStruct(square, jnp.float32), jax.ShapeDtypeStruct(square, jnp.bfloat16)),
        compiler_params=pltpu.CompilerParams(vmem_limit_bytes=SMALL_LIMIT),
        cost_estimate=pl.CostEstimate(
            flops=2 * 2 * BLOCK**3, bytes_accessed=4 * BLOCK * BLOCK * 4, transcendentals=2 * BLOCK**2
        ),
        name="gram",
    )(core, block, in_vmem(slab))


def slab_kernel(scale, chunk, block_ref, feat_ref, norm_ref, res_ref, coef_ref, slab_ref, piece_ref, bnorm, grad, cross, ahead_ref):
    scale2 = scale * LOG2E
    norm = scaled_norm(block_ref[...], scale2)
    bnorm[...] = jnp.broadcast_to(norm, bnorm.shape)
    grad[...] = jnp.zeros_like(grad)
    cross[...] = jnp.zeros_like(cross)
    part = BLOCK // 2
    parts = STEPS * BLOCK // part
    chunks = feat_ref.shape[0] // chunk
    rows_of = lambda i: pl.ds(pl.multiple_of(i * chunk, chunk), chunk)
    at_of = lambda p: slice(p * part, (p + 1) * part)

    def product(i, p):
        return lax.dot_general(block_ref[at_of(p)], feat_ref[rows_of(i), :], NT, preferred_element_type=jnp.float32)

    ahead_ref[...] = product(0, 0)

    def body(i, _):
        rows = rows_of(i)
        weighted = (res_ref[rows, :] - RIDGE * coef_ref[rows, :]).astype(jnp.bfloat16)
        norm_row = norm_ref[:, rows] * LOG2E
        dots = ahead_ref[...]
        for p in range(parts):
            ahead = product(i, p + 1) if p + 1 < parts else product(jnp.minimum(i + 1, chunks - 1), 0)
            norm_wide = jnp.concatenate([bnorm[at_of(p)]] * (chunk // bnorm.shape[1]), axis=1)
            slab = jnp.exp2(dots * (2.0 * scale2) - norm_wide - norm_row).astype(jnp.bfloat16)
            slab_ref[at_of(p), rows] = slab
            grad[at_of(p)] += jnp.dot(slab, weighted, preferred_element_type=jnp.float32)
            dots = ahead
        ahead_ref[...] = dots
        cross[...] += lax.dot_general(
            slab_ref[:BLOCK, rows], slab_ref[BLOCK:, rows], NT, preferred_element_type=jnp.float32
        )
        return 0

    lax.fori_loop(0, chunks, body, 0, unroll=2)
    grads = jnp.transpose(grad[...])
    groups = piece_ref.shape[0]
    own, depth = grads.shape[0] // groups, BLOCK // groups
    for d in range(groups):
        for s in range(STEPS):
            piece_ref[d, s * own : (s + 1) * own] = grads[d * own : (d + 1) * own, s * BLOCK : (s + 1) * BLOCK]
        piece_ref[d, STEPS * own :] = cross[d * depth : (d + 1) * depth]


def in_vmem(value):
    return pltpu.with_memory_space_constraint(value, pltpu.VMEM)


def slabs(block, features, norms, residual, coefficients, scale, groups, chunk=512):
    rows, width = features.shape
    targets = residual.shape[1]
    both = STEPS * BLOCK
    piece = (groups, STEPS * targets // groups + BLOCK // groups, BLOCK)
    return pl.pallas_call(
        functools.partial(slab_kernel, scale, chunk),
        out_shape=(pltpu.VMEM((both, rows), jnp.bfloat16), jax.ShapeDtypeStruct(piece, jnp.float32)),
        scratch_shapes=[
            pltpu.VMEM((both, 128), jnp.float32),
            pltpu.VMEM((both, targets), jnp.float32),
            pltpu.VMEM((BLOCK, BLOCK), jnp.float32),
            pltpu.VMEM((BLOCK // 2, chunk), jnp.float32),
        ],
        compiler_params=pltpu.CompilerParams(vmem_limit_bytes=VMEM_LIMIT),
        cost_estimate=pl.CostEstimate(
            flops=2 * rows * both * (width + targets + BLOCK // 2),
            bytes_accessed=rows * (width * 2 + targets * 8 + both * 2),
            transcendentals=rows * both,
        ),
        name="slabs",
    )(block, in_vmem(features), norms, in_vmem(residual), in_vmem(coefficients))


def eliminate(tiles, t, lane, scaled_ref, waiting):
    start, shape = 8 * t, tiles[t].shape
    wide = lambda tile, k: jnp.broadcast_to(tile[:, start + k : start + k + 1], shape)
    rows = [jnp.broadcast_to(tiles[t][k : k + 1], shape) for k in range(8)]
    at = {(i, k): wide(rows[i], k) for i in range(8) for k in range(i, 8)}
    units = [jnp.where(lane == start + k, 1.0, 0.0) for k in range(8)]
    rows = [row + unit for row, unit in zip(rows, units)]
    total, lower = [None] * 8, {}
    waiting, share = list(waiting), -(-len(waiting) // 4)
    for r in range(0, 8, 2):
        p, m, q = at[r, r], at[r, r + 1], at[r + 1, r + 1]
        det = p * q - m * m
        guess = pl.reciprocal(det, approx=True)
        for _ in range(min(share, len(waiting))):
            waiting.pop(0)()
        refine = 2.0 - det * guess
        inverse = guess * refine
        for k in range(r + 2, 8):
            first = q * at[r, k] - m * at[r + 1, k]
            second = p * at[r + 1, k] - m * at[r, k]
            lower[r, k], lower[r + 1, k] = first * inverse, second * inverse
            for i in range(r + 2, k + 1):
                product = at[r, i] * first + at[r + 1, i] * second
                change = product * guess * refine if k < r + 4 else product * inverse
                at[i, k] = at[i, k] - change
            rows[k] = rows[k] - (first * rows[r] + second * rows[r + 1]) * inverse
        total[r] = (q * rows[r] - m * rows[r + 1]) * inverse
        total[r + 1] = (p * rows[r + 1] - m * rows[r]) * inverse
    for r in (4, 2, 0):
        for k in range(7, r + 1, -1):
            total[r] = total[r] - lower[r, k] * total[k]
            total[r + 1] = total[r + 1] - lower[r + 1, k] * total[k]
    for k in range(8):
        scaled_ref[start + k : start + k + 1] = total[k][:1] - units[k][:1]

    def update(u):
        parts = [wide(tiles[u], k) * total[k] for k in range(8)]
        while len(parts) > 1:
            parts = [x + y for x, y in zip(parts[::2], parts[1::2])]
        tiles[u] = tiles[u] - parts[0]

    if t + 1 < len(tiles):
        update(t + 1)
    return [functools.partial(update, u) for u in range(t + 2, len(tiles))]


def factor_kernel(index, copied, *refs):
    refs = list(refs)
    rest_ref, _ = refs.pop(0), refs.pop(0)
    before_ref = refs.pop(0) if index else None
    scaled = refs.pop()
    if copied:
        sem = refs.pop()
        copy = pltpu.make_async_copy(refs.pop(0), refs.pop(), sem)
        copy.start()
    factor_ref = refs[0]
    here = slice(index * TILE, (index + 1) * TILE)
    dot = functools.partial(lax.dot_general, precision=HIGH, preferred_element_type=jnp.float32)
    plain = (((1,), (0,)), ((), ()))

    def updated(rows):
        if not index:
            return rest_ref[rows]
        then = slice((index - 1) * TILE, index * TILE)
        old = rest_ref[rows]
        inside = lax.broadcasted_iota(jnp.int32, old.shape, 1) // TILE == index - 1
        return jnp.where(inside, 0.0, old) - dot(rest_ref[rows, then], before_ref[TILE:], plain)

    first = TILE if index == 1 else 0
    factor_ref[:TILE] = updated(slice(first, first + TILE))
    row_ids = lax.broadcasted_iota(jnp.int32, (TILE, TILE), 0)
    col_ids = lax.broadcasted_iota(jnp.int32, (TILE, TILE), 1)
    lane = lax.broadcasted_iota(jnp.int32, (8, TILE), 1)
    tiles = [factor_ref[8 * t : 8 * t + 8, here] for t in range(TILE // 8)]
    if len(refs) > 1:
        refs[1][...] = updated(slice(first + TILE, rest_ref.shape[0]))
    waiting = []
    for t in range(TILE // 8):
        waiting = eliminate(tiles, t, lane, scaled, waiting)
    start = row_ids - row_ids % 8
    lower = jnp.where(col_ids < start, jnp.concatenate(tiles, axis=0), 0.0)
    lower = lower + jnp.where(col_ids == row_ids, 1.0, 0.0)
    right = jnp.where(col_ids < start + 8, scaled[...], 0.0)
    inv = dot(lower, right, (((0,), (0,)), ((), ())))
    panel = dot(inv, factor_ref[:TILE], plain)
    inside = lax.broadcasted_iota(jnp.int32, panel.shape, 1) // TILE == index
    factor_ref[TILE:] = jnp.where(inside, jnp.concatenate([inv] * (BLOCK // TILE), axis=1), panel)
    if copied:
        copy.wait()


def factor_step(rest, index, slab, before=None, copied=None):
    left = BLOCK - (index + 1) * TILE
    vmem, hbm = pl.BlockSpec(memory_space=pltpu.VMEM), pl.BlockSpec(memory_space=pltpu.HBM)
    out = [jax.ShapeDtypeStruct((2 * TILE, BLOCK), jnp.float32)]
    inputs, scratch = [rest, in_vmem(slab)], [pltpu.VMEM((TILE, TILE), jnp.float32)]
    if index:
        inputs.append(before)
        if left:
            out.append(jax.ShapeDtypeStruct((left, BLOCK), jnp.float32))
    in_specs, out_specs = [vmem] * len(inputs), [vmem] * len(out)
    if copied is not None:
        inputs.append(in_vmem(copied))
        in_specs.append(vmem)
        out.append(pltpu.HBM(copied.shape, copied.dtype))
        out_specs.append(hbm)
        scratch.insert(0, pltpu.SemaphoreType.DMA)
    return pl.pallas_call(
        functools.partial(factor_kernel, index, copied is not None),
        in_specs=in_specs,
        out_specs=tuple(out_specs),
        out_shape=tuple(out),
        scratch_shapes=scratch,
        compiler_params=pltpu.CompilerParams(vmem_limit_bytes=SMALL_LIMIT),
        cost_estimate=pl.CostEstimate(flops=6 * 10**9, bytes_accessed=4 * 1024 * 1024, transcendentals=0),
        name="factor",
    )(*inputs)


def apply_inverse(value, refs):
    upto = lambda k: slice(0, k * TILE)
    dot = functools.partial(lax.dot_general, precision=HIGH, preferred_element_type=jnp.float32)
    count = BLOCK // TILE
    middle = [dot(value[:, upto(k + 1)], refs[k][TILE:, upto(k + 1)], NT) for k in range(count)]
    added = {k: dot(middle[k], refs[k][:TILE, upto(k)], (((1,), (0,)), ((), ()))) for k in range(1, count)}
    out = []
    for j in range(count):
        total = middle[j]
        for k in range(j + 1, count):
            total = total + added[k][:, j * TILE : (j + 1) * TILE]
        out.append(total)
    return jnp.concatenate(out, axis=1)


def final_kernel(step_size, chunk, owner_ref, tiles_ref, me_ref, packed_ref, gram_ref, slab_ref, res_ref, coef_ref, base_ref, *refs):
    factors, refs = refs[: 2 * (BLOCK // TILE)], refs[2 * (BLOCK // TILE) :]
    res_out, coef_out, upd_ref, wide_ref, ahead_ref, res_buf, tile_buf, res_sems, tile_sems = refs
    rows, targets = res_ref.shape
    own = targets // packed_ref.shape[0]
    exact = STEPS * own
    count = BLOCK // TILE

    def gradient(s):
        high = packed_ref[:, s * own : (s + 1) * own].astype(jnp.float32)
        low = packed_ref[:, exact + s * own : exact + (s + 1) * own].astype(jnp.float32)
        return (high + low).reshape(targets, BLOCK)

    dot = functools.partial(jnp.dot, preferred_element_type=jnp.float32)
    first = apply_inverse(gradient(0), factors[:count]) * step_size
    high = first.astype(jnp.bfloat16)
    low = (first - high.astype(jnp.float32)).astype(jnp.bfloat16)
    cross = packed_ref[:, 2 * exact :].reshape(BLOCK, BLOCK)
    block_part = dot(high, gram_ref[...]) + dot(low, gram_ref[...])
    again = gradient(1) - dot(high, cross) - RIDGE * block_part
    second = apply_inverse(again, factors[count:]) * step_size
    wide_ref[:, :BLOCK] = first
    wide_ref[:, BLOCK:] = second
    upd_ref[:, :BLOCK] = high
    upd_ref[:, BLOCK:] = second.astype(jnp.bfloat16)

    def change_of(s, k):
        at = s * BLOCK + k * TILE
        return jnp.transpose(wide_ref[:, at : at + TILE])

    def tile_rows(s, k):
        return pl.ds(pl.multiple_of(tiles_ref[s, k] * TILE, TILE), TILE)

    def tile_copy(s, k):
        return pltpu.make_async_copy(tile_buf.at[s, k], coef_out.at[tile_rows(s, k), :], tile_sems.at[s, k])

    owned = [owner_ref[s] == me_ref[0] for s in range(STEPS)]

    def writes(s, k):
        kept = owned[s]
        for later in range(s + 1, STEPS):
            for j in range(count):
                kept = kept & jnp.logical_not(owned[later] & (tiles_ref[later, j] == tiles_ref[s, k]))
        return kept

    for s in range(STEPS):
        for k in range(count):

            @pl.when(writes(s, k))
            def _():
                tile_buf[s, k] = coef_ref[tile_rows(s, k), :] + change_of(s, k)
                for earlier in range(s):
                    for j in range(count):

                        @pl.when(owned[earlier] & (tiles_ref[earlier, j] == tiles_ref[s, k]))
                        def _():
                            tile_buf[s, k] += change_of(earlier, j)

                tile_copy(s, k).start()

    chunks = rows // chunk
    rows_of = lambda i: pl.ds(pl.multiple_of(i * chunk, chunk), chunk)

    def res_copy(i):
        return pltpu.make_async_copy(res_buf.at[rows_of(i), :], res_out.at[rows_of(i), :], res_sems.at[i])

    def product(i):
        return jnp.dot(upd_ref[...], slab_ref[:, rows_of(i)], preferred_element_type=jnp.float32)

    ahead_ref[...] = product(0)

    def body(i, _):
        change = ahead_ref[...]
        ahead = product(jnp.minimum(i + 1, chunks - 1))
        res_buf[rows_of(i), :] = res_ref[rows_of(i), :] - jnp.transpose(change)
        ahead_ref[...] = ahead
        res_copy(i).start()
        return 0

    lax.fori_loop(0, chunks, body, 0)
    for i in range(rows // chunk):
        res_copy(i).wait()
    for s in range(STEPS):
        for k in range(count):

            @pl.when(writes(s, k))
            def _():
                tile_copy(s, k).wait()


def finish(owner, tiles, me, packed, gram12, slab, residual, coefficients, base, factors, step_size, chunk=512):
    rows, targets = residual.shape
    both = STEPS * BLOCK
    count = BLOCK // TILE
    smem, vmem, hbm = (pl.BlockSpec(memory_space=space) for space in (pltpu.SMEM, pltpu.VMEM, pltpu.HBM))
    return pl.pallas_call(
        functools.partial(final_kernel, step_size, chunk),
        in_specs=[smem] * 3 + [vmem] * 5 + [hbm] + [vmem] * len(factors),
        out_specs=(hbm, hbm),
        out_shape=(
            pltpu.HBM(residual.shape, jnp.float32),
            pltpu.HBM(residual.shape, jnp.float32),
        ),
        scratch_shapes=[
            pltpu.VMEM((targets, both), jnp.bfloat16),
            pltpu.VMEM((targets, both), jnp.float32),
            pltpu.VMEM((targets, chunk), jnp.float32),
            pltpu.VMEM((rows, targets), jnp.float32),
            pltpu.VMEM((STEPS, count, TILE, targets), jnp.float32),
            pltpu.SemaphoreType.DMA((rows // chunk,)),
            pltpu.SemaphoreType.DMA((STEPS, count)),
        ],
        input_output_aliases={8: 1},
        compiler_params=pltpu.CompilerParams(vmem_limit_bytes=VMEM_LIMIT),
        cost_estimate=pl.CostEstimate(
            flops=2 * rows * both * targets, bytes_accessed=rows * (both * 2 + targets * 16), transcendentals=0
        ),
        name="finish",
    )(owner, tiles, me, packed, gram12, in_vmem(slab), in_vmem(residual), in_vmem(coefficients), base, *factors)


def local(features, residual, coefficients, block_owner, block_tiles):
    rows_dev, width = features.shape
    targets = residual.shape[1]
    sub_count = lax.axis_size("sub")
    devices = lax.axis_size("rows") * sub_count
    me = lax.axis_index(AXES).astype(jnp.int32)
    scale = 1.0 / width
    step_size = 1.0 / math.sqrt(rows_dev * devices)
    spread = Spread(AXES, sub_count) if devices <= 32 else Spread(("rows",), 1)
    groups = spread.count
    own = targets // groups

    wide = features.astype(jnp.float32)
    norms = (jnp.sum(wide * wide, axis=1) * scale).reshape(1, rows_dev)
    block, norms = fetch_blocks(features, norms, block_owner, block_tiles, me, devices, sub_count)
    slab, pieces = slabs(block, features, norms, residual, coefficients, scale, groups)
    if spread.axes != AXES:
        pieces = lax.psum(pieces, "sub")
    core, on_core = bit_of(me, sub_count), (me & sub_count) != 0
    rest, gram12 = gram(block, core.reshape(1), scale, slab)
    factors, before, copied = ([], []), None, []

    def beside(hop, index, rest):
        nonlocal before
        then, got = hop
        mine, *given = factor_step(rest, index, slab, before, None if index else coefficients)
        if not index:
            copied.append(given.pop())
        got, mine, given = lax.optimization_barrier((got, mine, given))
        before = mine
        other = swap(mine, AXES, sub_count)
        factors[0].append(jnp.where(on_core, other, mine))
        factors[1].append(jnp.where(on_core, mine, other))
        return then(got), given[0] if given else rest

    value = spread.core_sum(pieces)
    value, rest = beside(spread.near_sum(value, STEPS * own), 0, rest)
    for index, mask in enumerate(spread.far):
        value, rest = beside(spread.far_sum(value, STEPS * own, mask), 1 + index, rest)
    packed, rest = beside(spread.near_gather(pack(value, STEPS * own)), 3, rest)
    packed = spread.core_gather(packed)
    return finish(
        block_owner, block_tiles, me.reshape(1), packed, gram12, slab, residual, coefficients, copied[0],
        factors[0] + factors[1], step_size,
    )


def solution(mesh):
    row_spec = P(AXES, None)
    return jax.shard_map(
        local,
        mesh=mesh,
        in_specs=(row_spec, row_spec, row_spec, P(), P()),
        out_specs=(row_spec, row_spec),
        check_vma=False,
    )
```

```python
import functools
import math

import jax
import jax.numpy as jnp
from jax import lax
from jax.experimental import pallas as pl
from jax.experimental.pallas import tpu as pltpu
from jax.sharding import PartitionSpec as P

BLOCK = 512
TILE = 128
STEPS = 2
RIDGE = 0.5
AXES = ("rows", "sub")
HIGH = lax.Precision.HIGHEST
NT = (((1,), (1,)), ((), ()))
LOG2E = math.log2(math.e)
VMEM_LIMIT = 16 * 1024 * 1024
SMALL_LIMIT = 12 * 1024 * 1024


def pick_kernel(tiles_ref, core_ref, feat_ref, keep_ref, send_ref, sems):
    per_half = keep_ref.shape[1] // TILE
    copies = []
    for turn, out in enumerate((keep_ref, send_ref)):
        half = core_ref[0] if turn == 0 else 1 - core_ref[0]
        for s in range(STEPS):
            for i in range(per_half):
                source = pl.multiple_of(tiles_ref[s, half * per_half + i] * TILE, TILE)
                copies.append(
                    pltpu.make_async_copy(
                        feat_ref.at[pl.ds(source, TILE), :],
                        out.at[s, pl.ds(i * TILE, TILE), :],
                        sems.at[turn, s, i],
                    )
                )
    for copy in copies:
        copy.start()
    for copy in copies:
        copy.wait()


def pick_halves(features, block_tiles, core):
    width = features.shape[1]
    half = jax.ShapeDtypeStruct((STEPS, BLOCK // 2, width), features.dtype)
    return pl.pallas_call(
        pick_kernel,
        grid_spec=pltpu.PrefetchScalarGridSpec(
            num_scalar_prefetch=2,
            grid=(1,),
            in_specs=[pl.BlockSpec(memory_space=pltpu.HBM)],
            out_specs=[pl.BlockSpec(half.shape, lambda i, *_: (0, 0, 0))] * 2,
            scratch_shapes=[pltpu.SemaphoreType.DMA((2, STEPS, BLOCK // 2 // TILE))],
        ),
        out_shape=(half, half),
        compiler_params=pltpu.CompilerParams(vmem_limit_bytes=SMALL_LIMIT),
        name="pick",
    )(pltpu.with_memory_space_constraint(block_tiles, pltpu.HBM), core, pltpu.with_memory_space_constraint(features, pltpu.HBM))


def swap(value, axes, flip):
    flip_of = flip if callable(flip) else lambda i: flip
    return lax.ppermute(value, axes, [(i, i ^ flip_of(i)) for i in range(lax.axis_size(axes))])


def bit_of(index, mask):
    return ((index & mask) != 0).astype(jnp.int32)


def swap_among(pick, me, axes, low, high):
    place = bit_of(me, low) + 2 * bit_of(me, high)
    flips = [0, low, high, low | high]
    return place, [swap(pick(place ^ c), axes, flips[c]) for c in (1, 2, 3)]


def ordered(parts, me, low, high, axis):
    one, two = (me & low) != 0, (me & high) != 0
    parts = [jnp.where(one, parts[c ^ 1], parts[c]) for c in range(4)]
    return jnp.stack([jnp.where(two, parts[c ^ 2], parts[c]) for c in range(4)], axis=axis)


def fetch_blocks(features, norms, block_owner, block_tiles, me, devices, core):
    width = features.shape[1]
    low, high = 1, 2 * core
    differs = lambda mask: (((block_owner ^ me) & mask) != 0)[:, None, None]
    on_core = (me & core) != 0

    keep, send = pick_halves(features, block_tiles, bit_of(me, core).reshape(1))
    half = jnp.where(differs(core), swap(send, AXES, core), keep)
    quarters = half.reshape(STEPS, 4, BLOCK // 8, width)
    pick = lambda place: lax.dynamic_index_in_dim(quarters, place, 1, False)
    place, got = swap_among(pick, me, AXES, low, high)
    part = jnp.where(
        differs(high),
        jnp.where(differs(low), got[2], got[1]),
        jnp.where(differs(low), got[0], pick(place)),
    )
    far = [1 << b for b in range(devices.bit_length() - 1) if 1 << b not in (core, low, high)]
    hops = []
    for one, two in zip(far[::2], far[1::2]):
        for first, second in ((one, two), (two, one)):
            flip = lambda i, first=first, second=second: second if i & core else first
            hops.append((flip, jnp.where(on_core, second, first)))
    if len(far) % 2:
        hops.append((far[-1], far[-1]))
    for hop, (flip, mask) in enumerate(hops):
        other = swap(part, AXES, flip)
        if hop == len(hops) - 2:
            other, norms = lax.optimization_barrier((other, norms))
        part = jnp.where(differs(mask), other, part)
    _, got = swap_among(lambda place: part, me, AXES, low, high)
    half = ordered([part] + got, me, low, high, 1)
    other = swap(half, AXES, core)
    both = jnp.stack([jnp.where(on_core, other, half), jnp.where(on_core, half, other)], axis=1)
    return both.reshape(STEPS * BLOCK, width), norms


def pack(value, exact):
    high = lax.reduce_precision(value[..., :exact, :], 8, 7)
    low = value[..., :exact, :] - high
    return jnp.concatenate([part.astype(jnp.bfloat16) for part in (high, low, value[..., exact:, :])], axis=-2)


def unpack(value, exact):
    value = value.astype(jnp.float32)
    return jnp.concatenate([value[..., :exact, :] + value[..., exact : 2 * exact, :], value[..., 2 * exact :, :]], axis=-2)


class Spread:
    def __init__(self, axes, core):
        self.axes, self.core = axes, core
        self.me = lax.axis_index(axes).astype(jnp.int32)
        self.near = [1 << b for b in range(3) if 1 << b != core]
        self.far = [1 << b for b in range(3, lax.axis_size(axes).bit_length() - 1)]
        self.count = 8
        self.core_axis = 2 - (core.bit_length() - 1)

    def core_sum(self, packed, exact):
        packed = packed.reshape((2,) * 3 + packed.shape[1:])
        zero, one = (lax.index_in_dim(packed, i, self.core_axis, False) for i in (0, 1))
        bit = (self.me & self.core) != 0
        got = swap(jnp.where(bit, zero, one), self.axes, self.core)
        value = unpack(jnp.where(bit, one, zero), exact) + unpack(got, exact)
        return value.reshape((4,) + value.shape[2:])

    def near_sum(self, value, exact):
        packed = pack(value, exact)
        pick = lambda array, place: lax.dynamic_index_in_dim(array, place, 0, False)
        place, got = swap_among(lambda place: pick(packed, place), self.me, self.axes, *self.near)
        return lambda got: pick(value, place) + unpack(got[0], exact) + unpack(got[1], exact) + unpack(got[2], exact), got

    def far_sum(self, value, exact):
        packed = pack(value, exact)
        _, got = swap_among(lambda place: packed, self.me, self.axes, *self.far)
        return lambda got: value + unpack(got[0], exact) + unpack(got[1], exact) + unpack(got[2], exact), got

    def near_gather(self, value):
        _, got = swap_among(lambda place: value, self.me, self.axes, *self.near)
        return lambda got: ordered([value] + got, self.me, *self.near, 0), got

    def core_gather(self, value):
        rest = value.shape[1:]
        value = value.reshape((2, 2) + rest)
        bit = (self.me & self.core) != 0
        got = swap(value, self.axes, self.core)
        value = jnp.stack([jnp.where(bit, got, value), jnp.where(bit, value, got)], axis=self.core_axis)
        return value.reshape((self.count,) + rest)


def scaled_norm(rows, scale):
    wide = rows.astype(jnp.float32)
    return jnp.sum(wide * wide, axis=1, keepdims=True) * scale


def kernel_of(left, right, scale):
    dots = lax.dot_general(left, right, NT, preferred_element_type=jnp.float32)
    row = jnp.transpose(jnp.broadcast_to(scaled_norm(right, scale), (BLOCK, 128)))[:1]
    return jnp.exp(dots * (2.0 * scale) - scaled_norm(left, scale) - row)


def gram_kernel(scale, core_ref, block_ref, slab_ref, own_ref):
    mine = block_ref[pl.ds(pl.multiple_of(core_ref[0] * BLOCK, BLOCK), BLOCK), :]
    diagonal = lax.broadcasted_iota(jnp.int32, (BLOCK, BLOCK), 0) == lax.broadcasted_iota(jnp.int32, (BLOCK, BLOCK), 1)
    own_ref[...] = kernel_of(mine, mine, scale) + jnp.where(diagonal, RIDGE, 0.0)


def gram(block, core, scale, slab):
    vmem = pl.BlockSpec(memory_space=pltpu.VMEM)
    return pl.pallas_call(
        functools.partial(gram_kernel, scale),
        in_specs=[pl.BlockSpec(memory_space=pltpu.SMEM), vmem, vmem],
        out_shape=jax.ShapeDtypeStruct((BLOCK, BLOCK), jnp.float32),
        compiler_params=pltpu.CompilerParams(vmem_limit_bytes=SMALL_LIMIT),
        cost_estimate=pl.CostEstimate(
            flops=2 * BLOCK**3, bytes_accessed=4 * BLOCK * BLOCK * 2, transcendentals=BLOCK**2
        ),
        name="gram",
    )(core, block, in_vmem(slab))


def slab_kernel(scale, chunk, block_ref, feat_ref, norm_ref, res_ref, coef_ref, slab_ref, piece_ref, bnorm, grad, cross, ahead_ref):
    scale2 = scale * LOG2E
    norm = scaled_norm(block_ref[...], scale2)
    bnorm[...] = jnp.broadcast_to(norm, bnorm.shape)
    grad[...] = jnp.zeros_like(grad)
    cross[...] = jnp.zeros_like(cross)
    part = BLOCK // 2
    parts = STEPS * BLOCK // part
    chunks = feat_ref.shape[0] // chunk
    rows_of = lambda i: pl.ds(pl.multiple_of(i * chunk, chunk), chunk)
    at_of = lambda p: slice(p * part, (p + 1) * part)

    def product(i, p):
        return lax.dot_general(block_ref[at_of(p)], feat_ref[rows_of(i), :], NT, preferred_element_type=jnp.float32)

    ahead_ref[...] = product(0, 0)

    def body(i, _):
        rows = rows_of(i)
        weighted = (res_ref[rows, :] - RIDGE * coef_ref[rows, :]).astype(jnp.bfloat16)
        norm_row = norm_ref[:, rows] * LOG2E
        dots = ahead_ref[...]
        for p in range(parts):
            ahead = product(i, p + 1) if p + 1 < parts else product(jnp.minimum(i + 1, chunks - 1), 0)
            norm_wide = jnp.concatenate([bnorm[at_of(p)]] * (chunk // bnorm.shape[1]), axis=1)
            slab = jnp.exp2(dots * (2.0 * scale2) - norm_wide - norm_row).astype(jnp.bfloat16)
            slab_ref[at_of(p), rows] = slab
            if p < parts // 2:
                grad[at_of(p)] += jnp.dot(slab, weighted, preferred_element_type=jnp.float32)
            dots = ahead
        ahead_ref[...] = dots
        left = jnp.concatenate([slab_ref[:BLOCK, rows], jnp.transpose(weighted)], axis=0)
        cross[...] += lax.dot_general(left, slab_ref[BLOCK:, rows], NT, preferred_element_type=jnp.float32)
        return 0

    lax.fori_loop(0, chunks, body, 0, unroll=2)
    grads = jnp.concatenate([jnp.transpose(grad[...]), cross[BLOCK:]], axis=1)
    groups = piece_ref.shape[0]
    own, depth = grads.shape[0] // groups, BLOCK // groups
    exact = STEPS * own
    high = grads.astype(jnp.bfloat16)
    low = (grads - high.astype(jnp.float32)).astype(jnp.bfloat16)
    for d in range(groups):
        for s in range(STEPS):
            there = (slice(d * own, (d + 1) * own), slice(s * BLOCK, (s + 1) * BLOCK))
            piece_ref[d, s * own : (s + 1) * own] = high[there]
            piece_ref[d, exact + s * own : exact + (s + 1) * own] = low[there]
        piece_ref[d, 2 * exact :] = cross[d * depth : (d + 1) * depth].astype(jnp.bfloat16)


def in_vmem(value):
    return pltpu.with_memory_space_constraint(value, pltpu.VMEM)


def slabs(block, features, norms, residual, coefficients, scale, groups, chunk=512):
    rows, width = features.shape
    targets = residual.shape[1]
    both = STEPS * BLOCK
    piece = (groups, 2 * STEPS * targets // groups + BLOCK // groups, BLOCK)
    return pl.pallas_call(
        functools.partial(slab_kernel, scale, chunk),
        out_shape=(pltpu.VMEM((both, rows), jnp.bfloat16), jax.ShapeDtypeStruct(piece, jnp.bfloat16)),
        scratch_shapes=[
            pltpu.VMEM((both, 128), jnp.float32),
            pltpu.VMEM((BLOCK, targets), jnp.float32),
            pltpu.VMEM((BLOCK + targets, BLOCK), jnp.float32),
            pltpu.VMEM((BLOCK // 2, chunk), jnp.float32),
        ],
        compiler_params=pltpu.CompilerParams(vmem_limit_bytes=VMEM_LIMIT),
        cost_estimate=pl.CostEstimate(
            flops=2 * rows * both * (width + targets + BLOCK // 2),
            bytes_accessed=rows * (width * 2 + targets * 8 + both * 2),
            transcendentals=rows * both,
        ),
        name="slabs",
    )(block, in_vmem(features), norms, in_vmem(residual), in_vmem(coefficients))


def eliminate(tiles, t, lane, scaled_ref, waiting):
    start, shape = 8 * t, tiles[t].shape
    wide = lambda tile, k: jnp.broadcast_to(tile[:, start + k : start + k + 1], shape)
    rows = [jnp.broadcast_to(tiles[t][k : k + 1], shape) for k in range(8)]
    at = {(i, k): wide(rows[i], k) for i in range(8) for k in range(i, 8)}
    units = [jnp.where(lane == start + k, 1.0, 0.0) for k in range(8)]
    rows = [row + unit for row, unit in zip(rows, units)]
    total, lower = [None] * 8, {}
    waiting, share = list(waiting), -(-len(waiting) // 4)
    for r in range(0, 8, 2):
        p, m, q = at[r, r], at[r, r + 1], at[r + 1, r + 1]
        det = p * q - m * m
        guess = pl.reciprocal(det, approx=True)
        for _ in range(min(share, len(waiting))):
            waiting.pop(0)()
        refine = 2.0 - det * guess
        inverse = guess * refine
        for k in range(r + 2, 8):
            first = q * at[r, k] - m * at[r + 1, k]
            second = p * at[r + 1, k] - m * at[r, k]
            lower[r, k], lower[r + 1, k] = first * inverse, second * inverse
            for i in range(r + 2, k + 1):
                product = at[r, i] * first + at[r + 1, i] * second
                change = product * guess * refine if k < r + 4 else product * inverse
                at[i, k] = at[i, k] - change
            rows[k] = rows[k] - (first * rows[r] + second * rows[r + 1]) * inverse
        total[r] = (q * rows[r] - m * rows[r + 1]) * inverse
        total[r + 1] = (p * rows[r + 1] - m * rows[r]) * inverse
    for r in (4, 2, 0):
        for k in range(7, r + 1, -1):
            total[r] = total[r] - lower[r, k] * total[k]
            total[r + 1] = total[r + 1] - lower[r + 1, k] * total[k]
    for k in range(8):
        scaled_ref[start + k : start + k + 1] = total[k][:1] - units[k][:1]

    def update(u):
        parts = [wide(tiles[u], k) * total[k] for k in range(8)]
        while len(parts) > 1:
            parts = [x + y for x, y in zip(parts[::2], parts[1::2])]
        tiles[u] = tiles[u] - parts[0]

    if t + 1 < len(tiles):
        update(t + 1)
    return [functools.partial(update, u) for u in range(t + 2, len(tiles))]


def factor_kernel(index, copied, scale, *refs):
    refs = list(refs)
    rest_ref, _ = refs.pop(0), refs.pop(0)
    before_ref = refs.pop(0) if index else None
    scaled = refs.pop()
    if copied:
        sem = refs.pop()
        copy = pltpu.make_async_copy(refs.pop(0), refs.pop(), sem)
        copy.start()
    if index == 1:
        block_ref, cross_ref = refs.pop(0), refs.pop()
        cross_ref[...] = kernel_of(block_ref[:BLOCK], block_ref[BLOCK:], scale).astype(cross_ref.dtype)
    factor_ref = refs[0]
    here = slice(index * TILE, (index + 1) * TILE)
    dot = functools.partial(lax.dot_general, precision=HIGH, preferred_element_type=jnp.float32)
    plain = (((1,), (0,)), ((), ()))

    def updated(rows):
        if not index:
            return rest_ref[rows]
        then = slice((index - 1) * TILE, index * TILE)
        old = rest_ref[rows]
        inside = lax.broadcasted_iota(jnp.int32, old.shape, 1) // TILE == index - 1
        return jnp.where(inside, 0.0, old) - dot(rest_ref[rows, then], before_ref[TILE:], plain)

    first = TILE if index == 1 else 0
    factor_ref[:TILE] = updated(slice(first, first + TILE))
    row_ids = lax.broadcasted_iota(jnp.int32, (TILE, TILE), 0)
    col_ids = lax.broadcasted_iota(jnp.int32, (TILE, TILE), 1)
    lane = lax.broadcasted_iota(jnp.int32, (8, TILE), 1)
    tiles = [factor_ref[8 * t : 8 * t + 8, here] for t in range(TILE // 8)]
    if len(refs) > 1:
        refs[1][...] = updated(slice(first + TILE, rest_ref.shape[0]))
    waiting = []
    for t in range(TILE // 8):
        waiting = eliminate(tiles, t, lane, scaled, waiting)
    start = row_ids - row_ids % 8
    lower = jnp.where(col_ids < start, jnp.concatenate(tiles, axis=0), 0.0)
    lower = lower + jnp.where(col_ids == row_ids, 1.0, 0.0)
    right = jnp.where(col_ids < start + 8, scaled[...], 0.0)
    inv = dot(lower, right, (((0,), (0,)), ((), ())))
    panel = dot(inv, factor_ref[:TILE], plain)
    inside = lax.broadcasted_iota(jnp.int32, panel.shape, 1) // TILE == index
    factor_ref[TILE:] = jnp.where(inside, jnp.concatenate([inv] * (BLOCK // TILE), axis=1), panel)
    if copied:
        copy.wait()


def factor_step(rest, index, slab, before=None, copied=None, block=None, scale=None):
    left = BLOCK - (index + 1) * TILE
    vmem, hbm = pl.BlockSpec(memory_space=pltpu.VMEM), pl.BlockSpec(memory_space=pltpu.HBM)
    out = [jax.ShapeDtypeStruct((2 * TILE, BLOCK), jnp.float32)]
    inputs, scratch = [rest, in_vmem(slab)], [pltpu.VMEM((TILE, TILE), jnp.float32)]
    if index:
        inputs.append(before)
        if left:
            out.append(jax.ShapeDtypeStruct((left, BLOCK), jnp.float32))
    if block is not None:
        inputs.append(block)
        out.append(jax.ShapeDtypeStruct((BLOCK, BLOCK), jnp.bfloat16))
    in_specs, out_specs = [vmem] * len(inputs), [vmem] * len(out)
    if copied is not None:
        inputs.append(in_vmem(copied))
        in_specs.append(vmem)
        out.append(pltpu.HBM(copied.shape, copied.dtype))
        out_specs.append(hbm)
        scratch.insert(0, pltpu.SemaphoreType.DMA)
    return pl.pallas_call(
        functools.partial(factor_kernel, index, copied is not None, scale),
        in_specs=in_specs,
        out_specs=tuple(out_specs),
        out_shape=tuple(out),
        scratch_shapes=scratch,
        compiler_params=pltpu.CompilerParams(vmem_limit_bytes=SMALL_LIMIT),
        cost_estimate=pl.CostEstimate(flops=6 * 10**9, bytes_accessed=4 * 1024 * 1024, transcendentals=0),
        name="factor",
    )(*inputs)


def apply_inverse(value, refs):
    upto = lambda k: slice(0, k * TILE)
    dot = functools.partial(lax.dot_general, precision=HIGH, preferred_element_type=jnp.float32)
    count = BLOCK // TILE
    middle = [dot(value[:, upto(k + 1)], refs[k][TILE:, upto(k + 1)], NT) for k in range(count)]
    added = {k: dot(middle[k], refs[k][:TILE, upto(k)], (((1,), (0,)), ((), ()))) for k in range(1, count)}
    out = []
    for j in range(count):
        total = middle[j]
        for k in range(j + 1, count):
            total = total + added[k][:, j * TILE : (j + 1) * TILE]
        out.append(total)
    return jnp.concatenate(out, axis=1)


def final_kernel(step_size, chunk, owner_ref, tiles_ref, me_ref, packed_ref, gram_ref, slab_ref, res_ref, coef_ref, base_ref, *refs):
    factors, refs = refs[: 2 * (BLOCK // TILE)], refs[2 * (BLOCK // TILE) :]
    res_out, coef_out, upd_ref, wide_ref, part_ref, ahead_ref, res_buf, tile_buf, res_sems, tile_sems = refs
    rows, targets = res_ref.shape
    own = targets // packed_ref.shape[0]
    exact = STEPS * own
    count = BLOCK // TILE

    def gradient(s):
        high = packed_ref[:, s * own : (s + 1) * own].astype(jnp.float32)
        low = packed_ref[:, exact + s * own : exact + (s + 1) * own].astype(jnp.float32)
        return (high + low).reshape(targets, BLOCK)

    dot = functools.partial(jnp.dot, preferred_element_type=jnp.float32)
    first = apply_inverse(gradient(0), factors[:count]) * step_size
    high = first.astype(jnp.bfloat16)
    low = (first - high.astype(jnp.float32)).astype(jnp.bfloat16)
    for i in range(rows // chunk):
        at = slice(i * chunk, (i + 1) * chunk)
        part_ref[:, at] = dot(high, slab_ref[:BLOCK, at])
    cross = packed_ref[:, 2 * exact :].reshape(BLOCK, BLOCK)
    block_part = dot(high, gram_ref[...]) + dot(low, gram_ref[...])
    again = gradient(1) - dot(high, cross) - RIDGE * block_part
    second = apply_inverse(again, factors[count:]) * step_size
    wide_ref[:, :BLOCK] = first
    wide_ref[:, BLOCK:] = second
    upd_ref[...] = second.astype(jnp.bfloat16)

    def change_of(s, k):
        at = s * BLOCK + k * TILE
        return jnp.transpose(wide_ref[:, at : at + TILE])

    def tile_rows(s, k):
        return pl.ds(pl.multiple_of(tiles_ref[s, k] * TILE, TILE), TILE)

    def tile_copy(s, k):
        return pltpu.make_async_copy(tile_buf.at[s, k], coef_out.at[tile_rows(s, k), :], tile_sems.at[s, k])

    owned = [owner_ref[s] == me_ref[0] for s in range(STEPS)]

    def writes(s, k):
        kept = owned[s]
        for later in range(s + 1, STEPS):
            for j in range(count):
                kept = kept & jnp.logical_not(owned[later] & (tiles_ref[later, j] == tiles_ref[s, k]))
        return kept

    for s in range(STEPS):
        for k in range(count):

            @pl.when(writes(s, k))
            def _():
                tile_buf[s, k] = coef_ref[tile_rows(s, k), :] + change_of(s, k)
                for earlier in range(s):
                    for j in range(count):

                        @pl.when(owned[earlier] & (tiles_ref[earlier, j] == tiles_ref[s, k]))
                        def _():
                            tile_buf[s, k] += change_of(earlier, j)

                tile_copy(s, k).start()

    chunks = rows // chunk
    rows_of = lambda i: pl.ds(pl.multiple_of(i * chunk, chunk), chunk)

    def res_copy(i):
        return pltpu.make_async_copy(res_buf.at[rows_of(i), :], res_out.at[rows_of(i), :], res_sems.at[i])

    def product(i):
        change = jnp.dot(upd_ref[...], slab_ref[BLOCK:, rows_of(i)], preferred_element_type=jnp.float32)
        return part_ref[:, rows_of(i)] + change

    ahead_ref[...] = product(0)

    def body(i, _):
        change = ahead_ref[...]
        ahead = product(jnp.minimum(i + 1, chunks - 1))
        res_buf[rows_of(i), :] = res_ref[rows_of(i), :] - jnp.transpose(change)
        ahead_ref[...] = ahead
        res_copy(i).start()
        return 0

    lax.fori_loop(0, chunks, body, 0)
    for i in range(rows // chunk):
        res_copy(i).wait()
    for s in range(STEPS):
        for k in range(count):

            @pl.when(writes(s, k))
            def _():
                tile_copy(s, k).wait()


def finish(owner, tiles, me, packed, gram12, slab, residual, coefficients, base, factors, step_size, chunk=512):
    rows, targets = residual.shape
    both = STEPS * BLOCK
    count = BLOCK // TILE
    smem, vmem, hbm = (pl.BlockSpec(memory_space=space) for space in (pltpu.SMEM, pltpu.VMEM, pltpu.HBM))
    return pl.pallas_call(
        functools.partial(final_kernel, step_size, chunk),
        in_specs=[smem] * 3 + [vmem] * 5 + [hbm] + [vmem] * len(factors),
        out_specs=(hbm, hbm),
        out_shape=(
            pltpu.HBM(residual.shape, jnp.float32),
            pltpu.HBM(residual.shape, jnp.float32),
        ),
        scratch_shapes=[
            pltpu.VMEM((targets, BLOCK), jnp.bfloat16),
            pltpu.VMEM((targets, both), jnp.float32),
            pltpu.VMEM((targets, rows), jnp.float32),
            pltpu.VMEM((targets, chunk), jnp.float32),
            pltpu.VMEM((rows, targets), jnp.float32),
            pltpu.VMEM((STEPS, count, TILE, targets), jnp.float32),
            pltpu.SemaphoreType.DMA((rows // chunk,)),
            pltpu.SemaphoreType.DMA((STEPS, count)),
        ],
        input_output_aliases={8: 1},
        compiler_params=pltpu.CompilerParams(vmem_limit_bytes=VMEM_LIMIT),
        cost_estimate=pl.CostEstimate(
            flops=2 * rows * both * targets, bytes_accessed=rows * (both * 2 + targets * 16), transcendentals=0
        ),
        name="finish",
    )(owner, tiles, me, packed, gram12, in_vmem(slab), in_vmem(residual), in_vmem(coefficients), base, *factors)


def local(features, residual, coefficients, block_owner, block_tiles):
    rows_dev, width = features.shape
    targets = residual.shape[1]
    sub_count = lax.axis_size("sub")
    devices = lax.axis_size("rows") * sub_count
    me = lax.axis_index(AXES).astype(jnp.int32)
    scale = 1.0 / width
    step_size = 1.0 / math.sqrt(rows_dev * devices)
    spread = Spread(AXES, sub_count) if devices <= 32 else Spread(("rows",), 1)
    groups = spread.count
    own = targets // groups

    wide = features.astype(jnp.float32)
    norms = (jnp.sum(wide * wide, axis=1) * scale).reshape(1, rows_dev)
    block, norms = fetch_blocks(features, norms, block_owner, block_tiles, me, devices, sub_count)
    slab, pieces = slabs(block, features, norms, residual, coefficients, scale, groups)
    exact = STEPS * own
    if spread.axes != AXES:
        pieces = pack(lax.psum(unpack(pieces, exact), "sub"), exact)
    core, on_core = bit_of(me, sub_count), (me & sub_count) != 0
    rest = gram(block, core.reshape(1), scale, slab)
    factors, before, extra = ([], []), None, []

    def beside(hop, indices):
        nonlocal before, rest
        then, got = hop
        for index in indices:
            args = {0: {"copied": coefficients}, 1: {"block": block, "scale": scale}}.get(index, {})
            mine, *given = factor_step(rest, index, slab, before, **args)
            if args:
                extra.append(given.pop())
            if index == indices[-1]:
                got, mine, given = lax.optimization_barrier((got, mine, given))
            before, rest = mine, given[0] if given else rest
            other = swap(mine, AXES, sub_count)
            factors[0].append(jnp.where(on_core, other, mine))
            factors[1].append(jnp.where(on_core, mine, other))
        return then(got)

    value = spread.core_sum(pieces, exact)
    value = beside(spread.near_sum(value, exact), [0])
    value = beside(spread.far_sum(value, exact), [1, 2])
    packed = beside(spread.near_gather(pack(value, exact)), [3])
    base, gram12 = extra
    packed = spread.core_gather(packed)
    return finish(
        block_owner, block_tiles, me.reshape(1), packed, gram12, slab, residual, coefficients, base,
        factors[0] + factors[1], step_size,
    )


def solution(mesh):
    row_spec = P(AXES, None)
    return jax.shard_map(
        local,
        mesh=mesh,
        in_specs=(row_spec, row_spec, row_spec, P(), P()),
        out_specs=(row_spec, row_spec),
        check_vma=False,
    )
```

```python
import functools
import math

import jax
import jax.numpy as jnp
from jax import lax
from jax.experimental import pallas as pl
from jax.experimental.pallas import tpu as pltpu
from jax.sharding import PartitionSpec as P

BLOCK = 512
TILE = 128
STEPS = 2
RIDGE = 0.5
AXES = ("rows", "sub")
HIGH = lax.Precision.HIGHEST
NT = (((1,), (1,)), ((), ()))
LOG2E = math.log2(math.e)
VMEM_LIMIT = 16 * 1024 * 1024
SMALL_LIMIT = 12 * 1024 * 1024


def pick_kernel(tiles_ref, core_ref, feat_ref, keep_ref, send_ref, sems):
    per_half = keep_ref.shape[1] // TILE
    copies = []
    for turn, out in enumerate((keep_ref, send_ref)):
        half = core_ref[0] if turn == 0 else 1 - core_ref[0]
        for s in range(STEPS):
            for i in range(per_half):
                source = pl.multiple_of(tiles_ref[s, half * per_half + i] * TILE, TILE)
                copies.append(
                    pltpu.make_async_copy(
                        feat_ref.at[pl.ds(source, TILE), :],
                        out.at[s, pl.ds(i * TILE, TILE), :],
                        sems.at[turn, s, i],
                    )
                )
    for copy in copies:
        copy.start()
    for copy in copies:
        copy.wait()


def pick_halves(features, block_tiles, core):
    width = features.shape[1]
    half = jax.ShapeDtypeStruct((STEPS, BLOCK // 2, width), features.dtype)
    return pl.pallas_call(
        pick_kernel,
        grid_spec=pltpu.PrefetchScalarGridSpec(
            num_scalar_prefetch=2,
            grid=(1,),
            in_specs=[pl.BlockSpec(memory_space=pltpu.HBM)],
            out_specs=[pl.BlockSpec(half.shape, lambda i, *_: (0, 0, 0))] * 2,
            scratch_shapes=[pltpu.SemaphoreType.DMA((2, STEPS, BLOCK // 2 // TILE))],
        ),
        out_shape=(half, half),
        compiler_params=pltpu.CompilerParams(vmem_limit_bytes=SMALL_LIMIT),
        name="pick",
    )(pltpu.with_memory_space_constraint(block_tiles, pltpu.HBM), core, pltpu.with_memory_space_constraint(features, pltpu.HBM))


def swap(value, axes, flip):
    flip_of = flip if callable(flip) else lambda i: flip
    return lax.ppermute(value, axes, [(i, i ^ flip_of(i)) for i in range(lax.axis_size(axes))])


def bit_of(index, mask):
    return ((index & mask) != 0).astype(jnp.int32)


def swap_among(pick, me, axes, low, high):
    place = bit_of(me, low) + 2 * bit_of(me, high)
    flips = [0, low, high, low | high]
    return place, [swap(pick(place ^ c), axes, flips[c]) for c in (1, 2, 3)]


def ordered(parts, me, low, high, axis):
    one, two = (me & low) != 0, (me & high) != 0
    parts = [jnp.where(one, parts[c ^ 1], parts[c]) for c in range(4)]
    return jnp.stack([jnp.where(two, parts[c ^ 2], parts[c]) for c in range(4)], axis=axis)


def fetch_blocks(features, prepared, block_owner, block_tiles, me, devices, core):
    width = features.shape[1]
    low, high = 1, 2 * core
    differs = lambda mask: (((block_owner ^ me) & mask) != 0)[:, None, None]
    on_core = (me & core) != 0
    keep, send = pick_halves(features, block_tiles, bit_of(me, core).reshape(1))
    half = jnp.where(differs(core), swap(send, AXES, core), keep)
    quarters = half.reshape(STEPS, 4, BLOCK // 8, width)
    pick = lambda place: lax.dynamic_index_in_dim(quarters, place, 1, False)
    place, got = swap_among(pick, me, AXES, low, high)
    part = jnp.where(
        differs(high),
        jnp.where(differs(low), got[2], got[1]),
        jnp.where(differs(low), got[0], pick(place)),
    )
    far = [1 << b for b in range(devices.bit_length() - 1) if 1 << b not in (core, low, high)]
    hops = []
    for one, two in zip(far[::2], far[1::2]):
        for first, second in ((one, two), (two, one)):
            flip = lambda i, first=first, second=second: second if i & core else first
            hops.append((flip, jnp.where(on_core, second, first)))
    if len(far) % 2:
        hops.append((far[-1], far[-1]))
    for hop, (flip, mask) in enumerate(hops):
        other = swap(part, AXES, flip)
        if hop == len(hops) - 2:
            other, prepared = lax.optimization_barrier((other, prepared))
        part = jnp.where(differs(mask), other, part)
    _, got = swap_among(lambda place: part, me, AXES, low, high)
    half = ordered([part] + got, me, low, high, 1)
    half = half.reshape(BLOCK, width)
    return half, swap(half, AXES, core), prepared


def both_halves(half, other, on_core):
    half, other = (value.reshape(STEPS, BLOCK // 2, value.shape[1]) for value in (half, other))
    both = jnp.stack([jnp.where(on_core, other, half), jnp.where(on_core, half, other)], axis=1)
    return both.reshape(STEPS * BLOCK, half.shape[2])


def pack(value, exact):
    high = lax.reduce_precision(value[..., :exact, :], 8, 7)
    low = value[..., :exact, :] - high
    return jnp.concatenate([part.astype(jnp.bfloat16) for part in (high, low, value[..., exact:, :])], axis=-2)


def unpack(value, exact):
    value = value.astype(jnp.float32)
    return jnp.concatenate([value[..., :exact, :] + value[..., exact : 2 * exact, :], value[..., 2 * exact :, :]], axis=-2)


class Spread:
    def __init__(self, axes, core):
        self.axes, self.core = axes, core
        self.me = lax.axis_index(axes).astype(jnp.int32)
        self.near = [1 << b for b in range(3) if 1 << b != core]
        self.far = [1 << b for b in range(3, lax.axis_size(axes).bit_length() - 1)]
        self.count = 8
        self.core_axis = 2 - (core.bit_length() - 1)

    def core_sum(self, packed, exact):
        packed = packed.reshape((2,) * 3 + packed.shape[1:])
        zero, one = (lax.index_in_dim(packed, i, self.core_axis, False) for i in (0, 1))
        bit = (self.me & self.core) != 0
        got = swap(jnp.where(bit, zero, one), self.axes, self.core)
        value = unpack(jnp.where(bit, one, zero), exact) + unpack(got, exact)
        return value.reshape((4,) + value.shape[2:])

    def near_sum(self, value, exact):
        packed = pack(value, exact)
        pick = lambda array, place: lax.dynamic_index_in_dim(array, place, 0, False)
        place, got = swap_among(lambda place: pick(packed, place), self.me, self.axes, *self.near)
        return lambda got: pick(value, place) + unpack(got[0], exact) + unpack(got[1], exact) + unpack(got[2], exact), got

    def far_sum(self, value, exact):
        packed = pack(value, exact)
        _, got = swap_among(lambda place: packed, self.me, self.axes, *self.far)
        return lambda got: value + unpack(got[0], exact) + unpack(got[1], exact) + unpack(got[2], exact), got

    def near_gather(self, value):
        _, got = swap_among(lambda place: value, self.me, self.axes, *self.near)
        return lambda got: ordered([value] + got, self.me, *self.near, 0), got

    def core_gather(self, value):
        rest = value.shape[1:]
        value = value.reshape((2, 2) + rest)
        bit = (self.me & self.core) != 0
        got = swap(value, self.axes, self.core)
        value = jnp.stack([jnp.where(bit, got, value), jnp.where(bit, value, got)], axis=self.core_axis)
        return value.reshape((self.count,) + rest)


def scaled_norm(rows, scale):
    wide = rows.astype(jnp.float32)
    return jnp.sum(wide * wide, axis=1, keepdims=True) * scale


def kernel_of(left, right, scale):
    dots = lax.dot_general(left, right, NT, preferred_element_type=jnp.float32)
    row = jnp.transpose(jnp.broadcast_to(scaled_norm(right, scale), (BLOCK, 128)))[:1]
    return jnp.exp(dots * (2.0 * scale) - scaled_norm(left, scale) - row)


def gram_kernel(scale, core_ref, block_ref, slab0_ref, slab1_ref, own_ref):
    mine = block_ref[pl.ds(pl.multiple_of(core_ref[0] * BLOCK, BLOCK), BLOCK), :]
    diagonal = lax.broadcasted_iota(jnp.int32, (BLOCK, BLOCK), 0) == lax.broadcasted_iota(jnp.int32, (BLOCK, BLOCK), 1)
    own_ref[...] = kernel_of(mine, mine, scale) + jnp.where(diagonal, RIDGE, 0.0)


def gram(block, core, scale, slab):
    vmem = pl.BlockSpec(memory_space=pltpu.VMEM)
    return pl.pallas_call(
        functools.partial(gram_kernel, scale),
        in_specs=[pl.BlockSpec(memory_space=pltpu.SMEM)] + [vmem] * 3,
        out_shape=jax.ShapeDtypeStruct((BLOCK, BLOCK), jnp.float32),
        compiler_params=pltpu.CompilerParams(vmem_limit_bytes=SMALL_LIMIT),
        cost_estimate=pl.CostEstimate(
            flops=2 * BLOCK**3, bytes_accessed=4 * BLOCK * BLOCK * 2, transcendentals=BLOCK**2
        ),
        name="gram",
    )(core, block, *map(in_vmem, slab))


def slab_kernel(scale, chunk, *refs):
    refs = list(refs)
    ahead_ref, bnorm, grad = refs[-3], refs[-2], refs[-1]
    second = len(refs) > 10
    half_ref, feat_ref, norm_ref, res_ref, coef_ref = refs[:5]
    if second:
        core_ref, first_slab, first_grad, slab_ref, piece_ref, grads, cross = refs[5:12]
        cross[...] = jnp.zeros_like(cross)
    else:
        slab_ref = refs[5]
    scale2 = scale * LOG2E
    part = BLOCK // 2
    bnorm[...] = jnp.broadcast_to(scaled_norm(half_ref[...], scale2), bnorm.shape)
    grad[...] = jnp.zeros_like(grad)
    chunks = feat_ref.shape[0] // chunk
    rows_of = lambda i: pl.ds(pl.multiple_of(i * chunk, chunk), chunk)
    at_of = lambda p: slice(p * part, (p + 1) * part)

    def product(i, p):
        return lax.dot_general(half_ref[at_of(p)], feat_ref[rows_of(i), :], NT, preferred_element_type=jnp.float32)

    ahead_ref[...] = product(0, 0)

    def body(i, _):
        rows = rows_of(i)
        weighted = (res_ref[rows, :] - RIDGE * coef_ref[rows, :]).astype(jnp.bfloat16)
        norm_row = norm_ref[:, rows] * LOG2E
        dots = ahead_ref[...]
        for p in range(STEPS):
            ahead = product(i, p + 1) if p + 1 < STEPS else product(jnp.minimum(i + 1, chunks - 1), 0)
            norm_wide = jnp.concatenate([bnorm[at_of(p)]] * (chunk // bnorm.shape[1]), axis=1)
            slab = jnp.exp2(dots * (2.0 * scale2) - norm_wide - norm_row).astype(jnp.bfloat16)
            slab_ref[at_of(p), rows] = slab
            if p == 0:
                grad[...] += jnp.dot(slab, weighted, preferred_element_type=jnp.float32)
            dots = ahead
        ahead_ref[...] = dots
        if second:
            left = [first_slab[at_of(0), rows], slab_ref[at_of(0), rows], jnp.transpose(weighted)]
            right = [first_slab[at_of(1), rows], slab_ref[at_of(1), rows]]
            cross[...] += lax.dot_general(
                jnp.concatenate(left, axis=0), jnp.concatenate(right, axis=0), NT, preferred_element_type=jnp.float32
            )
        return 0

    lax.fori_loop(0, chunks, body, 0, unroll=2)
    if not second:
        refs[6][...] = grad[...]
        return
    grads[:, at_of(0)] = jnp.transpose(first_grad[...])
    grads[:, at_of(1)] = jnp.transpose(grad[...])
    grads[:, BLOCK:] = cross[BLOCK:]
    groups = piece_ref.shape[0]
    own, depth = grads.shape[0] // groups, BLOCK // groups
    exact = STEPS * own
    place = lambda h: ((1 - core_ref[0]) if h else core_ref[0]) * part
    lanes = lambda base, h: pl.ds(pl.multiple_of(base + place(h), part), part)
    for h in range(2):
        to = at_of(h)
        for s in range(STEPS):
            value = grads[:, lanes(s * BLOCK, h)]
            high = value.astype(jnp.bfloat16)
            low = (value - high.astype(jnp.float32)).astype(jnp.bfloat16)
            for d in range(groups):
                here = slice(d * own, (d + 1) * own)
                piece_ref[d, s * own : (s + 1) * own, to] = high[here]
                piece_ref[d, exact + s * own : exact + (s + 1) * own, to] = low[here]
        for d in range(groups):
            row = place(d * depth // part) + d * depth % part
            value = cross[pl.ds(pl.multiple_of(row, depth), depth), lanes(0, h)]
            piece_ref[d, 2 * exact :, to] = value.astype(jnp.bfloat16)


def in_vmem(value):
    return pltpu.with_memory_space_constraint(value, pltpu.VMEM)


def slabs(half, features, norms, residual, coefficients, scale, groups=0, core=None, first=(), chunk=512):
    rows, width = features.shape
    targets = residual.shape[1]
    vmem = pl.BlockSpec(memory_space=pltpu.VMEM)
    slab = pltpu.VMEM((BLOCK, rows), jnp.bfloat16)
    inputs = [half, in_vmem(features), norms, in_vmem(residual), in_vmem(coefficients)]
    in_specs = [vmem] * 5
    scratch = [
        pltpu.VMEM((BLOCK // 2, chunk), jnp.float32),
        pltpu.VMEM((BLOCK, 128), jnp.float32),
        pltpu.VMEM((BLOCK // 2, targets), jnp.float32),
    ]
    out = jax.ShapeDtypeStruct((BLOCK // 2, targets), jnp.float32)
    if first:
        piece = (groups, 2 * STEPS * targets // groups + BLOCK // groups, BLOCK)
        out = jax.ShapeDtypeStruct(piece, jnp.bfloat16)
        inputs += [core, in_vmem(first[0]), first[1]]
        in_specs += [pl.BlockSpec(memory_space=pltpu.SMEM), vmem, vmem]
        scratch = [
            pltpu.VMEM((targets, STEPS * BLOCK), jnp.float32),
            pltpu.VMEM((BLOCK + targets, BLOCK), jnp.float32),
        ] + scratch
    return pl.pallas_call(
        functools.partial(slab_kernel, scale, chunk),
        in_specs=in_specs,
        out_shape=(slab, out),
        scratch_shapes=scratch,
        compiler_params=pltpu.CompilerParams(vmem_limit_bytes=VMEM_LIMIT),
        cost_estimate=pl.CostEstimate(
            flops=2 * rows * BLOCK * (width + targets + (BLOCK if first else 0)),
            bytes_accessed=rows * (width * 2 + targets * 8 + BLOCK * 2),
            transcendentals=rows * BLOCK,
        ),
        name="slabs",
    )(*inputs)


def eliminate(tiles, t, lane, scaled_ref, waiting):
    start, shape = 8 * t, tiles[t].shape
    wide = lambda tile, k: jnp.broadcast_to(tile[:, start + k : start + k + 1], shape)
    rows = [jnp.broadcast_to(tiles[t][k : k + 1], shape) for k in range(8)]
    at = {(i, k): wide(rows[i], k) for i in range(8) for k in range(i, 8)}
    units = [jnp.where(lane == start + k, 1.0, 0.0) for k in range(8)]
    rows = [row + unit for row, unit in zip(rows, units)]
    total, lower = [None] * 8, {}
    waiting, share = list(waiting), -(-len(waiting) // 4)
    for r in range(0, 8, 2):
        p, m, q = at[r, r], at[r, r + 1], at[r + 1, r + 1]
        det = p * q - m * m
        guess = pl.reciprocal(det, approx=True)
        for _ in range(min(share, len(waiting))):
            waiting.pop(0)()
        refine = 2.0 - det * guess
        inverse = guess * refine
        for k in range(r + 2, 8):
            first = q * at[r, k] - m * at[r + 1, k]
            second = p * at[r + 1, k] - m * at[r, k]
            lower[r, k], lower[r + 1, k] = first * inverse, second * inverse
            for i in range(r + 2, k + 1):
                product = at[r, i] * first + at[r + 1, i] * second
                change = product * guess * refine if k < r + 4 else product * inverse
                at[i, k] = at[i, k] - change
            rows[k] = rows[k] - (first * rows[r] + second * rows[r + 1]) * inverse
        total[r] = (q * rows[r] - m * rows[r + 1]) * inverse
        total[r + 1] = (p * rows[r + 1] - m * rows[r]) * inverse
    for r in (4, 2, 0):
        for k in range(7, r + 1, -1):
            total[r] = total[r] - lower[r, k] * total[k]
            total[r + 1] = total[r + 1] - lower[r + 1, k] * total[k]
    for k in range(8):
        scaled_ref[start + k : start + k + 1] = total[k][:1] - units[k][:1]

    def update(u):
        parts = [wide(tiles[u], k) * total[k] for k in range(8)]
        while len(parts) > 1:
            parts = [x + y for x, y in zip(parts[::2], parts[1::2])]
        tiles[u] = tiles[u] - parts[0]

    if t + 1 < len(tiles):
        update(t + 1)
    return [functools.partial(update, u) for u in range(t + 2, len(tiles))]


def factor_kernel(index, copied, scale, *refs):
    refs = list(refs)
    rest_ref, _, _ = refs.pop(0), refs.pop(0), refs.pop(0)
    before_ref = refs.pop(0) if index else None
    scaled = refs.pop()
    if copied:
        sem = refs.pop()
        copy = pltpu.make_async_copy(refs.pop(0), refs.pop(), sem)
        copy.start()
    if index == 1:
        block_ref, cross_ref = refs.pop(0), refs.pop()
        cross_ref[...] = kernel_of(block_ref[:BLOCK], block_ref[BLOCK:], scale).astype(cross_ref.dtype)
    factor_ref = refs[0]
    here = slice(index * TILE, (index + 1) * TILE)
    dot = functools.partial(lax.dot_general, precision=HIGH, preferred_element_type=jnp.float32)
    plain = (((1,), (0,)), ((), ()))

    def updated(rows):
        if not index:
            return rest_ref[rows]
        then = slice((index - 1) * TILE, index * TILE)
        old = rest_ref[rows]
        inside = lax.broadcasted_iota(jnp.int32, old.shape, 1) // TILE == index - 1
        return jnp.where(inside, 0.0, old) - dot(rest_ref[rows, then], before_ref[TILE:], plain)

    first = TILE if index == 1 else 0
    factor_ref[:TILE] = updated(slice(first, first + TILE))
    row_ids = lax.broadcasted_iota(jnp.int32, (TILE, TILE), 0)
    col_ids = lax.broadcasted_iota(jnp.int32, (TILE, TILE), 1)
    lane = lax.broadcasted_iota(jnp.int32, (8, TILE), 1)
    tiles = [factor_ref[8 * t : 8 * t + 8, here] for t in range(TILE // 8)]
    if len(refs) > 1:
        refs[1][...] = updated(slice(first + TILE, rest_ref.shape[0]))
    waiting = []
    for t in range(TILE // 8):
        waiting = eliminate(tiles, t, lane, scaled, waiting)
    start = row_ids - row_ids % 8
    lower = jnp.where(col_ids < start, jnp.concatenate(tiles, axis=0), 0.0)
    lower = lower + jnp.where(col_ids == row_ids, 1.0, 0.0)
    right = jnp.where(col_ids < start + 8, scaled[...], 0.0)
    inv = dot(lower, right, (((0,), (0,)), ((), ())))
    panel = dot(inv, factor_ref[:TILE], plain)
    inside = lax.broadcasted_iota(jnp.int32, panel.shape, 1) // TILE == index
    factor_ref[TILE:] = jnp.where(inside, jnp.concatenate([inv] * (BLOCK // TILE), axis=1), panel)
    if copied:
        copy.wait()


def factor_step(rest, index, slab, before=None, copied=None, block=None, scale=None):
    left = BLOCK - (index + 1) * TILE
    vmem, hbm = pl.BlockSpec(memory_space=pltpu.VMEM), pl.BlockSpec(memory_space=pltpu.HBM)
    out = [jax.ShapeDtypeStruct((2 * TILE, BLOCK), jnp.float32)]
    inputs, scratch = [rest, *map(in_vmem, slab)], [pltpu.VMEM((TILE, TILE), jnp.float32)]
    if index:
        inputs.append(before)
        if left:
            out.append(jax.ShapeDtypeStruct((left, BLOCK), jnp.float32))
    if block is not None:
        inputs.append(block)
        out.append(jax.ShapeDtypeStruct((BLOCK, BLOCK), jnp.bfloat16))
    in_specs, out_specs = [vmem] * len(inputs), [vmem] * len(out)
    if copied is not None:
        inputs.append(in_vmem(copied))
        in_specs.append(vmem)
        out.append(pltpu.HBM(copied.shape, copied.dtype))
        out_specs.append(hbm)
        scratch.insert(0, pltpu.SemaphoreType.DMA)
    return pl.pallas_call(
        functools.partial(factor_kernel, index, copied is not None, scale),
        in_specs=in_specs,
        out_specs=tuple(out_specs),
        out_shape=tuple(out),
        scratch_shapes=scratch,
        compiler_params=pltpu.CompilerParams(vmem_limit_bytes=SMALL_LIMIT),
        cost_estimate=pl.CostEstimate(flops=6 * 10**9, bytes_accessed=4 * 1024 * 1024, transcendentals=0),
        name="factor",
    )(*inputs)


def apply_inverse(value, refs):
    upto = lambda k: slice(0, k * TILE)
    dot = functools.partial(lax.dot_general, precision=HIGH, preferred_element_type=jnp.float32)
    count = BLOCK // TILE
    middle = [dot(value[:, upto(k + 1)], refs[k][TILE:, upto(k + 1)], NT) for k in range(count)]
    added = {k: dot(middle[k], refs[k][:TILE, upto(k)], (((1,), (0,)), ((), ()))) for k in range(1, count)}
    out = []
    for j in range(count):
        total = middle[j]
        for k in range(j + 1, count):
            total = total + added[k][:, j * TILE : (j + 1) * TILE]
        out.append(total)
    return jnp.concatenate(out, axis=1)


def final_kernel(step_size, chunk, owner_ref, tiles_ref, me_ref, core_ref, packed_ref, gram_ref, slab0_ref, slab1_ref, res_ref, coef_ref, base_ref, *refs):
    factors, refs = refs[: 2 * (BLOCK // TILE)], refs[2 * (BLOCK // TILE) :]
    res_out, coef_out, upd_ref, wide_ref, part_ref, ahead_ref, res_buf, tile_buf, res_sems, tile_sems = refs
    rows, targets = res_ref.shape
    own = targets // packed_ref.shape[0]
    exact = STEPS * own
    count = BLOCK // TILE

    def gradient(s):
        high = packed_ref[:, s * own : (s + 1) * own].astype(jnp.float32)
        low = packed_ref[:, exact + s * own : exact + (s + 1) * own].astype(jnp.float32)
        return (high + low).reshape(targets, BLOCK)

    dot = functools.partial(jnp.dot, preferred_element_type=jnp.float32)
    first = apply_inverse(gradient(0), factors[:count]) * step_size
    high = first.astype(jnp.bfloat16)
    low = (first - high.astype(jnp.float32)).astype(jnp.bfloat16)
    half = BLOCK // 2
    upd_ref[...] = high
    mine, theirs = (pl.ds(pl.multiple_of(c * half, half), half) for c in (core_ref[0], 1 - core_ref[0]))
    mine_high, theirs_high = upd_ref[:, mine], upd_ref[:, theirs]
    for i in range(rows // chunk):
        at = slice(i * chunk, (i + 1) * chunk)
        part_ref[:, at] = dot(mine_high, slab0_ref[:half, at]) + dot(theirs_high, slab1_ref[:half, at])
    cross = packed_ref[:, 2 * exact :].reshape(BLOCK, BLOCK)
    block_part = dot(high, gram_ref[...]) + dot(low, gram_ref[...])
    again = gradient(1) - dot(high, cross) - RIDGE * block_part
    second = apply_inverse(again, factors[count:]) * step_size
    wide_ref[:, :BLOCK] = first
    wide_ref[:, BLOCK:] = second
    upd_ref[...] = second.astype(jnp.bfloat16)

    def change_of(s, k):
        at = s * BLOCK + k * TILE
        return jnp.transpose(wide_ref[:, at : at + TILE])

    def tile_rows(s, k):
        return pl.ds(pl.multiple_of(tiles_ref[s, k] * TILE, TILE), TILE)

    def tile_copy(s, k):
        return pltpu.make_async_copy(tile_buf.at[s, k], coef_out.at[tile_rows(s, k), :], tile_sems.at[s, k])

    owned = [owner_ref[s] == me_ref[0] for s in range(STEPS)]

    def writes(s, k):
        kept = owned[s]
        for later in range(s + 1, STEPS):
            for j in range(count):
                kept = kept & jnp.logical_not(owned[later] & (tiles_ref[later, j] == tiles_ref[s, k]))
        return kept

    for s in range(STEPS):
        for k in range(count):

            @pl.when(writes(s, k))
            def _():
                tile_buf[s, k] = coef_ref[tile_rows(s, k), :] + change_of(s, k)
                for earlier in range(s):
                    for j in range(count):

                        @pl.when(owned[earlier] & (tiles_ref[earlier, j] == tiles_ref[s, k]))
                        def _():
                            tile_buf[s, k] += change_of(earlier, j)

                tile_copy(s, k).start()

    chunks = rows // chunk
    rows_of = lambda i: pl.ds(pl.multiple_of(i * chunk, chunk), chunk)

    def res_copy(i):
        return pltpu.make_async_copy(res_buf.at[rows_of(i), :], res_out.at[rows_of(i), :], res_sems.at[i])

    def product(i):
        change = dot(upd_ref[:, mine], slab0_ref[half:, rows_of(i)])
        return part_ref[:, rows_of(i)] + change + dot(upd_ref[:, theirs], slab1_ref[half:, rows_of(i)])

    ahead_ref[...] = product(0)

    def body(i, _):
        change = ahead_ref[...]
        ahead = product(jnp.minimum(i + 1, chunks - 1))
        res_buf[rows_of(i), :] = res_ref[rows_of(i), :] - jnp.transpose(change)
        ahead_ref[...] = ahead
        res_copy(i).start()
        return 0

    lax.fori_loop(0, chunks, body, 0)
    for i in range(rows // chunk):
        res_copy(i).wait()
    for s in range(STEPS):
        for k in range(count):

            @pl.when(writes(s, k))
            def _():
                tile_copy(s, k).wait()


def finish(owner, tiles, me, core, packed, gram12, slab, residual, coefficients, base, factors, step_size, chunk=512):
    rows, targets = residual.shape
    both = STEPS * BLOCK
    count = BLOCK // TILE
    smem, vmem, hbm = (pl.BlockSpec(memory_space=space) for space in (pltpu.SMEM, pltpu.VMEM, pltpu.HBM))
    return pl.pallas_call(
        functools.partial(final_kernel, step_size, chunk),
        in_specs=[smem] * 4 + [vmem] * 6 + [hbm] + [vmem] * len(factors),
        out_specs=(hbm, hbm),
        out_shape=(
            pltpu.HBM(residual.shape, jnp.float32),
            pltpu.HBM(residual.shape, jnp.float32),
        ),
        scratch_shapes=[
            pltpu.VMEM((targets, BLOCK), jnp.bfloat16),
            pltpu.VMEM((targets, both), jnp.float32),
            pltpu.VMEM((targets, rows), jnp.float32),
            pltpu.VMEM((targets, chunk), jnp.float32),
            pltpu.VMEM((rows, targets), jnp.float32),
            pltpu.VMEM((STEPS, count, TILE, targets), jnp.float32),
            pltpu.SemaphoreType.DMA((rows // chunk,)),
            pltpu.SemaphoreType.DMA((STEPS, count)),
        ],
        input_output_aliases={10: 1},
        compiler_params=pltpu.CompilerParams(vmem_limit_bytes=VMEM_LIMIT),
        cost_estimate=pl.CostEstimate(
            flops=2 * rows * both * targets, bytes_accessed=rows * (both * 2 + targets * 16), transcendentals=0
        ),
        name="finish",
    )(owner, tiles, me, core, packed, gram12, *map(in_vmem, slab), in_vmem(residual), in_vmem(coefficients), base, *factors)


def local(features, residual, coefficients, block_owner, block_tiles):
    rows_dev, width = features.shape
    targets = residual.shape[1]
    sub_count = lax.axis_size("sub")
    devices = lax.axis_size("rows") * sub_count
    me = lax.axis_index(AXES).astype(jnp.int32)
    scale = 1.0 / width
    step_size = 1.0 / math.sqrt(rows_dev * devices)
    spread = Spread(AXES, sub_count) if devices <= 32 else Spread(("rows",), 1)
    groups = spread.count
    own = targets // groups

    wide = features.astype(jnp.float32)
    norms = (jnp.sum(wide * wide, axis=1) * scale).reshape(1, rows_dev)
    half, other, norms = fetch_blocks(features, norms, block_owner, block_tiles, me, devices, sub_count)
    core, on_core = bit_of(me, sub_count).reshape(1), (me & sub_count) != 0
    first = slabs(half, features, norms, residual, coefficients, scale)
    other, first = lax.optimization_barrier((other, first))
    last = slabs(other, features, norms, residual, coefficients, scale, groups, core, first)
    slab, pieces = (first[0], last[0]), last[1]
    block = both_halves(half, other, on_core)
    exact = STEPS * own
    if spread.axes != AXES:
        pieces = pack(lax.psum(unpack(pieces, exact), "sub"), exact)
    rest = gram(block, core, scale, slab)
    factors, before, extra = ([], []), None, []

    def beside(hop, indices):
        nonlocal before, rest
        then, got = hop
        for index in indices:
            args = {0: {"copied": coefficients}, 1: {"block": block, "scale": scale}}.get(index, {})
            mine, *given = factor_step(rest, index, slab, before, **args)
            if args:
                extra.append(given.pop())
            if index == indices[-1]:
                got, mine, given = lax.optimization_barrier((got, mine, given))
            before, rest = mine, given[0] if given else rest
            other = swap(mine, AXES, sub_count)
            factors[0].append(jnp.where(on_core, other, mine))
            factors[1].append(jnp.where(on_core, mine, other))
        return then(got)

    value = spread.core_sum(pieces, exact)
    value = beside(spread.near_sum(value, exact), [0])
    value = beside(spread.far_sum(value, exact), [1, 2])
    packed = beside(spread.near_gather(pack(value, exact)), [3])
    base, gram12 = extra
    packed = spread.core_gather(packed)
    return finish(
        block_owner, block_tiles, me.reshape(1), core, packed, gram12, slab, residual, coefficients, base,
        factors[0] + factors[1], step_size,
    )


def solution(mesh):
    row_spec = P(AXES, None)
    return jax.shard_map(
        local,
        mesh=mesh,
        in_specs=(row_spec, row_spec, row_spec, P(), P()),
        out_specs=(row_spec, row_spec),
        check_vma=False,
    )
```

```python
import functools
import math

import jax
import jax.numpy as jnp
import numpy as np
from jax import lax
from jax.experimental import pallas as pl
from jax.experimental.pallas import tpu as pltpu
from jax.sharding import PartitionSpec as P

BLOCK = 512
TILE = 128
STEPS = 2
RIDGE = 0.5
AXES = ("rows", "sub")
HIGH = lax.Precision.HIGHEST
NT = (((1,), (1,)), ((), ()))
LOG2E = math.log2(math.e)
VMEM_LIMIT = 16 * 1024 * 1024
SMALL_LIMIT = 12 * 1024 * 1024


def pick_kernel(tiles_ref, core_ref, feat_ref, keep_ref, send_ref, sems):
    per_half = keep_ref.shape[1] // TILE
    copies = []
    for turn, out in enumerate((keep_ref, send_ref)):
        half = core_ref[0] if turn == 0 else 1 - core_ref[0]
        for s in range(STEPS):
            for i in range(per_half):
                source = pl.multiple_of(tiles_ref[s, half * per_half + i] * TILE, TILE)
                copies.append(
                    pltpu.make_async_copy(
                        feat_ref.at[pl.ds(source, TILE), :],
                        out.at[s, pl.ds(i * TILE, TILE), :],
                        sems.at[turn, s, i],
                    )
                )
    for copy in copies:
        copy.start()
    for copy in copies:
        copy.wait()


def pick_halves(features, block_tiles, core):
    width = features.shape[1]
    half = jax.ShapeDtypeStruct((STEPS, BLOCK // 2, width), features.dtype)
    return pl.pallas_call(
        pick_kernel,
        grid_spec=pltpu.PrefetchScalarGridSpec(
            num_scalar_prefetch=2,
            grid=(1,),
            in_specs=[pl.BlockSpec(memory_space=pltpu.HBM)],
            out_specs=[pl.BlockSpec(half.shape, lambda i, *_: (0, 0, 0))] * 2,
            scratch_shapes=[pltpu.SemaphoreType.DMA((2, STEPS, BLOCK // 2 // TILE))],
        ),
        out_shape=(half, half),
        compiler_params=pltpu.CompilerParams(vmem_limit_bytes=SMALL_LIMIT),
        name="pick",
    )(pltpu.with_memory_space_constraint(block_tiles, pltpu.HBM), core, pltpu.with_memory_space_constraint(features, pltpu.HBM))


def swap(value, axes, flip):
    flip_of = flip if callable(flip) else lambda i: flip
    return lax.ppermute(value, axes, [(i, i ^ flip_of(i)) for i in range(lax.axis_size(axes))])


def bit_of(index, mask):
    return ((index & mask) != 0).astype(jnp.int32)


def swap_among(pick, me, axes, low, high):
    place = (bit_of(me, low) + 2 * bit_of(me, high)).astype(jnp.uint32)
    flips = [0, low, high, low | high]
    return place, [swap(pick(place ^ np.uint32(c)), axes, flips[c]) for c in (1, 2, 3)]


def ordered(parts, me, low, high, axis):
    one, two = (me & low) != 0, (me & high) != 0
    parts = [jnp.where(one, parts[c ^ 1], parts[c]) for c in range(4)]
    return jnp.stack([jnp.where(two, parts[c ^ 2], parts[c]) for c in range(4)], axis=axis)


def fetch_blocks(features, prepared, block_owner, block_tiles, me, devices, core):
    width = features.shape[1]
    low, high = 1, 2 * core
    differs = lambda mask: (((block_owner ^ me) & mask) != 0)[:, None, None]
    on_core = (me & core) != 0
    keep, send = pick_halves(features, block_tiles, bit_of(me, core).reshape(1))
    half = jnp.where(differs(core), swap(send, AXES, core), keep)
    quarters = half.reshape(STEPS, 4, BLOCK // 8, width)
    pick = lambda place: lax.dynamic_index_in_dim(quarters, place, 1, False)
    place, got = swap_among(pick, me, AXES, low, high)
    got, prepared = lax.optimization_barrier((got, prepared))
    part = jnp.where(
        differs(high),
        jnp.where(differs(low), got[2], got[1]),
        jnp.where(differs(low), got[0], pick(place)),
    )
    far = [1 << b for b in range(devices.bit_length() - 1) if 1 << b not in (core, low, high)]
    hops = []
    for one, two in zip(far[::2], far[1::2]):
        for first, second in ((one, two), (two, one)):
            flip = lambda i, first=first, second=second: second if i & core else first
            hops.append((flip, jnp.where(on_core, second, first)))
    if len(far) % 2:
        hops.append((far[-1], far[-1]))
    for flip, mask in hops:
        other = swap(part, AXES, flip)
        part = jnp.where(differs(mask), other, part)
    _, got = swap_among(lambda place: part, me, AXES, low, high)
    half = ordered([part] + got, me, low, high, 1)
    half = half.reshape(BLOCK, width)
    return half, swap(half, AXES, core), prepared


def both_halves(half, other, on_core):
    half, other = (value.reshape(STEPS, BLOCK // 2, value.shape[1]) for value in (half, other))
    both = jnp.stack([jnp.where(on_core, other, half), jnp.where(on_core, half, other)], axis=1)
    return both.reshape(STEPS * BLOCK, half.shape[2])


def pack(value, exact):
    high = lax.reduce_precision(value[..., :exact, :], 8, 7)
    low = value[..., :exact, :] - high
    return jnp.concatenate([part.astype(jnp.bfloat16) for part in (high, low, value[..., exact:, :])], axis=-2)


def unpack(value, exact):
    value = value.astype(jnp.float32)
    return jnp.concatenate([value[..., :exact, :] + value[..., exact : 2 * exact, :], value[..., 2 * exact :, :]], axis=-2)


class Spread:
    def __init__(self, axes, core):
        self.axes, self.core = axes, core
        self.me = lax.axis_index(axes).astype(jnp.int32)
        self.near = [1 << b for b in range(3) if 1 << b != core]
        self.far = [1 << b for b in range(3, lax.axis_size(axes).bit_length() - 1)]
        self.count = 8
        self.core_axis = 2 - (core.bit_length() - 1)

    def core_sum(self, packed, exact):
        packed = packed.reshape((2,) * 3 + packed.shape[1:])
        zero, one = (lax.index_in_dim(packed, i, self.core_axis, False) for i in (0, 1))
        bit = (self.me & self.core) != 0
        got = swap(jnp.where(bit, zero, one), self.axes, self.core)
        value = unpack(jnp.where(bit, one, zero), exact) + unpack(got, exact)
        return value.reshape((4,) + value.shape[2:])

    def near_sum(self, value, exact):
        packed = pack(value, exact)
        pick = lambda array, place: lax.dynamic_index_in_dim(array, place, 0, False)
        place, got = swap_among(lambda place: pick(packed, place), self.me, self.axes, *self.near)
        return lambda got: pick(value, place) + unpack(got[0], exact) + unpack(got[1], exact) + unpack(got[2], exact), got

    def far_sum(self, value, exact):
        packed = pack(value, exact)
        _, got = swap_among(lambda place: packed, self.me, self.axes, *self.far)
        return lambda got: value + unpack(got[0], exact) + unpack(got[1], exact) + unpack(got[2], exact), got

    def near_gather(self, value):
        _, got = swap_among(lambda place: value, self.me, self.axes, *self.near)
        return lambda got: ordered([value] + got, self.me, *self.near, 0), got

    def core_gather(self, value):
        rest = value.shape[1:]
        value = value.reshape((2, 2) + rest)
        bit = (self.me & self.core) != 0
        got = swap(value, self.axes, self.core)
        value = jnp.stack([jnp.where(bit, got, value), jnp.where(bit, value, got)], axis=self.core_axis)
        return value.reshape((self.count,) + rest)


def scaled_norm(rows, scale):
    wide = rows.astype(jnp.float32)
    return jnp.sum(wide * wide, axis=1, keepdims=True) * scale


def kernel_of(left, right, scale):
    dots = lax.dot_general(left, right, NT, preferred_element_type=jnp.float32)
    row = jnp.transpose(jnp.broadcast_to(scaled_norm(right, scale), (BLOCK, 128)))[:1]
    return jnp.exp(dots * (2.0 * scale) - scaled_norm(left, scale) - row)


def gram_kernel(scale, core_ref, block_ref, slab0_ref, slab1_ref, own_ref):
    mine = block_ref[pl.ds(pl.multiple_of(core_ref[0] * BLOCK, BLOCK), BLOCK), :]
    diagonal = lax.broadcasted_iota(jnp.int32, (BLOCK, BLOCK), 0) == lax.broadcasted_iota(jnp.int32, (BLOCK, BLOCK), 1)
    own_ref[...] = kernel_of(mine, mine, scale) + jnp.where(diagonal, RIDGE, 0.0)


def gram(block, core, scale, slab):
    vmem = pl.BlockSpec(memory_space=pltpu.VMEM)
    return pl.pallas_call(
        functools.partial(gram_kernel, scale),
        in_specs=[pl.BlockSpec(memory_space=pltpu.SMEM)] + [vmem] * 3,
        out_shape=jax.ShapeDtypeStruct((BLOCK, BLOCK), jnp.float32),
        compiler_params=pltpu.CompilerParams(vmem_limit_bytes=SMALL_LIMIT),
        cost_estimate=pl.CostEstimate(
            flops=2 * BLOCK**3, bytes_accessed=4 * BLOCK * BLOCK * 2, transcendentals=BLOCK**2
        ),
        name="gram",
    )(core, block, *map(in_vmem, slab))


def load_kernel(scale, chunk, feat_in, res_in, coef_in, norm_ref, feat_ref, res_ref, coef_ref, sems, more_sems):
    chunks = feat_in.shape[0] // chunk
    rows_of = lambda i: pl.ds(pl.multiple_of(i * chunk, chunk), chunk)

    def load(i):
        return pltpu.make_async_copy(feat_in.at[rows_of(i), :], feat_ref.at[rows_of(i), :], sems.at[i])

    others = [
        pltpu.make_async_copy(source, target, more_sems.at[i])
        for i, (source, target) in enumerate(((res_in, res_ref), (coef_in, coef_ref)))
    ]
    for i in range(chunks):
        load(i).start()
    for copy in others:
        copy.start()
    ones = jnp.ones((16, feat_in.shape[1]), jnp.bfloat16)

    def body(i, _):
        load(i).wait()
        wide = feat_ref[rows_of(i), :].astype(jnp.float32)
        square = wide * wide
        high = square.astype(jnp.bfloat16)
        low = (square - high.astype(jnp.float32)).astype(jnp.bfloat16)
        sums = [lax.dot_general(ones, part, NT, preferred_element_type=jnp.float32) for part in (high, low)]
        norm_ref[:, rows_of(i)] = (sums[0] + sums[1])[:1] * scale
        return 0

    lax.fori_loop(0, chunks, body, 0)
    for copy in others:
        copy.wait()


def load_all(features, residual, coefficients, scale, chunk=512):
    rows = features.shape[0]
    arrays = (features, residual, coefficients)
    vmem, hbm = pl.BlockSpec(memory_space=pltpu.VMEM), pl.BlockSpec(memory_space=pltpu.HBM)
    return pl.pallas_call(
        functools.partial(load_kernel, scale, chunk),
        in_specs=[hbm] * 3,
        out_specs=(vmem,) * 4,
        out_shape=(jax.ShapeDtypeStruct((1, rows), jnp.float32),)
        + tuple(pltpu.VMEM(value.shape, value.dtype) for value in arrays),
        scratch_shapes=[pltpu.SemaphoreType.DMA((rows // chunk,)), pltpu.SemaphoreType.DMA((2,))],
        compiler_params=pltpu.CompilerParams(vmem_limit_bytes=SMALL_LIMIT),
        cost_estimate=pl.CostEstimate(flops=3 * 10**9, bytes_accessed=8 * 1024 * 1024, transcendentals=0),
        name="load",
    )(*(pltpu.with_memory_space_constraint(value, pltpu.HBM) for value in arrays))


def slab_kernel(scale, chunk, *refs):
    refs = list(refs)
    ahead_ref, bnorm, grad = refs[-3], refs[-2], refs[-1]
    second = len(refs) > 10
    half_ref, feat_ref, norm_ref, res_ref, coef_ref = refs[:5]
    if second:
        core_ref, first_slab, first_grad, slab_ref, piece_ref, grads, cross = refs[5:12]
        cross[...] = jnp.zeros_like(cross)
    else:
        slab_ref = refs[5]
    scale2 = scale * LOG2E
    part = BLOCK // 2
    bnorm[...] = jnp.broadcast_to(scaled_norm(half_ref[...], scale2), bnorm.shape)
    grad[...] = jnp.zeros_like(grad)
    chunks = feat_ref.shape[0] // chunk
    rows_of = lambda i: pl.ds(pl.multiple_of(i * chunk, chunk), chunk)
    at_of = lambda p: slice(p * part, (p + 1) * part)

    def product(i, p):
        return lax.dot_general(half_ref[at_of(p)], feat_ref[rows_of(i), :], NT, preferred_element_type=jnp.float32)

    ahead_ref[...] = product(0, 0)

    def body(i, _):
        rows = rows_of(i)
        weighted = (res_ref[rows, :] - RIDGE * coef_ref[rows, :]).astype(jnp.bfloat16)
        norm_row = norm_ref[:, rows] * LOG2E
        dots = ahead_ref[...]
        for p in range(STEPS):
            ahead = product(i, p + 1) if p + 1 < STEPS else product(jnp.minimum(i + 1, chunks - 1), 0)
            norm_wide = jnp.concatenate([bnorm[at_of(p)]] * (chunk // bnorm.shape[1]), axis=1)
            slab = jnp.exp2(dots * (2.0 * scale2) - norm_wide - norm_row).astype(jnp.bfloat16)
            slab_ref[at_of(p), rows] = slab
            if p == 0:
                grad[...] += jnp.dot(slab, weighted, preferred_element_type=jnp.float32)
            dots = ahead
        ahead_ref[...] = dots
        if second:
            left = [first_slab[at_of(0), rows], slab_ref[at_of(0), rows], jnp.transpose(weighted)]
            right = [first_slab[at_of(1), rows], slab_ref[at_of(1), rows]]
            cross[...] += lax.dot_general(
                jnp.concatenate(left, axis=0), jnp.concatenate(right, axis=0), NT, preferred_element_type=jnp.float32
            )
        return 0

    lax.fori_loop(0, chunks, body, 0, unroll=2)
    if not second:
        refs[6][...] = grad[...]
        return
    grads[:, at_of(0)] = jnp.transpose(first_grad[...])
    grads[:, at_of(1)] = jnp.transpose(grad[...])
    grads[:, BLOCK:] = cross[BLOCK:]
    groups = piece_ref.shape[0]
    own, depth = grads.shape[0] // groups, BLOCK // groups
    exact = STEPS * own
    place = lambda h: ((1 - core_ref[0]) if h else core_ref[0]) * part
    lanes = lambda base, h: pl.ds(pl.multiple_of(base + place(h), part), part)
    for h in range(2):
        to = at_of(h)
        for s in range(STEPS):
            value = grads[:, lanes(s * BLOCK, h)]
            high = value.astype(jnp.bfloat16)
            low = (value - high.astype(jnp.float32)).astype(jnp.bfloat16)
            for d in range(groups):
                here = slice(d * own, (d + 1) * own)
                piece_ref[d, s * own : (s + 1) * own, to] = high[here]
                piece_ref[d, exact + s * own : exact + (s + 1) * own, to] = low[here]
        for d in range(groups):
            row = place(d * depth // part) + d * depth % part
            value = cross[pl.ds(pl.multiple_of(row, depth), depth), lanes(0, h)]
            piece_ref[d, 2 * exact :, to] = value.astype(jnp.bfloat16)


def in_vmem(value):
    return pltpu.with_memory_space_constraint(value, pltpu.VMEM)


def slabs(half, features, norms, residual, coefficients, scale, groups=0, core=None, first=(), chunk=512):
    rows, width = features.shape
    targets = residual.shape[1]
    vmem = pl.BlockSpec(memory_space=pltpu.VMEM)
    slab = pltpu.VMEM((BLOCK, rows), jnp.bfloat16)
    inputs = [half, in_vmem(features), norms, in_vmem(residual), in_vmem(coefficients)]
    in_specs = [vmem] * 5
    scratch = [
        pltpu.VMEM((BLOCK // 2, chunk), jnp.float32),
        pltpu.VMEM((BLOCK, 128), jnp.float32),
        pltpu.VMEM((BLOCK // 2, targets), jnp.float32),
    ]
    out = jax.ShapeDtypeStruct((BLOCK // 2, targets), jnp.float32)
    if first:
        piece = (groups, 2 * STEPS * targets // groups + BLOCK // groups, BLOCK)
        out = jax.ShapeDtypeStruct(piece, jnp.bfloat16)
        inputs += [core, in_vmem(first[0]), first[1]]
        in_specs += [pl.BlockSpec(memory_space=pltpu.SMEM), vmem, vmem]
        scratch = [
            pltpu.VMEM((targets, STEPS * BLOCK), jnp.float32),
            pltpu.VMEM((BLOCK + targets, BLOCK), jnp.float32),
        ] + scratch
    return pl.pallas_call(
        functools.partial(slab_kernel, scale, chunk),
        in_specs=in_specs,
        out_shape=(slab, out),
        scratch_shapes=scratch,
        compiler_params=pltpu.CompilerParams(vmem_limit_bytes=VMEM_LIMIT),
        cost_estimate=pl.CostEstimate(
            flops=2 * rows * BLOCK * (width + targets + (BLOCK if first else 0)),
            bytes_accessed=rows * (width * 2 + targets * 8 + BLOCK * 2),
            transcendentals=rows * BLOCK,
        ),
        name="slabs",
    )(*inputs)


def eliminate(tiles, t, lane, scaled_ref, waiting):
    start, shape = 8 * t, tiles[t].shape
    wide = lambda tile, k: jnp.broadcast_to(tile[:, start + k : start + k + 1], shape)
    rows = [jnp.broadcast_to(tiles[t][k : k + 1], shape) for k in range(8)]
    at = {(i, k): wide(rows[i], k) for i in range(8) for k in range(i, 8)}
    units = [jnp.where(lane == start + k, 1.0, 0.0) for k in range(8)]
    rows = [row + unit for row, unit in zip(rows, units)]
    total, lower = [None] * 8, {}
    waiting, share = list(waiting), -(-len(waiting) // 4)
    for r in range(0, 8, 2):
        p, m, q = at[r, r], at[r, r + 1], at[r + 1, r + 1]
        det = p * q - m * m
        guess = pl.reciprocal(det, approx=True)
        for _ in range(min(share, len(waiting))):
            waiting.pop(0)()
        refine = 2.0 - det * guess
        inverse = guess * refine
        for k in range(r + 2, 8):
            first = q * at[r, k] - m * at[r + 1, k]
            second = p * at[r + 1, k] - m * at[r, k]
            lower[r, k], lower[r + 1, k] = first * inverse, second * inverse
            for i in range(r + 2, k + 1):
                product = at[r, i] * first + at[r + 1, i] * second
                change = product * guess * refine if k < r + 4 else product * inverse
                at[i, k] = at[i, k] - change
            rows[k] = rows[k] - (first * rows[r] + second * rows[r + 1]) * inverse
        total[r] = (q * rows[r] - m * rows[r + 1]) * inverse
        total[r + 1] = (p * rows[r + 1] - m * rows[r]) * inverse
    for r in (4, 2, 0):
        for k in range(7, r + 1, -1):
            total[r] = total[r] - lower[r, k] * total[k]
            total[r + 1] = total[r + 1] - lower[r + 1, k] * total[k]
    for k in range(8):
        scaled_ref[start + k : start + k + 1] = total[k][:1] - units[k][:1]

    def update(u):
        parts = [wide(tiles[u], k) * total[k] for k in range(8)]
        while len(parts) > 1:
            parts = [x + y for x, y in zip(parts[::2], parts[1::2])]
        tiles[u] = tiles[u] - parts[0]

    if t + 1 < len(tiles):
        update(t + 1)
    return [functools.partial(update, u) for u in range(t + 2, len(tiles))]


def factor_kernel(index, copied, scale, *refs):
    refs = list(refs)
    rest_ref, _, _ = refs.pop(0), refs.pop(0), refs.pop(0)
    before_ref = refs.pop(0) if index else None
    scaled = refs.pop()
    if copied:
        sem = refs.pop()
        copy = pltpu.make_async_copy(refs.pop(0), refs.pop(), sem)
        copy.start()
    if index == 1:
        block_ref, cross_ref = refs.pop(0), refs.pop()
        cross_ref[...] = kernel_of(block_ref[:BLOCK], block_ref[BLOCK:], scale).astype(cross_ref.dtype)
    factor_ref = refs[0]
    here = slice(index * TILE, (index + 1) * TILE)
    dot = functools.partial(lax.dot_general, precision=HIGH, preferred_element_type=jnp.float32)
    plain = (((1,), (0,)), ((), ()))

    def updated(rows):
        if not index:
            return rest_ref[rows]
        then = slice((index - 1) * TILE, index * TILE)
        old = rest_ref[rows]
        inside = lax.broadcasted_iota(jnp.int32, old.shape, 1) // TILE == index - 1
        return jnp.where(inside, 0.0, old) - dot(rest_ref[rows, then], before_ref[TILE:], plain)

    first = TILE if index == 1 else 0
    factor_ref[:TILE] = updated(slice(first, first + TILE))
    row_ids = lax.broadcasted_iota(jnp.int32, (TILE, TILE), 0)
    col_ids = lax.broadcasted_iota(jnp.int32, (TILE, TILE), 1)
    lane = lax.broadcasted_iota(jnp.int32, (8, TILE), 1)
    tiles = [factor_ref[8 * t : 8 * t + 8, here] for t in range(TILE // 8)]
    if len(refs) > 1:
        refs[1][...] = updated(slice(first + TILE, rest_ref.shape[0]))
    waiting = []
    for t in range(TILE // 8):
        waiting = eliminate(tiles, t, lane, scaled, waiting)
    start = row_ids - row_ids % 8
    lower = jnp.where(col_ids < start, jnp.concatenate(tiles, axis=0), 0.0)
    lower = lower + jnp.where(col_ids == row_ids, 1.0, 0.0)
    right = jnp.where(col_ids < start + 8, scaled[...], 0.0)
    inv = dot(lower, right, (((0,), (0,)), ((), ())))
    panel = dot(inv, factor_ref[:TILE], plain)
    inside = lax.broadcasted_iota(jnp.int32, panel.shape, 1) // TILE == index
    factor_ref[TILE:] = jnp.where(inside, jnp.concatenate([inv] * (BLOCK // TILE), axis=1), panel)
    if copied:
        copy.wait()


def factor_step(rest, index, slab, before=None, copied=None, block=None, scale=None):
    left = BLOCK - (index + 1) * TILE
    vmem, hbm = pl.BlockSpec(memory_space=pltpu.VMEM), pl.BlockSpec(memory_space=pltpu.HBM)
    out = [jax.ShapeDtypeStruct((2 * TILE, BLOCK), jnp.float32)]
    inputs, scratch = [rest, *map(in_vmem, slab)], [pltpu.VMEM((TILE, TILE), jnp.float32)]
    if index:
        inputs.append(before)
        if left:
            out.append(jax.ShapeDtypeStruct((left, BLOCK), jnp.float32))
    if block is not None:
        inputs.append(block)
        out.append(jax.ShapeDtypeStruct((BLOCK, BLOCK), jnp.bfloat16))
    in_specs, out_specs = [vmem] * len(inputs), [vmem] * len(out)
    if copied is not None:
        inputs.append(in_vmem(copied))
        in_specs.append(vmem)
        out.append(pltpu.HBM(copied.shape, copied.dtype))
        out_specs.append(hbm)
        scratch.insert(0, pltpu.SemaphoreType.DMA)
    return pl.pallas_call(
        functools.partial(factor_kernel, index, copied is not None, scale),
        in_specs=in_specs,
        out_specs=tuple(out_specs),
        out_shape=tuple(out),
        scratch_shapes=scratch,
        compiler_params=pltpu.CompilerParams(vmem_limit_bytes=SMALL_LIMIT),
        cost_estimate=pl.CostEstimate(flops=6 * 10**9, bytes_accessed=4 * 1024 * 1024, transcendentals=0),
        name="factor",
    )(*inputs)


def apply_inverse(value, refs):
    upto = lambda k: slice(0, k * TILE)
    dot = functools.partial(lax.dot_general, precision=HIGH, preferred_element_type=jnp.float32)
    count = BLOCK // TILE
    middle = [dot(value[:, upto(k + 1)], refs[k][TILE:, upto(k + 1)], NT) for k in range(count)]
    added = {k: dot(middle[k], refs[k][:TILE, upto(k)], (((1,), (0,)), ((), ()))) for k in range(1, count)}
    out = []
    for j in range(count):
        total = middle[j]
        for k in range(j + 1, count):
            total = total + added[k][:, j * TILE : (j + 1) * TILE]
        out.append(total)
    return jnp.concatenate(out, axis=1)


def final_kernel(step_size, chunk, owner_ref, tiles_ref, me_ref, core_ref, packed_ref, gram_ref, slab0_ref, slab1_ref, res_ref, coef_ref, base_ref, *refs):
    factors, refs = refs[: 2 * (BLOCK // TILE)], refs[2 * (BLOCK // TILE) :]
    res_out, coef_out, upd_ref, wide_ref, part_ref, ahead_ref, res_buf, tile_buf, res_sems, tile_sems = refs
    rows, targets = res_ref.shape
    own = targets // packed_ref.shape[0]
    exact = STEPS * own
    count = BLOCK // TILE

    def gradient(s):
        high = packed_ref[:, s * own : (s + 1) * own].astype(jnp.float32)
        low = packed_ref[:, exact + s * own : exact + (s + 1) * own].astype(jnp.float32)
        return (high + low).reshape(targets, BLOCK)

    dot = functools.partial(jnp.dot, preferred_element_type=jnp.float32)
    first = apply_inverse(gradient(0), factors[:count]) * step_size
    high = first.astype(jnp.bfloat16)
    low = (first - high.astype(jnp.float32)).astype(jnp.bfloat16)
    half = BLOCK // 2
    upd_ref[...] = high
    mine, theirs = (pl.ds(pl.multiple_of(c * half, half), half) for c in (core_ref[0], 1 - core_ref[0]))
    mine_high, theirs_high = upd_ref[:, mine], upd_ref[:, theirs]
    for i in range(rows // chunk):
        at = slice(i * chunk, (i + 1) * chunk)
        part_ref[:, at] = dot(mine_high, slab0_ref[:half, at]) + dot(theirs_high, slab1_ref[:half, at])
    cross = packed_ref[:, 2 * exact :].reshape(BLOCK, BLOCK)
    block_part = dot(high, gram_ref[...]) + dot(low, gram_ref[...])
    again = gradient(1) - dot(high, cross) - RIDGE * block_part
    second = apply_inverse(again, factors[count:]) * step_size
    wide_ref[:, :BLOCK] = first
    wide_ref[:, BLOCK:] = second
    upd_ref[...] = second.astype(jnp.bfloat16)

    def change_of(s, k):
        at = s * BLOCK + k * TILE
        return jnp.transpose(wide_ref[:, at : at + TILE])

    def tile_rows(s, k):
        return pl.ds(pl.multiple_of(tiles_ref[s, k] * TILE, TILE), TILE)

    def tile_copy(s, k):
        return pltpu.make_async_copy(tile_buf.at[s, k], coef_out.at[tile_rows(s, k), :], tile_sems.at[s, k])

    owned = [owner_ref[s] == me_ref[0] for s in range(STEPS)]

    def writes(s, k):
        kept = owned[s]
        for later in range(s + 1, STEPS):
            for j in range(count):
                kept = kept & jnp.logical_not(owned[later] & (tiles_ref[later, j] == tiles_ref[s, k]))
        return kept

    for s in range(STEPS):
        for k in range(count):

            @pl.when(writes(s, k))
            def _():
                tile_buf[s, k] = coef_ref[tile_rows(s, k), :] + change_of(s, k)
                for earlier in range(s):
                    for j in range(count):

                        @pl.when(owned[earlier] & (tiles_ref[earlier, j] == tiles_ref[s, k]))
                        def _():
                            tile_buf[s, k] += change_of(earlier, j)

                tile_copy(s, k).start()

    chunks = rows // chunk
    rows_of = lambda i: pl.ds(pl.multiple_of(i * chunk, chunk), chunk)

    def res_copy(i):
        return pltpu.make_async_copy(res_buf.at[rows_of(i), :], res_out.at[rows_of(i), :], res_sems.at[i])

    def product(i):
        change = dot(upd_ref[:, mine], slab0_ref[half:, rows_of(i)])
        return part_ref[:, rows_of(i)] + change + dot(upd_ref[:, theirs], slab1_ref[half:, rows_of(i)])

    ahead_ref[...] = product(0)

    def body(i, _):
        change = ahead_ref[...]
        ahead = product(jnp.minimum(i + 1, chunks - 1))
        res_buf[rows_of(i), :] = res_ref[rows_of(i), :] - jnp.transpose(change)
        ahead_ref[...] = ahead
        res_copy(i).start()
        return 0

    lax.fori_loop(0, chunks, body, 0)
    for i in range(rows // chunk):
        res_copy(i).wait()
    for s in range(STEPS):
        for k in range(count):

            @pl.when(writes(s, k))
            def _():
                tile_copy(s, k).wait()


def finish(owner, tiles, me, core, packed, gram12, slab, residual, coefficients, base, factors, step_size, chunk=512):
    rows, targets = residual.shape
    both = STEPS * BLOCK
    count = BLOCK // TILE
    smem, vmem, hbm = (pl.BlockSpec(memory_space=space) for space in (pltpu.SMEM, pltpu.VMEM, pltpu.HBM))
    return pl.pallas_call(
        functools.partial(final_kernel, step_size, chunk),
        in_specs=[smem] * 4 + [vmem] * 6 + [hbm] + [vmem] * len(factors),
        out_specs=(hbm, hbm),
        out_shape=(
            pltpu.HBM(residual.shape, jnp.float32),
            pltpu.HBM(residual.shape, jnp.float32),
        ),
        scratch_shapes=[
            pltpu.VMEM((targets, BLOCK), jnp.bfloat16),
            pltpu.VMEM((targets, both), jnp.float32),
            pltpu.VMEM((targets, rows), jnp.float32),
            pltpu.VMEM((targets, chunk), jnp.float32),
            pltpu.VMEM((rows, targets), jnp.float32),
            pltpu.VMEM((STEPS, count, TILE, targets), jnp.float32),
            pltpu.SemaphoreType.DMA((rows // chunk,)),
            pltpu.SemaphoreType.DMA((STEPS, count)),
        ],
        input_output_aliases={10: 1},
        compiler_params=pltpu.CompilerParams(vmem_limit_bytes=VMEM_LIMIT),
        cost_estimate=pl.CostEstimate(
            flops=2 * rows * both * targets, bytes_accessed=rows * (both * 2 + targets * 16), transcendentals=0
        ),
        name="finish",
    )(owner, tiles, me, core, packed, gram12, *map(in_vmem, slab), in_vmem(residual), in_vmem(coefficients), base, *factors)


def local(features, residual, coefficients, block_owner, block_tiles):
    rows_dev, width = features.shape
    targets = residual.shape[1]
    sub_count = lax.axis_size("sub")
    devices = lax.axis_size("rows") * sub_count
    me = lax.axis_index(AXES).astype(jnp.int32)
    scale = 1.0 / width
    step_size = 1.0 / math.sqrt(rows_dev * devices)
    spread = Spread(AXES, sub_count) if devices <= 32 else Spread(("rows",), 1)
    groups = spread.count
    own = targets // groups

    loaded = load_all(features, residual, coefficients, scale)
    half, other, loaded = fetch_blocks(features, loaded, block_owner, block_tiles, me, devices, sub_count)
    norms, features, residual, coefficients = loaded
    core, on_core = bit_of(me, sub_count).reshape(1), (me & sub_count) != 0
    first = slabs(half, features, norms, residual, coefficients, scale)
    other, first = lax.optimization_barrier((other, first))
    last = slabs(other, features, norms, residual, coefficients, scale, groups, core, first)
    slab, pieces = (first[0], last[0]), last[1]
    block = both_halves(half, other, on_core)
    exact = STEPS * own
    if spread.axes != AXES:
        pieces = pack(lax.psum(unpack(pieces, exact), "sub"), exact)
    rest = gram(block, core, scale, slab)
    factors, before, extra = ([], []), None, []

    def beside(hop, indices):
        nonlocal before, rest
        then, got = hop
        for index in indices:
            args = {0: {"copied": coefficients}, 1: {"block": block, "scale": scale}}.get(index, {})
            mine, *given = factor_step(rest, index, slab, before, **args)
            if args:
                extra.append(given.pop())
            if index == indices[-1]:
                got, mine, given = lax.optimization_barrier((got, mine, given))
            before, rest = mine, given[0] if given else rest
            other = swap(mine, AXES, sub_count)
            factors[0].append(jnp.where(on_core, other, mine))
            factors[1].append(jnp.where(on_core, mine, other))
        return then(got)

    value = spread.core_sum(pieces, exact)
    value = beside(spread.near_sum(value, exact), [0])
    value = beside(spread.far_sum(value, exact), [1, 2])
    packed = beside(spread.near_gather(pack(value, exact)), [3])
    base, gram12 = extra
    packed = spread.core_gather(packed)
    return finish(
        block_owner, block_tiles, me.reshape(1), core, packed, gram12, slab, residual, coefficients, base,
        factors[0] + factors[1], step_size,
    )


def solution(mesh):
    row_spec = P(AXES, None)
    return jax.shard_map(
        local,
        mesh=mesh,
        in_specs=(row_spec, row_spec, row_spec, P(), P()),
        out_specs=(row_spec, row_spec),
        check_vma=False,
    )
```

```python
import functools
import math

import jax
import jax.numpy as jnp
import numpy as np
from jax import lax
from jax.experimental import pallas as pl
from jax.experimental.pallas import tpu as pltpu
from jax.sharding import PartitionSpec as P

BLOCK = 512
TILE = 128
STEPS = 2
RIDGE = 0.5
AXES = ("rows", "sub")
HIGH = lax.Precision.HIGHEST
NT = (((1,), (1,)), ((), ()))
LOG2E = math.log2(math.e)
VMEM_LIMIT = 16 * 1024 * 1024
SMALL_LIMIT = 12 * 1024 * 1024


def pick_kernel(tiles_ref, core_ref, feat_ref, keep_ref, send_ref, sems):
    per_half = keep_ref.shape[1] // TILE
    copies = []
    for turn, out in enumerate((keep_ref, send_ref)):
        half = core_ref[0] if turn == 0 else 1 - core_ref[0]
        for s in range(STEPS):
            for i in range(per_half):
                source = pl.multiple_of(tiles_ref[s, half * per_half + i] * TILE, TILE)
                copies.append(
                    pltpu.make_async_copy(
                        feat_ref.at[pl.ds(source, TILE), :],
                        out.at[s, pl.ds(i * TILE, TILE), :],
                        sems.at[turn, s, i],
                    )
                )
    for copy in copies:
        copy.start()
    for copy in copies:
        copy.wait()


def pick_halves(features, block_tiles, core):
    width = features.shape[1]
    half = jax.ShapeDtypeStruct((STEPS, BLOCK // 2, width), features.dtype)
    return pl.pallas_call(
        pick_kernel,
        grid_spec=pltpu.PrefetchScalarGridSpec(
            num_scalar_prefetch=2,
            grid=(1,),
            in_specs=[pl.BlockSpec(memory_space=pltpu.HBM)],
            out_specs=[pl.BlockSpec(half.shape, lambda i, *_: (0, 0, 0))] * 2,
            scratch_shapes=[pltpu.SemaphoreType.DMA((2, STEPS, BLOCK // 2 // TILE))],
        ),
        out_shape=(half, half),
        compiler_params=pltpu.CompilerParams(vmem_limit_bytes=SMALL_LIMIT),
        name="pick",
    )(pltpu.with_memory_space_constraint(block_tiles, pltpu.HBM), core, pltpu.with_memory_space_constraint(features, pltpu.HBM))


def swap(value, axes, flip):
    flip_of = flip if callable(flip) else lambda i: flip
    return lax.ppermute(value, axes, [(i, i ^ flip_of(i)) for i in range(lax.axis_size(axes))])


def bit_of(index, mask):
    return ((index & mask) != 0).astype(jnp.int32)


def swap_among(pick, me, axes, low, high):
    place = (bit_of(me, low) + 2 * bit_of(me, high)).astype(jnp.uint32)
    flips = [0, low, high, low | high]
    return place, [swap(pick(place ^ np.uint32(c)), axes, flips[c]) for c in (1, 2, 3)]


def ordered(parts, me, low, high, axis):
    one, two = (me & low) != 0, (me & high) != 0
    parts = [jnp.where(one, parts[c ^ 1], parts[c]) for c in range(4)]
    return jnp.stack([jnp.where(two, parts[c ^ 2], parts[c]) for c in range(4)], axis=axis)


def fetch_blocks(features, prepared, block_owner, block_tiles, me, devices, core):
    width = features.shape[1]
    low, high = 1, 2 * core
    differs = lambda mask: (((block_owner ^ me) & mask) != 0)[:, None, None]
    on_core = (me & core) != 0
    keep, send = pick_halves(features, block_tiles, bit_of(me, core).reshape(1))
    half = jnp.where(differs(core), swap(send, AXES, core), keep)
    quarters = half.reshape(STEPS, 4, BLOCK // 8, width)
    pick = lambda place: lax.dynamic_index_in_dim(quarters, place, 1, False)
    place, got = swap_among(pick, me, AXES, low, high)
    got, prepared = lax.optimization_barrier((got, prepared))
    part = jnp.where(
        differs(high),
        jnp.where(differs(low), got[2], got[1]),
        jnp.where(differs(low), got[0], pick(place)),
    )
    far = [1 << b for b in range(devices.bit_length() - 1) if 1 << b not in (core, low, high)]
    hops = []
    for one, two in zip(far[::2], far[1::2]):
        for first, second in ((one, two), (two, one)):
            flip = lambda i, first=first, second=second: second if i & core else first
            hops.append((flip, jnp.where(on_core, second, first)))
    if len(far) % 2:
        hops.append((far[-1], far[-1]))
    for flip, mask in hops:
        other = swap(part, AXES, flip)
        part = jnp.where(differs(mask), other, part)
    _, got = swap_among(lambda place: part, me, AXES, low, high)
    half = ordered([part] + got, me, low, high, 1)
    half = half.reshape(BLOCK, width)
    return half, swap(half, AXES, core), prepared


def both_halves(half, other, on_core):
    half, other = (value.reshape(STEPS, BLOCK // 2, value.shape[1]) for value in (half, other))
    both = jnp.stack([jnp.where(on_core, other, half), jnp.where(on_core, half, other)], axis=1)
    return both.reshape(STEPS * BLOCK, half.shape[2])


def pack(value, exact):
    high = lax.reduce_precision(value[..., :exact, :], 8, 7)
    low = value[..., :exact, :] - high
    return jnp.concatenate([part.astype(jnp.bfloat16) for part in (high, low, value[..., exact:, :])], axis=-2)


def unpack(value, exact):
    value = value.astype(jnp.float32)
    return jnp.concatenate([value[..., :exact, :] + value[..., exact : 2 * exact, :], value[..., 2 * exact :, :]], axis=-2)


class Spread:
    def __init__(self, axes, core):
        self.axes, self.core = axes, core
        self.me = lax.axis_index(axes).astype(jnp.int32)
        self.near = [1 << b for b in range(3) if 1 << b != core]
        self.far = [1 << b for b in range(3, lax.axis_size(axes).bit_length() - 1)]
        self.count = 8
        self.core_axis = 2 - (core.bit_length() - 1)

    def core_sum(self, packed, exact):
        packed = packed.reshape((2,) * 3 + packed.shape[1:])
        zero, one = (lax.index_in_dim(packed, i, self.core_axis, False) for i in (0, 1))
        bit = (self.me & self.core) != 0
        got = swap(jnp.where(bit, zero, one), self.axes, self.core)
        value = unpack(jnp.where(bit, one, zero), exact) + unpack(got, exact)
        return value.reshape((4,) + value.shape[2:])

    def near_sum(self, value, exact):
        packed = pack(value, exact)
        pick = lambda array, place: lax.dynamic_index_in_dim(array, place, 0, False)
        place, got = swap_among(lambda place: pick(packed, place), self.me, self.axes, *self.near)
        return lambda got: pick(value, place) + unpack(got[0], exact) + unpack(got[1], exact) + unpack(got[2], exact), got

    def far_sum(self, value, exact):
        packed = pack(value, exact)
        _, got = swap_among(lambda place: packed, self.me, self.axes, *self.far)
        return lambda got: value + unpack(got[0], exact) + unpack(got[1], exact) + unpack(got[2], exact), got

    def near_gather(self, value):
        _, got = swap_among(lambda place: value, self.me, self.axes, *self.near)
        return lambda got: ordered([value] + got, self.me, *self.near, 0), got

    def core_gather(self, value):
        rest = value.shape[1:]
        value = value.reshape((2, 2) + rest)
        bit = (self.me & self.core) != 0
        got = swap(value, self.axes, self.core)
        value = jnp.stack([jnp.where(bit, got, value), jnp.where(bit, value, got)], axis=self.core_axis)
        return value.reshape((self.count,) + rest)


def scaled_norm(rows, scale):
    wide = rows.astype(jnp.float32)
    return jnp.sum(wide * wide, axis=1, keepdims=True) * scale


def kernel_of(left, right, scale):
    dots = lax.dot_general(left, right, NT, preferred_element_type=jnp.float32)
    row = jnp.transpose(jnp.broadcast_to(scaled_norm(right, scale), (BLOCK, 128)))[:1]
    return jnp.exp(dots * (2.0 * scale) - scaled_norm(left, scale) - row)


def gram_kernel(scale, core_ref, block_ref, slab0_ref, slab1_ref, own_ref):
    mine = block_ref[pl.ds(pl.multiple_of(core_ref[0] * BLOCK, BLOCK), BLOCK), :]
    diagonal = lax.broadcasted_iota(jnp.int32, (BLOCK, BLOCK), 0) == lax.broadcasted_iota(jnp.int32, (BLOCK, BLOCK), 1)
    own_ref[...] = kernel_of(mine, mine, scale) + jnp.where(diagonal, RIDGE, 0.0)


def gram(block, core, scale, slab):
    vmem = pl.BlockSpec(memory_space=pltpu.VMEM)
    return pl.pallas_call(
        functools.partial(gram_kernel, scale),
        in_specs=[pl.BlockSpec(memory_space=pltpu.SMEM)] + [vmem] * 3,
        out_shape=jax.ShapeDtypeStruct((BLOCK, BLOCK), jnp.float32),
        compiler_params=pltpu.CompilerParams(vmem_limit_bytes=SMALL_LIMIT),
        cost_estimate=pl.CostEstimate(
            flops=2 * BLOCK**3, bytes_accessed=4 * BLOCK * BLOCK * 2, transcendentals=BLOCK**2
        ),
        name="gram",
    )(core, block, *map(in_vmem, slab))


def load_kernel(scale, chunk, feat_in, res_in, coef_in, norm_ref, feat_ref, res_ref, coef_ref, sems, more_sems):
    chunks = feat_in.shape[0] // chunk
    rows_of = lambda i: pl.ds(pl.multiple_of(i * chunk, chunk), chunk)

    def load(i):
        return pltpu.make_async_copy(feat_in.at[rows_of(i), :], feat_ref.at[rows_of(i), :], sems.at[i])

    others = [
        pltpu.make_async_copy(source, target, more_sems.at[i])
        for i, (source, target) in enumerate(((res_in, res_ref), (coef_in, coef_ref)))
    ]
    for i in range(chunks):
        load(i).start()
    for copy in others:
        copy.start()
    ones = jnp.ones((16, feat_in.shape[1]), jnp.bfloat16)

    def body(i, _):
        load(i).wait()
        wide = feat_ref[rows_of(i), :].astype(jnp.float32)
        square = wide * wide
        high = square.astype(jnp.bfloat16)
        low = (square - high.astype(jnp.float32)).astype(jnp.bfloat16)
        sums = [lax.dot_general(ones, part, NT, preferred_element_type=jnp.float32) for part in (high, low)]
        norm_ref[:, rows_of(i)] = (sums[0] + sums[1])[:1] * scale
        return 0

    lax.fori_loop(0, chunks, body, 0)
    for copy in others:
        copy.wait()


def load_all(features, residual, coefficients, scale, chunk=512):
    rows = features.shape[0]
    arrays = (features, residual, coefficients)
    vmem, hbm = pl.BlockSpec(memory_space=pltpu.VMEM), pl.BlockSpec(memory_space=pltpu.HBM)
    return pl.pallas_call(
        functools.partial(load_kernel, scale, chunk),
        in_specs=[hbm] * 3,
        out_specs=(vmem,) * 4,
        out_shape=(jax.ShapeDtypeStruct((1, rows), jnp.float32),)
        + tuple(pltpu.VMEM(value.shape, value.dtype) for value in arrays),
        scratch_shapes=[pltpu.SemaphoreType.DMA((rows // chunk,)), pltpu.SemaphoreType.DMA((2,))],
        compiler_params=pltpu.CompilerParams(vmem_limit_bytes=SMALL_LIMIT),
        cost_estimate=pl.CostEstimate(flops=3 * 10**9, bytes_accessed=8 * 1024 * 1024, transcendentals=0),
        name="load",
    )(*(pltpu.with_memory_space_constraint(value, pltpu.HBM) for value in arrays))


def slab_kernel(scale, chunk, *refs):
    refs = list(refs)
    ahead_ref, bnorm, grad = refs[-3], refs[-2], refs[-1]
    second = len(refs) > 10
    half_ref, feat_ref, norm_ref, res_ref, coef_ref = refs[:5]
    if second:
        core_ref, first_slab, first_grad, slab_ref, piece_ref, grads, cross = refs[5:12]
        cross[...] = jnp.zeros_like(cross)
    else:
        slab_ref = refs[5]
    scale2 = scale * LOG2E
    part = BLOCK // 2
    bnorm[...] = jnp.broadcast_to(scaled_norm(half_ref[...], scale2), bnorm.shape)
    grad[...] = jnp.zeros_like(grad)
    chunks = feat_ref.shape[0] // chunk
    rows_of = lambda i: pl.ds(pl.multiple_of(i * chunk, chunk), chunk)
    at_of = lambda p: slice(p * part, (p + 1) * part)

    def product(i, p):
        return lax.dot_general(half_ref[at_of(p)], feat_ref[rows_of(i), :], NT, preferred_element_type=jnp.float32)

    ahead_ref[...] = product(0, 0)

    def body(i, _):
        rows = rows_of(i)
        weighted = (res_ref[rows, :] - RIDGE * coef_ref[rows, :]).astype(jnp.bfloat16)
        norm_row = norm_ref[:, rows] * LOG2E
        dots = ahead_ref[...]
        for p in range(STEPS):
            ahead = product(i, p + 1) if p + 1 < STEPS else product(jnp.minimum(i + 1, chunks - 1), 0)
            norm_wide = jnp.concatenate([bnorm[at_of(p)]] * (chunk // bnorm.shape[1]), axis=1)
            slab = jnp.exp2(dots * (2.0 * scale2) - norm_wide - norm_row).astype(jnp.bfloat16)
            slab_ref[at_of(p), rows] = slab
            if p == 0:
                grad[...] += jnp.dot(slab, weighted, preferred_element_type=jnp.float32)
            dots = ahead
        ahead_ref[...] = dots
        if second:
            left = [first_slab[at_of(0), rows], slab_ref[at_of(0), rows], jnp.transpose(weighted)]
            right = [first_slab[at_of(1), rows], slab_ref[at_of(1), rows]]
            cross[...] += lax.dot_general(
                jnp.concatenate(left, axis=0), jnp.concatenate(right, axis=0), NT, preferred_element_type=jnp.float32
            )
        return 0

    lax.fori_loop(0, chunks, body, 0, unroll=2)
    if not second:
        refs[6][...] = grad[...]
        return
    grads[:, at_of(0)] = jnp.transpose(first_grad[...])
    grads[:, at_of(1)] = jnp.transpose(grad[...])
    grads[:, BLOCK:] = cross[BLOCK:]
    groups = piece_ref.shape[0]
    own, depth = grads.shape[0] // groups, BLOCK // groups
    exact = STEPS * own
    place = lambda h: ((1 - core_ref[0]) if h else core_ref[0]) * part
    lanes = lambda base, h: pl.ds(pl.multiple_of(base + place(h), part), part)
    for h in range(2):
        to = at_of(h)
        for s in range(STEPS):
            value = grads[:, lanes(s * BLOCK, h)]
            high = value.astype(jnp.bfloat16)
            low = (value - high.astype(jnp.float32)).astype(jnp.bfloat16)
            for d in range(groups):
                here = slice(d * own, (d + 1) * own)
                piece_ref[d, s * own : (s + 1) * own, to] = high[here]
                piece_ref[d, exact + s * own : exact + (s + 1) * own, to] = low[here]
        for d in range(groups):
            row = place(d * depth // part) + d * depth % part
            value = cross[pl.ds(pl.multiple_of(row, depth), depth), lanes(0, h)]
            piece_ref[d, 2 * exact :, to] = value.astype(jnp.bfloat16)


def in_vmem(value):
    return pltpu.with_memory_space_constraint(value, pltpu.VMEM)


def slabs(half, features, norms, residual, coefficients, scale, groups=0, core=None, first=(), chunk=512):
    rows, width = features.shape
    targets = residual.shape[1]
    vmem = pl.BlockSpec(memory_space=pltpu.VMEM)
    slab = pltpu.VMEM((BLOCK, rows), jnp.bfloat16)
    inputs = [half, in_vmem(features), norms, in_vmem(residual), in_vmem(coefficients)]
    in_specs = [vmem] * 5
    scratch = [
        pltpu.VMEM((BLOCK // 2, chunk), jnp.float32),
        pltpu.VMEM((BLOCK, 128), jnp.float32),
        pltpu.VMEM((BLOCK // 2, targets), jnp.float32),
    ]
    out = jax.ShapeDtypeStruct((BLOCK // 2, targets), jnp.float32)
    if first:
        piece = (groups, 2 * STEPS * targets // groups + BLOCK // groups, BLOCK)
        out = jax.ShapeDtypeStruct(piece, jnp.bfloat16)
        inputs += [core, in_vmem(first[0]), first[1]]
        in_specs += [pl.BlockSpec(memory_space=pltpu.SMEM), vmem, vmem]
        scratch = [
            pltpu.VMEM((targets, STEPS * BLOCK), jnp.float32),
            pltpu.VMEM((BLOCK + targets, BLOCK), jnp.float32),
        ] + scratch
    return pl.pallas_call(
        functools.partial(slab_kernel, scale, chunk),
        in_specs=in_specs,
        out_shape=(slab, out),
        scratch_shapes=scratch,
        compiler_params=pltpu.CompilerParams(vmem_limit_bytes=VMEM_LIMIT),
        cost_estimate=pl.CostEstimate(
            flops=2 * rows * BLOCK * (width + targets + (BLOCK if first else 0)),
            bytes_accessed=rows * (width * 2 + targets * 8 + BLOCK * 2),
            transcendentals=rows * BLOCK,
        ),
        name="slabs",
    )(*inputs)


def eliminate(tiles, t, lane, scaled_ref, waiting):
    start, shape = 8 * t, tiles[t].shape
    wide = lambda tile, k: jnp.broadcast_to(tile[:, start + k : start + k + 1], shape)
    rows = [jnp.broadcast_to(tiles[t][k : k + 1], shape) for k in range(8)]
    at = {(i, k): wide(rows[i], k) for i in range(8) for k in range(i, 8)}
    units = [jnp.where(lane == start + k, 1.0, 0.0) for k in range(8)]
    rows = [row + unit for row, unit in zip(rows, units)]
    total, lower = [None] * 8, {}
    waiting, share = list(waiting), -(-len(waiting) // 4)
    for r in range(0, 8, 2):
        p, m, q = at[r, r], at[r, r + 1], at[r + 1, r + 1]
        det = p * q - m * m
        guess = pl.reciprocal(det, approx=True)
        for _ in range(min(share, len(waiting))):
            waiting.pop(0)()
        refine = 2.0 - det * guess
        inverse = guess * refine
        for k in range(r + 2, 8):
            first = q * at[r, k] - m * at[r + 1, k]
            second = p * at[r + 1, k] - m * at[r, k]
            lower[r, k], lower[r + 1, k] = first * inverse, second * inverse
            for i in range(r + 2, k + 1):
                product = at[r, i] * first + at[r + 1, i] * second
                change = product * guess * refine if k < r + 4 else product * inverse
                at[i, k] = at[i, k] - change
            rows[k] = rows[k] - (first * rows[r] + second * rows[r + 1]) * inverse
        total[r] = (q * rows[r] - m * rows[r + 1]) * inverse
        total[r + 1] = (p * rows[r + 1] - m * rows[r]) * inverse
    for r in (4, 2, 0):
        for k in range(7, r + 1, -1):
            total[r] = total[r] - lower[r, k] * total[k]
            total[r + 1] = total[r + 1] - lower[r + 1, k] * total[k]
    for k in range(8):
        scaled_ref[start + k : start + k + 1] = total[k][:1] - units[k][:1]

    def update(u):
        parts = [wide(tiles[u], k) * total[k] for k in range(8)]
        while len(parts) > 1:
            parts = [x + y for x, y in zip(parts[::2], parts[1::2])]
        tiles[u] = tiles[u] - parts[0]

    if t + 1 < len(tiles):
        update(t + 1)
    return [functools.partial(update, u) for u in range(t + 2, len(tiles))]


def factor_kernel(index, copied, scale, *refs):
    refs = list(refs)
    rest_ref, _, _ = refs.pop(0), refs.pop(0), refs.pop(0)
    before_ref = refs.pop(0) if index else None
    scaled = refs.pop()
    if copied:
        sem = refs.pop()
        copy = pltpu.make_async_copy(refs.pop(0), refs.pop(), sem)
        copy.start()
    if index == 1:
        block_ref, cross_ref = refs.pop(0), refs.pop()
        cross_ref[...] = kernel_of(block_ref[:BLOCK], block_ref[BLOCK:], scale).astype(cross_ref.dtype)
    factor_ref = refs[0]
    here = slice(index * TILE, (index + 1) * TILE)
    dot = functools.partial(lax.dot_general, precision=HIGH, preferred_element_type=jnp.float32)
    plain = (((1,), (0,)), ((), ()))

    def updated(rows):
        if not index:
            return rest_ref[rows]
        then = slice((index - 1) * TILE, index * TILE)
        old = rest_ref[rows]
        inside = lax.broadcasted_iota(jnp.int32, old.shape, 1) // TILE == index - 1
        return jnp.where(inside, 0.0, old) - dot(rest_ref[rows, then], before_ref[TILE:], plain)

    first = TILE if index == 1 else 0
    factor_ref[:TILE] = updated(slice(first, first + TILE))
    row_ids = lax.broadcasted_iota(jnp.int32, (TILE, TILE), 0)
    col_ids = lax.broadcasted_iota(jnp.int32, (TILE, TILE), 1)
    lane = lax.broadcasted_iota(jnp.int32, (8, TILE), 1)
    tiles = [factor_ref[8 * t : 8 * t + 8, here] for t in range(TILE // 8)]
    if len(refs) > 1:
        refs[1][...] = updated(slice(first + TILE, rest_ref.shape[0]))
    waiting = []
    for t in range(TILE // 8):
        waiting = eliminate(tiles, t, lane, scaled, waiting)
    start = row_ids - row_ids % 8
    lower = jnp.where(col_ids < start, jnp.concatenate(tiles, axis=0), 0.0)
    lower = lower + jnp.where(col_ids == row_ids, 1.0, 0.0)
    right = jnp.where(col_ids < start + 8, scaled[...], 0.0)
    inv = dot(lower, right, (((0,), (0,)), ((), ())))
    panel = dot(inv, factor_ref[:TILE], plain)
    inside = lax.broadcasted_iota(jnp.int32, panel.shape, 1) // TILE == index
    factor_ref[TILE:] = jnp.where(inside, jnp.concatenate([inv] * (BLOCK // TILE), axis=1), panel)
    if copied:
        copy.wait()


def factor_step(rest, index, slab, before=None, copied=None, block=None, scale=None):
    left = BLOCK - (index + 1) * TILE
    vmem, hbm = pl.BlockSpec(memory_space=pltpu.VMEM), pl.BlockSpec(memory_space=pltpu.HBM)
    out = [jax.ShapeDtypeStruct((2 * TILE, BLOCK), jnp.float32)]
    inputs, scratch = [rest, *map(in_vmem, slab)], [pltpu.VMEM((TILE, TILE), jnp.float32)]
    if index:
        inputs.append(before)
        if left:
            out.append(jax.ShapeDtypeStruct((left, BLOCK), jnp.float32))
    if block is not None:
        inputs.append(block)
        out.append(jax.ShapeDtypeStruct((BLOCK, BLOCK), jnp.bfloat16))
    in_specs, out_specs = [vmem] * len(inputs), [vmem] * len(out)
    if copied is not None:
        inputs.append(in_vmem(copied))
        in_specs.append(vmem)
        out.append(pltpu.HBM(copied.shape, copied.dtype))
        out_specs.append(hbm)
        scratch.insert(0, pltpu.SemaphoreType.DMA)
    return pl.pallas_call(
        functools.partial(factor_kernel, index, copied is not None, scale),
        in_specs=in_specs,
        out_specs=tuple(out_specs),
        out_shape=tuple(out),
        scratch_shapes=scratch,
        compiler_params=pltpu.CompilerParams(vmem_limit_bytes=SMALL_LIMIT),
        cost_estimate=pl.CostEstimate(flops=6 * 10**9, bytes_accessed=4 * 1024 * 1024, transcendentals=0),
        name="factor",
    )(*inputs)


def apply_inverse(value, refs):
    upto = lambda k: slice(0, k * TILE)
    dot = functools.partial(lax.dot_general, precision=HIGH, preferred_element_type=jnp.float32)
    count = BLOCK // TILE
    middle = [dot(value[:, upto(k + 1)], refs[k][TILE:, upto(k + 1)], NT) for k in range(count)]
    added = {k: dot(middle[k], refs[k][:TILE, upto(k)], (((1,), (0,)), ((), ()))) for k in range(1, count)}
    out = []
    for j in range(count):
        total = middle[j]
        for k in range(j + 1, count):
            total = total + added[k][:, j * TILE : (j + 1) * TILE]
        out.append(total)
    return jnp.concatenate(out, axis=1)


def final_kernel(step_size, chunk, owner_ref, tiles_ref, me_ref, core_ref, packed_ref, gram_ref, slab0_ref, slab1_ref, res_ref, coef_ref, base_ref, *refs):
    factors, refs = refs[: 2 * (BLOCK // TILE)], refs[2 * (BLOCK // TILE) :]
    res_out, coef_out, upd_ref, wide_ref, part_ref, ahead_ref, res_buf, tile_buf, res_sems, tile_sems = refs
    rows, targets = res_ref.shape
    own = targets // packed_ref.shape[0]
    exact = STEPS * own
    count = BLOCK // TILE

    def gradient(s):
        high = packed_ref[:, s * own : (s + 1) * own].astype(jnp.float32)
        low = packed_ref[:, exact + s * own : exact + (s + 1) * own].astype(jnp.float32)
        return (high + low).reshape(targets, BLOCK)

    dot = functools.partial(jnp.dot, preferred_element_type=jnp.float32)
    first = apply_inverse(gradient(0), factors[:count]) * step_size
    high = first.astype(jnp.bfloat16)
    low = (first - high.astype(jnp.float32)).astype(jnp.bfloat16)
    half = BLOCK // 2
    upd_ref[...] = high
    mine, theirs = (pl.ds(pl.multiple_of(c * half, half), half) for c in (core_ref[0], 1 - core_ref[0]))
    mine_high, theirs_high = upd_ref[:, mine], upd_ref[:, theirs]
    for i in range(rows // chunk):
        at = slice(i * chunk, (i + 1) * chunk)
        part_ref[:, at] = dot(mine_high, slab0_ref[:half, at]) + dot(theirs_high, slab1_ref[:half, at])
    cross = packed_ref[:, 2 * exact :].reshape(BLOCK, BLOCK)
    block_part = dot(high, gram_ref[...]) + dot(low, gram_ref[...])
    again = gradient(1) - dot(high, cross) - RIDGE * block_part
    second = apply_inverse(again, factors[count:]) * step_size
    wide_ref[:, :BLOCK] = first
    wide_ref[:, BLOCK:] = second
    upd_ref[...] = second.astype(jnp.bfloat16)

    def change_of(s, k):
        at = s * BLOCK + k * TILE
        return jnp.transpose(wide_ref[:, at : at + TILE])

    def tile_rows(s, k):
        return pl.ds(pl.multiple_of(tiles_ref[s, k] * TILE, TILE), TILE)

    def tile_copy(s, k):
        return pltpu.make_async_copy(tile_buf.at[s, k], coef_out.at[tile_rows(s, k), :], tile_sems.at[s, k])

    owned = [owner_ref[s] == me_ref[0] for s in range(STEPS)]

    def writes(s, k):
        kept = owned[s]
        for later in range(s + 1, STEPS):
            for j in range(count):
                kept = kept & jnp.logical_not(owned[later] & (tiles_ref[later, j] == tiles_ref[s, k]))
        return kept

    for s in range(STEPS):
        for k in range(count):

            @pl.when(writes(s, k))
            def _():
                tile_buf[s, k] = coef_ref[tile_rows(s, k), :] + change_of(s, k)
                for earlier in range(s):
                    for j in range(count):

                        @pl.when(owned[earlier] & (tiles_ref[earlier, j] == tiles_ref[s, k]))
                        def _():
                            tile_buf[s, k] += change_of(earlier, j)

                tile_copy(s, k).start()

    chunks = rows // chunk
    rows_of = lambda i: pl.ds(pl.multiple_of(i * chunk, chunk), chunk)

    def res_copy(i):
        return pltpu.make_async_copy(res_buf.at[rows_of(i), :], res_out.at[rows_of(i), :], res_sems.at[i])

    def product(i):
        change = dot(upd_ref[:, mine], slab0_ref[half:, rows_of(i)])
        return part_ref[:, rows_of(i)] + change + dot(upd_ref[:, theirs], slab1_ref[half:, rows_of(i)])

    ahead_ref[...] = product(0)

    def body(i, _):
        change = ahead_ref[...]
        ahead = product(jnp.minimum(i + 1, chunks - 1))
        res_buf[rows_of(i), :] = res_ref[rows_of(i), :] - jnp.transpose(change)
        ahead_ref[...] = ahead
        res_copy(i).start()
        return 0

    lax.fori_loop(0, chunks, body, 0)
    for i in range(rows // chunk):
        res_copy(i).wait()
    for s in range(STEPS):
        for k in range(count):

            @pl.when(writes(s, k))
            def _():
                tile_copy(s, k).wait()


def finish(owner, tiles, me, core, packed, gram12, slab, residual, coefficients, base, factors, step_size, chunk=512):
    rows, targets = residual.shape
    both = STEPS * BLOCK
    count = BLOCK // TILE
    smem, vmem, hbm = (pl.BlockSpec(memory_space=space) for space in (pltpu.SMEM, pltpu.VMEM, pltpu.HBM))
    return pl.pallas_call(
        functools.partial(final_kernel, step_size, chunk),
        in_specs=[smem] * 4 + [vmem] * 6 + [hbm] + [vmem] * len(factors),
        out_specs=(hbm, hbm),
        out_shape=(
            pltpu.HBM(residual.shape, jnp.float32),
            pltpu.HBM(residual.shape, jnp.float32),
        ),
        scratch_shapes=[
            pltpu.VMEM((targets, BLOCK), jnp.bfloat16),
            pltpu.VMEM((targets, both), jnp.float32),
            pltpu.VMEM((targets, rows), jnp.float32),
            pltpu.VMEM((targets, chunk), jnp.float32),
            pltpu.VMEM((rows, targets), jnp.float32),
            pltpu.VMEM((STEPS, count, TILE, targets), jnp.float32),
            pltpu.SemaphoreType.DMA((rows // chunk,)),
            pltpu.SemaphoreType.DMA((STEPS, count)),
        ],
        input_output_aliases={10: 1},
        compiler_params=pltpu.CompilerParams(vmem_limit_bytes=VMEM_LIMIT),
        cost_estimate=pl.CostEstimate(
            flops=2 * rows * both * targets, bytes_accessed=rows * (both * 2 + targets * 16), transcendentals=0
        ),
        name="finish",
    )(owner, tiles, me, core, packed, gram12, *map(in_vmem, slab), in_vmem(residual), in_vmem(coefficients), base, *factors)


def local(features, residual, coefficients, block_owner, block_tiles):
    rows_dev, width = features.shape
    targets = residual.shape[1]
    sub_count = lax.axis_size("sub")
    devices = lax.axis_size("rows") * sub_count
    me = lax.axis_index(AXES).astype(jnp.int32)
    scale = 1.0 / width
    step_size = 1.0 / math.sqrt(rows_dev * devices)
    spread = Spread(AXES, sub_count) if devices <= 32 else Spread(("rows",), 1)
    groups = spread.count
    own = targets // groups

    loaded = load_all(features, residual, coefficients, scale)
    half, other, loaded = fetch_blocks(features, loaded, block_owner, block_tiles, me, devices, sub_count)
    norms, features, residual, coefficients = loaded
    core, on_core = bit_of(me, sub_count).reshape(1), (me & sub_count) != 0
    first = slabs(half, features, norms, residual, coefficients, scale)
    other, first = lax.optimization_barrier((other, first))
    last = slabs(other, features, norms, residual, coefficients, scale, groups, core, first)
    slab, pieces = (first[0], last[0]), last[1]
    block = both_halves(half, other, on_core)
    exact = STEPS * own
    if spread.axes != AXES:
        pieces = pack(lax.psum(unpack(pieces, exact), "sub"), exact)
    rest = gram(block, core, scale, slab)
    kept, sent, before, extra = [], [], None, []

    def beside(hop, indices):
        nonlocal before, rest, sent
        then, got = hop
        for index in indices:
            args = {0: {"copied": coefficients}, 1: {"block": block, "scale": scale}}.get(index, {})
            mine, *given = factor_step(rest, index, slab, before, **args)
            if args:
                extra.append(given.pop())
            if index == indices[-1]:
                got, mine, given, sent = lax.optimization_barrier((got, mine, given, sent))
            before, rest = mine, given[0] if given else rest
            sent = sent + [swap(mine, AXES, sub_count)]
            kept.append(mine)
        return then(got)

    value = spread.core_sum(pieces, exact)
    value = beside(spread.near_sum(value, exact), [0])
    value = beside(spread.far_sum(value, exact), [1, 2])
    packed = beside(spread.near_gather(pack(value, exact)), [3])
    base, gram12 = extra
    factors = [jnp.where(on_core, other, mine) for mine, other in zip(kept, sent)]
    factors += [jnp.where(on_core, mine, other) for mine, other in zip(kept, sent)]
    packed = spread.core_gather(packed)
    return finish(
        block_owner, block_tiles, me.reshape(1), core, packed, gram12, slab, residual, coefficients, base,
        factors, step_size,
    )


def solution(mesh):
    row_spec = P(AXES, None)
    return jax.shard_map(
        local,
        mesh=mesh,
        in_specs=(row_spec, row_spec, row_spec, P(), P()),
        out_specs=(row_spec, row_spec),
        check_vma=False,
    )
```

```python
import functools
import math

import jax
import jax.numpy as jnp
import numpy as np
from jax import lax
from jax.experimental import pallas as pl
from jax.experimental.pallas import tpu as pltpu
from jax.sharding import PartitionSpec as P

BLOCK = 512
TILE = 128
STEPS = 2
RIDGE = 0.5
AXES = ("rows", "sub")
HIGH = lax.Precision.HIGHEST
NT = (((1,), (1,)), ((), ()))
LOG2E = math.log2(math.e)
VMEM_LIMIT = 16 * 1024 * 1024
SMALL_LIMIT = 12 * 1024 * 1024


def pick_kernel(tiles_ref, core_ref, feat_ref, keep_ref, send_ref, sems):
    per_half = keep_ref.shape[1] // TILE
    copies = []
    for turn, out in enumerate((keep_ref, send_ref)):
        half = core_ref[0] if turn == 0 else 1 - core_ref[0]
        for s in range(STEPS):
            for i in range(per_half):
                source = pl.multiple_of(tiles_ref[s, half * per_half + i] * TILE, TILE)
                copies.append(
                    pltpu.make_async_copy(
                        feat_ref.at[pl.ds(source, TILE), :],
                        out.at[s, pl.ds(i * TILE, TILE), :],
                        sems.at[turn, s, i],
                    )
                )
    for copy in copies:
        copy.start()
    for copy in copies:
        copy.wait()


def pick_halves(features, block_tiles, core):
    width = features.shape[1]
    half = jax.ShapeDtypeStruct((STEPS, BLOCK // 2, width), features.dtype)
    return pl.pallas_call(
        pick_kernel,
        grid_spec=pltpu.PrefetchScalarGridSpec(
            num_scalar_prefetch=2,
            grid=(1,),
            in_specs=[pl.BlockSpec(memory_space=pltpu.HBM)],
            out_specs=[pl.BlockSpec(half.shape, lambda i, *_: (0, 0, 0))] * 2,
            scratch_shapes=[pltpu.SemaphoreType.DMA((2, STEPS, BLOCK // 2 // TILE))],
        ),
        out_shape=(half, half),
        compiler_params=pltpu.CompilerParams(vmem_limit_bytes=SMALL_LIMIT),
        name="pick",
    )(pltpu.with_memory_space_constraint(block_tiles, pltpu.HBM), core, pltpu.with_memory_space_constraint(features, pltpu.HBM))


def swap(value, axes, flip):
    flip_of = flip if callable(flip) else lambda i: flip
    return lax.ppermute(value, axes, [(i, i ^ flip_of(i)) for i in range(lax.axis_size(axes))])


def bit_of(index, mask):
    return ((index & mask) != 0).astype(jnp.int32)


def swap_among(pick, me, axes, low, high):
    place = (bit_of(me, low) + 2 * bit_of(me, high)).astype(jnp.uint32)
    flips = [0, low, high, low | high]
    return place, [swap(pick(place ^ np.uint32(c)), axes, flips[c]) for c in (1, 2, 3)]


def ordered(parts, me, low, high, axis):
    one, two = (me & low) != 0, (me & high) != 0
    parts = [jnp.where(one, parts[c ^ 1], parts[c]) for c in range(4)]
    return jnp.stack([jnp.where(two, parts[c ^ 2], parts[c]) for c in range(4)], axis=axis)


def fetch_blocks(features, prepared, block_owner, block_tiles, me, devices, core):
    width = features.shape[1]
    low, high = 1, 2 * core
    differs = lambda mask: (((block_owner ^ me) & mask) != 0)[:, None, None]
    on_core = (me & core) != 0
    keep, send = pick_halves(features, block_tiles, bit_of(me, core).reshape(1))
    half = jnp.where(differs(core), swap(send, AXES, core), keep)
    quarters = half.reshape(STEPS, 4, BLOCK // 8, width)
    pick = lambda place: lax.dynamic_index_in_dim(quarters, place, 1, False)
    place, got = swap_among(pick, me, AXES, low, high)
    got, prepared = lax.optimization_barrier((got, prepared))
    part = jnp.where(
        differs(high),
        jnp.where(differs(low), got[2], got[1]),
        jnp.where(differs(low), got[0], pick(place)),
    )
    far = [1 << b for b in range(devices.bit_length() - 1) if 1 << b not in (core, low, high)]
    hops = []
    for one, two in zip(far[::2], far[1::2]):
        for first, second in ((one, two), (two, one)):
            flip = lambda i, first=first, second=second: second if i & core else first
            hops.append((flip, jnp.where(on_core, second, first)))
    if len(far) % 2:
        hops.append((far[-1], far[-1]))
    for flip, mask in hops:
        other = swap(part, AXES, flip)
        part = jnp.where(differs(mask), other, part)
    _, got = swap_among(lambda place: part, me, AXES, low, high)
    half = ordered([part] + got, me, low, high, 1)
    half = half.reshape(BLOCK, width)
    return half, swap(half, AXES, core), prepared


def both_halves(half, other, on_core):
    half, other = (value.reshape(STEPS, BLOCK // 2, value.shape[1]) for value in (half, other))
    both = jnp.stack([jnp.where(on_core, other, half), jnp.where(on_core, half, other)], axis=1)
    return both.reshape(STEPS * BLOCK, half.shape[2])


def pack(value, exact):
    high = lax.reduce_precision(value[..., :exact, :], 8, 7)
    low = value[..., :exact, :] - high
    return jnp.concatenate([part.astype(jnp.bfloat16) for part in (high, low, value[..., exact:, :])], axis=-2)


def unpack(value, exact):
    value = value.astype(jnp.float32)
    return jnp.concatenate([value[..., :exact, :] + value[..., exact : 2 * exact, :], value[..., 2 * exact :, :]], axis=-2)


class Spread:
    def __init__(self, axes, core):
        self.axes, self.core = axes, core
        self.me = lax.axis_index(axes).astype(jnp.int32)
        self.near = [1 << b for b in range(3) if 1 << b != core]
        self.far = [1 << b for b in range(3, lax.axis_size(axes).bit_length() - 1)]
        self.count = 8
        self.core_axis = 2 - (core.bit_length() - 1)

    def core_sum(self, packed, exact):
        packed = packed.reshape((2,) * 3 + packed.shape[1:])
        zero, one = (lax.index_in_dim(packed, i, self.core_axis, False) for i in (0, 1))
        bit = (self.me & self.core) != 0
        got = swap(jnp.where(bit, zero, one), self.axes, self.core)
        value = unpack(jnp.where(bit, one, zero), exact) + unpack(got, exact)
        return value.reshape((4,) + value.shape[2:])

    def near_sum(self, value, exact):
        packed = pack(value, exact)
        pick = lambda array, place: lax.dynamic_index_in_dim(array, place, 0, False)
        place, got = swap_among(lambda place: pick(packed, place), self.me, self.axes, *self.near)
        return lambda got: pick(value, place) + unpack(got[0], exact) + unpack(got[1], exact) + unpack(got[2], exact), got

    def far_sum(self, value, exact):
        packed = pack(value, exact)
        _, got = swap_among(lambda place: packed, self.me, self.axes, *self.far)
        return lambda got: value + unpack(got[0], exact) + unpack(got[1], exact) + unpack(got[2], exact), got

    def near_gather(self, value):
        _, got = swap_among(lambda place: value, self.me, self.axes, *self.near)
        return lambda got: ordered([value] + got, self.me, *self.near, 0), got

    def core_gather(self, value):
        rest = value.shape[1:]
        value = value.reshape((2, 2) + rest)
        bit = (self.me & self.core) != 0
        got = swap(value, self.axes, self.core)
        value = jnp.stack([jnp.where(bit, got, value), jnp.where(bit, value, got)], axis=self.core_axis)
        return value.reshape((self.count,) + rest)


def scaled_norm(rows, scale):
    wide = rows.astype(jnp.float32)
    return jnp.sum(wide * wide, axis=1, keepdims=True) * scale


def kernel_of(left, right, scale):
    dots = lax.dot_general(left, right, NT, preferred_element_type=jnp.float32)
    row = jnp.transpose(jnp.broadcast_to(scaled_norm(right, scale), (BLOCK, 128)))[:1]
    return jnp.exp(dots * (2.0 * scale) - scaled_norm(left, scale) - row)


def gram_kernel(scale, core_ref, block_ref, slab0_ref, slab1_ref, own_ref):
    mine = block_ref[pl.ds(pl.multiple_of(core_ref[0] * BLOCK, BLOCK), BLOCK), :]
    diagonal = lax.broadcasted_iota(jnp.int32, (BLOCK, BLOCK), 0) == lax.broadcasted_iota(jnp.int32, (BLOCK, BLOCK), 1)
    own_ref[...] = kernel_of(mine, mine, scale) + jnp.where(diagonal, RIDGE, 0.0)


def gram(block, core, scale, slab):
    vmem = pl.BlockSpec(memory_space=pltpu.VMEM)
    return pl.pallas_call(
        functools.partial(gram_kernel, scale),
        in_specs=[pl.BlockSpec(memory_space=pltpu.SMEM)] + [vmem] * 3,
        out_shape=jax.ShapeDtypeStruct((BLOCK, BLOCK), jnp.float32),
        compiler_params=pltpu.CompilerParams(vmem_limit_bytes=SMALL_LIMIT),
        cost_estimate=pl.CostEstimate(
            flops=2 * BLOCK**3, bytes_accessed=4 * BLOCK * BLOCK * 2, transcendentals=BLOCK**2
        ),
        name="gram",
    )(core, block, *map(in_vmem, slab))


def load_kernel(scale, chunk, feat_in, res_in, coef_in, norm_ref, feat_ref, res_ref, coef_ref, sems, more_sems):
    chunks = feat_in.shape[0] // chunk
    rows_of = lambda i: pl.ds(pl.multiple_of(i * chunk, chunk), chunk)

    def load(i):
        return pltpu.make_async_copy(feat_in.at[rows_of(i), :], feat_ref.at[rows_of(i), :], sems.at[i])

    others = [
        pltpu.make_async_copy(source, target, more_sems.at[i])
        for i, (source, target) in enumerate(((res_in, res_ref), (coef_in, coef_ref)))
    ]
    for i in range(chunks):
        load(i).start()
    for copy in others:
        copy.start()
    ones = jnp.ones((16, feat_in.shape[1]), jnp.bfloat16)

    def body(i, _):
        load(i).wait()
        wide = feat_ref[rows_of(i), :].astype(jnp.float32)
        square = wide * wide
        high = square.astype(jnp.bfloat16)
        low = (square - high.astype(jnp.float32)).astype(jnp.bfloat16)
        sums = [lax.dot_general(ones, part, NT, preferred_element_type=jnp.float32) for part in (high, low)]
        norm_ref[:, rows_of(i)] = (sums[0] + sums[1])[:1] * scale
        return 0

    lax.fori_loop(0, chunks, body, 0)
    for copy in others:
        copy.wait()


def load_all(features, residual, coefficients, scale, chunk=512):
    rows = features.shape[0]
    arrays = (features, residual, coefficients)
    vmem, hbm = pl.BlockSpec(memory_space=pltpu.VMEM), pl.BlockSpec(memory_space=pltpu.HBM)
    return pl.pallas_call(
        functools.partial(load_kernel, scale, chunk),
        in_specs=[hbm] * 3,
        out_specs=(vmem,) * 4,
        out_shape=(jax.ShapeDtypeStruct((1, rows), jnp.float32),)
        + tuple(pltpu.VMEM(value.shape, value.dtype) for value in arrays),
        scratch_shapes=[pltpu.SemaphoreType.DMA((rows // chunk,)), pltpu.SemaphoreType.DMA((2,))],
        compiler_params=pltpu.CompilerParams(vmem_limit_bytes=SMALL_LIMIT),
        cost_estimate=pl.CostEstimate(flops=3 * 10**9, bytes_accessed=8 * 1024 * 1024, transcendentals=0),
        name="load",
    )(*(pltpu.with_memory_space_constraint(value, pltpu.HBM) for value in arrays))


def slab_kernel(scale, chunk, *refs):
    refs = list(refs)
    ahead_ref, bnorm, grad = refs[-3], refs[-2], refs[-1]
    second = len(refs) > 10
    half_ref, feat_ref, norm_ref, res_ref, coef_ref = refs[:5]
    if second:
        core_ref, first_slab, first_grad, slab_ref, piece_ref, grads, cross = refs[5:12]
        cross[...] = jnp.zeros_like(cross)
    else:
        slab_ref = refs[5]
    scale2 = scale * LOG2E
    part = BLOCK // 2
    bnorm[...] = jnp.broadcast_to(scaled_norm(half_ref[...], scale2), bnorm.shape)
    grad[...] = jnp.zeros_like(grad)
    chunks = feat_ref.shape[0] // chunk
    rows_of = lambda i: pl.ds(pl.multiple_of(i * chunk, chunk), chunk)
    at_of = lambda p: slice(p * part, (p + 1) * part)

    def product(i, p):
        return lax.dot_general(half_ref[at_of(p)], feat_ref[rows_of(i), :], NT, preferred_element_type=jnp.float32)

    ahead_ref[...] = product(0, 0)

    def body(i, _):
        rows = rows_of(i)
        weighted = (res_ref[rows, :] - RIDGE * coef_ref[rows, :]).astype(jnp.bfloat16)
        norm_row = norm_ref[:, rows] * LOG2E
        dots = ahead_ref[...]
        for p in range(STEPS):
            ahead = product(i, p + 1) if p + 1 < STEPS else product(jnp.minimum(i + 1, chunks - 1), 0)
            norm_wide = jnp.concatenate([bnorm[at_of(p)]] * (chunk // bnorm.shape[1]), axis=1)
            slab = jnp.exp2(dots * (2.0 * scale2) - norm_wide - norm_row).astype(jnp.bfloat16)
            slab_ref[at_of(p), rows] = slab
            if p == 0:
                grad[...] += jnp.dot(slab, weighted, preferred_element_type=jnp.float32)
            dots = ahead
        ahead_ref[...] = dots
        if second:
            left = [first_slab[at_of(0), rows], slab_ref[at_of(0), rows], jnp.transpose(weighted)]
            right = [first_slab[at_of(1), rows], slab_ref[at_of(1), rows]]
            cross[...] += lax.dot_general(
                jnp.concatenate(left, axis=0), jnp.concatenate(right, axis=0), NT, preferred_element_type=jnp.float32
            )
        return 0

    lax.fori_loop(0, chunks, body, 0, unroll=4)
    if not second:
        refs[6][...] = grad[...]
        return
    grads[:, at_of(0)] = jnp.transpose(first_grad[...])
    grads[:, at_of(1)] = jnp.transpose(grad[...])
    grads[:, BLOCK:] = cross[BLOCK:]
    groups = piece_ref.shape[0]
    own, depth = grads.shape[0] // groups, BLOCK // groups
    exact = STEPS * own
    place = lambda h: ((1 - core_ref[0]) if h else core_ref[0]) * part
    lanes = lambda base, h: pl.ds(pl.multiple_of(base + place(h), part), part)
    for h in range(2):
        to = at_of(h)
        for s in range(STEPS):
            value = grads[:, lanes(s * BLOCK, h)]
            high = value.astype(jnp.bfloat16)
            low = (value - high.astype(jnp.float32)).astype(jnp.bfloat16)
            for d in range(groups):
                here = slice(d * own, (d + 1) * own)
                piece_ref[d, s * own : (s + 1) * own, to] = high[here]
                piece_ref[d, exact + s * own : exact + (s + 1) * own, to] = low[here]
        for d in range(groups):
            row = place(d * depth // part) + d * depth % part
            value = cross[pl.ds(pl.multiple_of(row, depth), depth), lanes(0, h)]
            piece_ref[d, 2 * exact :, to] = value.astype(jnp.bfloat16)


def in_vmem(value):
    return pltpu.with_memory_space_constraint(value, pltpu.VMEM)


def slabs(half, features, norms, residual, coefficients, scale, groups=0, core=None, first=(), chunk=512):
    rows, width = features.shape
    targets = residual.shape[1]
    vmem = pl.BlockSpec(memory_space=pltpu.VMEM)
    slab = pltpu.VMEM((BLOCK, rows), jnp.bfloat16)
    inputs = [half, in_vmem(features), norms, in_vmem(residual), in_vmem(coefficients)]
    in_specs = [vmem] * 5
    scratch = [
        pltpu.VMEM((BLOCK // 2, chunk), jnp.float32),
        pltpu.VMEM((BLOCK, 128), jnp.float32),
        pltpu.VMEM((BLOCK // 2, targets), jnp.float32),
    ]
    out = jax.ShapeDtypeStruct((BLOCK // 2, targets), jnp.float32)
    if first:
        piece = (groups, 2 * STEPS * targets // groups + BLOCK // groups, BLOCK)
        out = jax.ShapeDtypeStruct(piece, jnp.bfloat16)
        inputs += [core, in_vmem(first[0]), first[1]]
        in_specs += [pl.BlockSpec(memory_space=pltpu.SMEM), vmem, vmem]
        scratch = [
            pltpu.VMEM((targets, STEPS * BLOCK), jnp.float32),
            pltpu.VMEM((BLOCK + targets, BLOCK), jnp.float32),
        ] + scratch
    return pl.pallas_call(
        functools.partial(slab_kernel, scale, chunk),
        in_specs=in_specs,
        out_shape=(slab, out),
        scratch_shapes=scratch,
        compiler_params=pltpu.CompilerParams(vmem_limit_bytes=VMEM_LIMIT),
        cost_estimate=pl.CostEstimate(
            flops=2 * rows * BLOCK * (width + targets + (BLOCK if first else 0)),
            bytes_accessed=rows * (width * 2 + targets * 8 + BLOCK * 2),
            transcendentals=rows * BLOCK,
        ),
        name="slabs",
    )(*inputs)


def eliminate(tiles, t, lane, scaled_ref, waiting):
    start, shape = 8 * t, tiles[t].shape
    wide = lambda tile, k: jnp.broadcast_to(tile[:, start + k : start + k + 1], shape)
    rows = [jnp.broadcast_to(tiles[t][k : k + 1], shape) for k in range(8)]
    at = {(i, k): wide(rows[i], k) for i in range(8) for k in range(i, 8)}
    units = [jnp.where(lane == start + k, 1.0, 0.0) for k in range(8)]
    rows = [row + unit for row, unit in zip(rows, units)]
    total, lower = [None] * 8, {}
    waiting, share = list(waiting), -(-len(waiting) // 4)
    for r in range(0, 8, 2):
        p, m, q = at[r, r], at[r, r + 1], at[r + 1, r + 1]
        det = p * q - m * m
        guess = pl.reciprocal(det, approx=True)
        for _ in range(min(share, len(waiting))):
            waiting.pop(0)()
        refine = 2.0 - det * guess
        inverse = guess * refine
        for k in range(r + 2, 8):
            first = q * at[r, k] - m * at[r + 1, k]
            second = p * at[r + 1, k] - m * at[r, k]
            lower[r, k], lower[r + 1, k] = first * inverse, second * inverse
            for i in range(r + 2, k + 1):
                product = at[r, i] * first + at[r + 1, i] * second
                change = product * guess * refine if k < r + 4 else product * inverse
                at[i, k] = at[i, k] - change
            rows[k] = rows[k] - (first * rows[r] + second * rows[r + 1]) * inverse
        total[r] = (q * rows[r] - m * rows[r + 1]) * inverse
        total[r + 1] = (p * rows[r + 1] - m * rows[r]) * inverse
    for r in (4, 2, 0):
        for k in range(7, r + 1, -1):
            total[r] = total[r] - lower[r, k] * total[k]
            total[r + 1] = total[r + 1] - lower[r + 1, k] * total[k]
    for k in range(8):
        scaled_ref[start + k : start + k + 1] = total[k][:1] - units[k][:1]

    def update(u):
        parts = [wide(tiles[u], k) * total[k] for k in range(8)]
        while len(parts) > 1:
            parts = [x + y for x, y in zip(parts[::2], parts[1::2])]
        tiles[u] = tiles[u] - parts[0]

    if t + 1 < len(tiles):
        update(t + 1)
    return [functools.partial(update, u) for u in range(t + 2, len(tiles))]


def factor_kernel(index, copied, scale, *refs):
    refs = list(refs)
    rest_ref, _, _ = refs.pop(0), refs.pop(0), refs.pop(0)
    before_ref = refs.pop(0) if index else None
    scaled = refs.pop()
    if copied:
        sem = refs.pop()
        copy = pltpu.make_async_copy(refs.pop(0), refs.pop(), sem)
        copy.start()
    if index == 1:
        block_ref, cross_ref = refs.pop(0), refs.pop()
        cross_ref[...] = kernel_of(block_ref[:BLOCK], block_ref[BLOCK:], scale).astype(cross_ref.dtype)
    factor_ref = refs[0]
    here = slice(index * TILE, (index + 1) * TILE)
    dot = functools.partial(lax.dot_general, precision=HIGH, preferred_element_type=jnp.float32)
    plain = (((1,), (0,)), ((), ()))

    def updated(rows):
        if not index:
            return rest_ref[rows]
        then = slice((index - 1) * TILE, index * TILE)
        old = rest_ref[rows]
        inside = lax.broadcasted_iota(jnp.int32, old.shape, 1) // TILE == index - 1
        return jnp.where(inside, 0.0, old) - dot(rest_ref[rows, then], before_ref[TILE:], plain)

    first = TILE if index == 1 else 0
    factor_ref[:TILE] = updated(slice(first, first + TILE))
    row_ids = lax.broadcasted_iota(jnp.int32, (TILE, TILE), 0)
    col_ids = lax.broadcasted_iota(jnp.int32, (TILE, TILE), 1)
    lane = lax.broadcasted_iota(jnp.int32, (8, TILE), 1)
    tiles = [factor_ref[8 * t : 8 * t + 8, here] for t in range(TILE // 8)]
    if len(refs) > 1:
        refs[1][...] = updated(slice(first + TILE, rest_ref.shape[0]))
    waiting = []
    for t in range(TILE // 8):
        waiting = eliminate(tiles, t, lane, scaled, waiting)
    start = row_ids - row_ids % 8
    lower = jnp.where(col_ids < start, jnp.concatenate(tiles, axis=0), 0.0)
    lower = lower + jnp.where(col_ids == row_ids, 1.0, 0.0)
    right = jnp.where(col_ids < start + 8, scaled[...], 0.0)
    inv = dot(lower, right, (((0,), (0,)), ((), ())))
    panel = dot(inv, factor_ref[:TILE], plain)
    inside = lax.broadcasted_iota(jnp.int32, panel.shape, 1) // TILE == index
    factor_ref[TILE:] = jnp.where(inside, jnp.concatenate([inv] * (BLOCK // TILE), axis=1), panel)
    if copied:
        copy.wait()


def factor_step(rest, index, slab, before=None, copied=None, block=None, scale=None):
    left = BLOCK - (index + 1) * TILE
    vmem, hbm = pl.BlockSpec(memory_space=pltpu.VMEM), pl.BlockSpec(memory_space=pltpu.HBM)
    out = [jax.ShapeDtypeStruct((2 * TILE, BLOCK), jnp.float32)]
    inputs, scratch = [rest, *map(in_vmem, slab)], [pltpu.VMEM((TILE, TILE), jnp.float32)]
    if index:
        inputs.append(before)
        if left:
            out.append(jax.ShapeDtypeStruct((left, BLOCK), jnp.float32))
    if block is not None:
        inputs.append(block)
        out.append(jax.ShapeDtypeStruct((BLOCK, BLOCK), jnp.bfloat16))
    in_specs, out_specs = [vmem] * len(inputs), [vmem] * len(out)
    if copied is not None:
        inputs.append(in_vmem(copied))
        in_specs.append(vmem)
        out.append(pltpu.HBM(copied.shape, copied.dtype))
        out_specs.append(hbm)
        scratch.insert(0, pltpu.SemaphoreType.DMA)
    return pl.pallas_call(
        functools.partial(factor_kernel, index, copied is not None, scale),
        in_specs=in_specs,
        out_specs=tuple(out_specs),
        out_shape=tuple(out),
        scratch_shapes=scratch,
        compiler_params=pltpu.CompilerParams(vmem_limit_bytes=SMALL_LIMIT),
        cost_estimate=pl.CostEstimate(flops=6 * 10**9, bytes_accessed=4 * 1024 * 1024, transcendentals=0),
        name="factor",
    )(*inputs)


def apply_inverse(value, refs):
    upto = lambda k: slice(0, k * TILE)
    dot = functools.partial(lax.dot_general, precision=HIGH, preferred_element_type=jnp.float32)
    count = BLOCK // TILE
    middle = [dot(value[:, upto(k + 1)], refs[k][TILE:, upto(k + 1)], NT) for k in range(count)]
    added = {k: dot(middle[k], refs[k][:TILE, upto(k)], (((1,), (0,)), ((), ()))) for k in range(1, count)}
    out = []
    for j in range(count):
        total = middle[j]
        for k in range(j + 1, count):
            total = total + added[k][:, j * TILE : (j + 1) * TILE]
        out.append(total)
    return jnp.concatenate(out, axis=1)


def final_kernel(step_size, chunk, owner_ref, tiles_ref, me_ref, core_ref, packed_ref, gram_ref, slab0_ref, slab1_ref, res_ref, coef_ref, base_ref, *refs):
    factors, refs = refs[: 2 * (BLOCK // TILE)], refs[2 * (BLOCK // TILE) :]
    res_out, coef_out, upd_ref, wide_ref, part_ref, ahead_ref, res_buf, tile_buf, res_sems, tile_sems = refs
    rows, targets = res_ref.shape
    own = targets // packed_ref.shape[0]
    exact = STEPS * own
    count = BLOCK // TILE

    def gradient(s):
        high = packed_ref[:, s * own : (s + 1) * own].astype(jnp.float32)
        low = packed_ref[:, exact + s * own : exact + (s + 1) * own].astype(jnp.float32)
        return (high + low).reshape(targets, BLOCK)

    dot = functools.partial(jnp.dot, preferred_element_type=jnp.float32)
    first = apply_inverse(gradient(0), factors[:count]) * step_size
    high = first.astype(jnp.bfloat16)
    low = (first - high.astype(jnp.float32)).astype(jnp.bfloat16)
    half = BLOCK // 2
    upd_ref[...] = high
    mine, theirs = (pl.ds(pl.multiple_of(c * half, half), half) for c in (core_ref[0], 1 - core_ref[0]))
    mine_high, theirs_high = upd_ref[:, mine], upd_ref[:, theirs]
    for i in range(rows // chunk):
        at = slice(i * chunk, (i + 1) * chunk)
        part_ref[:, at] = dot(mine_high, slab0_ref[:half, at]) + dot(theirs_high, slab1_ref[:half, at])
    cross = packed_ref[:, 2 * exact :].reshape(BLOCK, BLOCK)
    block_part = dot(high, gram_ref[...]) + dot(low, gram_ref[...])
    again = gradient(1) - dot(high, cross) - RIDGE * block_part
    second = apply_inverse(again, factors[count:]) * step_size
    wide_ref[:, :BLOCK] = first
    wide_ref[:, BLOCK:] = second
    upd_ref[...] = second.astype(jnp.bfloat16)

    def change_of(s, k):
        at = s * BLOCK + k * TILE
        return jnp.transpose(wide_ref[:, at : at + TILE])

    def tile_rows(s, k):
        return pl.ds(pl.multiple_of(tiles_ref[s, k] * TILE, TILE), TILE)

    def tile_copy(s, k):
        return pltpu.make_async_copy(tile_buf.at[s, k], coef_out.at[tile_rows(s, k), :], tile_sems.at[s, k])

    owned = [owner_ref[s] == me_ref[0] for s in range(STEPS)]

    def writes(s, k):
        kept = owned[s]
        for later in range(s + 1, STEPS):
            for j in range(count):
                kept = kept & jnp.logical_not(owned[later] & (tiles_ref[later, j] == tiles_ref[s, k]))
        return kept

    for s in range(STEPS):
        for k in range(count):

            @pl.when(writes(s, k))
            def _():
                tile_buf[s, k] = coef_ref[tile_rows(s, k), :] + change_of(s, k)
                for earlier in range(s):
                    for j in range(count):

                        @pl.when(owned[earlier] & (tiles_ref[earlier, j] == tiles_ref[s, k]))
                        def _():
                            tile_buf[s, k] += change_of(earlier, j)

                tile_copy(s, k).start()

    chunks = rows // chunk
    rows_of = lambda i: pl.ds(pl.multiple_of(i * chunk, chunk), chunk)

    def res_copy(i):
        return pltpu.make_async_copy(res_buf.at[rows_of(i), :], res_out.at[rows_of(i), :], res_sems.at[i])

    def product(i):
        change = dot(upd_ref[:, mine], slab0_ref[half:, rows_of(i)])
        return part_ref[:, rows_of(i)] + change + dot(upd_ref[:, theirs], slab1_ref[half:, rows_of(i)])

    ahead_ref[...] = product(0)

    def body(i, _):
        change = ahead_ref[...]
        ahead = product(jnp.minimum(i + 1, chunks - 1))
        res_buf[rows_of(i), :] = res_ref[rows_of(i), :] - jnp.transpose(change)
        ahead_ref[...] = ahead
        res_copy(i).start()
        return 0

    lax.fori_loop(0, chunks, body, 0, unroll=2)
    for i in range(rows // chunk):
        res_copy(i).wait()
    for s in range(STEPS):
        for k in range(count):

            @pl.when(writes(s, k))
            def _():
                tile_copy(s, k).wait()


def finish(owner, tiles, me, core, packed, gram12, slab, residual, coefficients, base, factors, step_size, chunk=512):
    rows, targets = residual.shape
    both = STEPS * BLOCK
    count = BLOCK // TILE
    smem, vmem, hbm = (pl.BlockSpec(memory_space=space) for space in (pltpu.SMEM, pltpu.VMEM, pltpu.HBM))
    return pl.pallas_call(
        functools.partial(final_kernel, step_size, chunk),
        in_specs=[smem] * 4 + [vmem] * 6 + [hbm] + [vmem] * len(factors),
        out_specs=(hbm, hbm),
        out_shape=(
            pltpu.HBM(residual.shape, jnp.float32),
            pltpu.HBM(residual.shape, jnp.float32),
        ),
        scratch_shapes=[
            pltpu.VMEM((targets, BLOCK), jnp.bfloat16),
            pltpu.VMEM((targets, both), jnp.float32),
            pltpu.VMEM((targets, rows), jnp.float32),
            pltpu.VMEM((targets, chunk), jnp.float32),
            pltpu.VMEM((rows, targets), jnp.float32),
            pltpu.VMEM((STEPS, count, TILE, targets), jnp.float32),
            pltpu.SemaphoreType.DMA((rows // chunk,)),
            pltpu.SemaphoreType.DMA((STEPS, count)),
        ],
        input_output_aliases={10: 1},
        compiler_params=pltpu.CompilerParams(vmem_limit_bytes=VMEM_LIMIT),
        cost_estimate=pl.CostEstimate(
            flops=2 * rows * both * targets, bytes_accessed=rows * (both * 2 + targets * 16), transcendentals=0
        ),
        name="finish",
    )(owner, tiles, me, core, packed, gram12, *map(in_vmem, slab), in_vmem(residual), in_vmem(coefficients), base, *factors)


def local(features, residual, coefficients, block_owner, block_tiles):
    rows_dev, width = features.shape
    targets = residual.shape[1]
    sub_count = lax.axis_size("sub")
    devices = lax.axis_size("rows") * sub_count
    me = lax.axis_index(AXES).astype(jnp.int32)
    scale = 1.0 / width
    step_size = 1.0 / math.sqrt(rows_dev * devices)
    spread = Spread(AXES, sub_count) if devices <= 32 else Spread(("rows",), 1)
    groups = spread.count
    own = targets // groups

    loaded = load_all(features, residual, coefficients, scale)
    half, other, loaded = fetch_blocks(features, loaded, block_owner, block_tiles, me, devices, sub_count)
    norms, features, residual, coefficients = loaded
    core, on_core = bit_of(me, sub_count).reshape(1), (me & sub_count) != 0
    first = slabs(half, features, norms, residual, coefficients, scale)
    other, first = lax.optimization_barrier((other, first))
    last = slabs(other, features, norms, residual, coefficients, scale, groups, core, first)
    slab, pieces = (first[0], last[0]), last[1]
    block = both_halves(half, other, on_core)
    exact = STEPS * own
    if spread.axes != AXES:
        pieces = pack(lax.psum(unpack(pieces, exact), "sub"), exact)
    rest = gram(block, core, scale, slab)
    kept, sent, before, extra = [], [], None, []

    def beside(hop, indices):
        nonlocal before, rest, sent
        then, got = hop
        for index in indices:
            args = {0: {"copied": coefficients}, 1: {"block": block, "scale": scale}}.get(index, {})
            mine, *given = factor_step(rest, index, slab, before, **args)
            if args:
                extra.append(given.pop())
            if index == indices[-1]:
                got, mine, given, sent = lax.optimization_barrier((got, mine, given, sent))
            before, rest = mine, given[0] if given else rest
            sent = sent + [swap(mine, AXES, sub_count)]
            kept.append(mine)
        return then(got)

    value = spread.core_sum(pieces, exact)
    value = beside(spread.near_sum(value, exact), [0])
    value = beside(spread.far_sum(value, exact), [1, 2])
    packed = beside(spread.near_gather(pack(value, exact)), [3])
    base, gram12 = extra
    factors = [jnp.where(on_core, other, mine) for mine, other in zip(kept, sent)]
    factors += [jnp.where(on_core, mine, other) for mine, other in zip(kept, sent)]
    packed = spread.core_gather(packed)
    return finish(
        block_owner, block_tiles, me.reshape(1), core, packed, gram12, slab, residual, coefficients, base,
        factors, step_size,
    )


def solution(mesh):
    row_spec = P(AXES, None)
    return jax.shard_map(
        local,
        mesh=mesh,
        in_specs=(row_spec, row_spec, row_spec, P(), P()),
        out_specs=(row_spec, row_spec),
        check_vma=False,
    )
```

```python
import functools
import math

import jax
import jax.numpy as jnp
import numpy as np
from jax import lax
from jax.experimental import pallas as pl
from jax.experimental.pallas import tpu as pltpu
from jax.sharding import PartitionSpec as P

BLOCK = 512
TILE = 128
STEPS = 2
RIDGE = 0.5
AXES = ("rows", "sub")
HIGH = lax.Precision.HIGHEST
NT = (((1,), (1,)), ((), ()))
LOG2E = math.log2(math.e)
VMEM_LIMIT = 16 * 1024 * 1024
SMALL_LIMIT = 12 * 1024 * 1024


def pick_kernel(tiles_ref, core_ref, feat_ref, keep_ref, send_ref, sems):
    per_half = keep_ref.shape[1] // TILE
    copies = []
    for turn, out in enumerate((keep_ref, send_ref)):
        half = core_ref[0] if turn == 0 else 1 - core_ref[0]
        for s in range(STEPS):
            for i in range(per_half):
                source = pl.multiple_of(tiles_ref[s, half * per_half + i] * TILE, TILE)
                copies.append(
                    pltpu.make_async_copy(
                        feat_ref.at[pl.ds(source, TILE), :],
                        out.at[s, pl.ds(i * TILE, TILE), :],
                        sems.at[turn, s, i],
                    )
                )
    for copy in copies:
        copy.start()
    for copy in copies:
        copy.wait()


def pick_halves(features, block_tiles, core):
    width = features.shape[1]
    half = jax.ShapeDtypeStruct((STEPS, BLOCK // 2, width), features.dtype)
    return pl.pallas_call(
        pick_kernel,
        grid_spec=pltpu.PrefetchScalarGridSpec(
            num_scalar_prefetch=2,
            grid=(1,),
            in_specs=[pl.BlockSpec(memory_space=pltpu.HBM)],
            out_specs=[pl.BlockSpec(half.shape, lambda i, *_: (0, 0, 0))] * 2,
            scratch_shapes=[pltpu.SemaphoreType.DMA((2, STEPS, BLOCK // 2 // TILE))],
        ),
        out_shape=(half, half),
        compiler_params=pltpu.CompilerParams(vmem_limit_bytes=SMALL_LIMIT),
        name="pick",
    )(pltpu.with_memory_space_constraint(block_tiles, pltpu.HBM), core, pltpu.with_memory_space_constraint(features, pltpu.HBM))


def swap(value, axes, flip):
    flip_of = flip if callable(flip) else lambda i: flip
    return lax.ppermute(value, axes, [(i, i ^ flip_of(i)) for i in range(lax.axis_size(axes))])


def bit_of(index, mask):
    return ((index & mask) != 0).astype(jnp.int32)


def swap_among(pick, me, axes, low, high):
    place = (bit_of(me, low) + 2 * bit_of(me, high)).astype(jnp.uint32)
    flips = [0, low, high, low | high]
    return place, [swap(pick(place ^ np.uint32(c)), axes, flips[c]) for c in (1, 2, 3)]


def ordered(parts, me, low, high, axis):
    one, two = (me & low) != 0, (me & high) != 0
    parts = [jnp.where(one, parts[c ^ 1], parts[c]) for c in range(4)]
    return jnp.stack([jnp.where(two, parts[c ^ 2], parts[c]) for c in range(4)], axis=axis)


def fetch_blocks(features, prepared, block_owner, block_tiles, me, devices, core):
    width = features.shape[1]
    low, high = 1, 2 * core
    differs = lambda mask: (((block_owner ^ me) & mask) != 0)[:, None, None]
    on_core = (me & core) != 0
    keep, send = pick_halves(features, block_tiles, bit_of(me, core).reshape(1))
    half = jnp.where(differs(core), swap(send, AXES, core), keep)
    quarters = half.reshape(STEPS, 4, BLOCK // 8, width)
    pick = lambda place: lax.dynamic_index_in_dim(quarters, place, 1, False)
    place, got = swap_among(pick, me, AXES, low, high)
    got, prepared = lax.optimization_barrier((got, prepared))
    part = jnp.where(
        differs(high),
        jnp.where(differs(low), got[2], got[1]),
        jnp.where(differs(low), got[0], pick(place)),
    )
    far = [1 << b for b in range(devices.bit_length() - 1) if 1 << b not in (core, low, high)]
    hops = []
    for one, two in zip(far[::2], far[1::2]):
        for first, second in ((one, two), (two, one)):
            flip = lambda i, first=first, second=second: second if i & core else first
            hops.append((flip, jnp.where(on_core, second, first)))
    if len(far) % 2:
        hops.append((far[-1], far[-1]))
    for flip, mask in hops:
        other = swap(part, AXES, flip)
        part = jnp.where(differs(mask), other, part)
    _, got = swap_among(lambda place: part, me, AXES, low, high)
    half = ordered([part] + got, me, low, high, 1)
    half = half.reshape(BLOCK, width)
    return half, swap(half, AXES, core), prepared


def both_halves(half, other, on_core):
    half, other = (value.reshape(STEPS, BLOCK // 2, value.shape[1]) for value in (half, other))
    both = jnp.stack([jnp.where(on_core, other, half), jnp.where(on_core, half, other)], axis=1)
    return both.reshape(STEPS * BLOCK, half.shape[2])


def pack(value, exact):
    high = lax.reduce_precision(value[..., :exact, :], 8, 7)
    low = value[..., :exact, :] - high
    return jnp.concatenate([part.astype(jnp.bfloat16) for part in (high, low, value[..., exact:, :])], axis=-2)


def unpack(value, exact):
    value = value.astype(jnp.float32)
    return jnp.concatenate([value[..., :exact, :] + value[..., exact : 2 * exact, :], value[..., 2 * exact :, :]], axis=-2)


class Spread:
    def __init__(self, axes, core):
        self.axes, self.core = axes, core
        self.me = lax.axis_index(axes).astype(jnp.int32)
        self.near = [1 << b for b in range(3) if 1 << b != core]
        self.far = [1 << b for b in range(3, lax.axis_size(axes).bit_length() - 1)]
        self.count = 8
        self.core_axis = 2 - (core.bit_length() - 1)

    def core_sum(self, packed, exact):
        packed = packed.reshape((2,) * 3 + packed.shape[1:])
        zero, one = (lax.index_in_dim(packed, i, self.core_axis, False) for i in (0, 1))
        bit = (self.me & self.core) != 0
        got = swap(jnp.where(bit, zero, one), self.axes, self.core)
        value = unpack(jnp.where(bit, one, zero), exact) + unpack(got, exact)
        return value.reshape((4,) + value.shape[2:])

    def near_sum(self, value, exact):
        packed = pack(value, exact)
        pick = lambda array, place: lax.dynamic_index_in_dim(array, place, 0, False)
        place, got = swap_among(lambda place: pick(packed, place), self.me, self.axes, *self.near)
        return lambda got: pick(value, place) + unpack(got[0], exact) + unpack(got[1], exact) + unpack(got[2], exact), got

    def far_sum(self, value, exact):
        packed = pack(value, exact)
        _, got = swap_among(lambda place: packed, self.me, self.axes, *self.far)
        return lambda got: value + unpack(got[0], exact) + unpack(got[1], exact) + unpack(got[2], exact), got

    def near_gather(self, value):
        _, got = swap_among(lambda place: value, self.me, self.axes, *self.near)
        return lambda got: ordered([value] + got, self.me, *self.near, 0), got

    def core_gather(self, value):
        rest = value.shape[1:]
        value = value.reshape((2, 2) + rest)
        bit = (self.me & self.core) != 0
        got = swap(value, self.axes, self.core)
        value = jnp.stack([jnp.where(bit, got, value), jnp.where(bit, value, got)], axis=self.core_axis)
        return value.reshape((self.count,) + rest)


def scaled_norm(rows, scale):
    wide = rows.astype(jnp.float32)
    return jnp.sum(wide * wide, axis=1, keepdims=True) * scale


def kernel_of(left, right, scale):
    dots = lax.dot_general(left, right, NT, preferred_element_type=jnp.float32)
    row = jnp.transpose(jnp.broadcast_to(scaled_norm(right, scale), (BLOCK, 128)))[:1]
    return jnp.exp(dots * (2.0 * scale) - scaled_norm(left, scale) - row)


def gram_kernel(scale, core_ref, block_ref, slab0_ref, slab1_ref, own_ref):
    mine = block_ref[pl.ds(pl.multiple_of(core_ref[0] * BLOCK, BLOCK), BLOCK), :]
    diagonal = lax.broadcasted_iota(jnp.int32, (BLOCK, BLOCK), 0) == lax.broadcasted_iota(jnp.int32, (BLOCK, BLOCK), 1)
    own_ref[...] = kernel_of(mine, mine, scale) + jnp.where(diagonal, RIDGE, 0.0)


def gram(block, core, scale, slab):
    vmem = pl.BlockSpec(memory_space=pltpu.VMEM)
    return pl.pallas_call(
        functools.partial(gram_kernel, scale),
        in_specs=[pl.BlockSpec(memory_space=pltpu.SMEM)] + [vmem] * 3,
        out_shape=jax.ShapeDtypeStruct((BLOCK, BLOCK), jnp.float32),
        compiler_params=pltpu.CompilerParams(vmem_limit_bytes=SMALL_LIMIT),
        cost_estimate=pl.CostEstimate(
            flops=2 * BLOCK**3, bytes_accessed=4 * BLOCK * BLOCK * 2, transcendentals=BLOCK**2
        ),
        name="gram",
    )(core, block, *map(in_vmem, slab))


def load_kernel(scale, chunk, feat_in, res_in, coef_in, norm_ref, feat_ref, res_ref, coef_ref, sems, more_sems):
    chunks = feat_in.shape[0] // chunk
    rows_of = lambda i: pl.ds(pl.multiple_of(i * chunk, chunk), chunk)

    def load(i):
        return pltpu.make_async_copy(feat_in.at[rows_of(i), :], feat_ref.at[rows_of(i), :], sems.at[i])

    others = [
        pltpu.make_async_copy(source, target, more_sems.at[i])
        for i, (source, target) in enumerate(((res_in, res_ref), (coef_in, coef_ref)))
    ]
    for i in range(chunks):
        load(i).start()
    for copy in others:
        copy.start()
    ones = jnp.ones((16, feat_in.shape[1]), jnp.bfloat16)

    def body(i, _):
        load(i).wait()
        wide = feat_ref[rows_of(i), :].astype(jnp.float32)
        square = wide * wide
        high = square.astype(jnp.bfloat16)
        low = (square - high.astype(jnp.float32)).astype(jnp.bfloat16)
        sums = [lax.dot_general(ones, part, NT, preferred_element_type=jnp.float32) for part in (high, low)]
        norm_ref[:, rows_of(i)] = (sums[0] + sums[1])[:1] * scale
        return 0

    lax.fori_loop(0, chunks, body, 0)
    for copy in others:
        copy.wait()


def load_all(features, residual, coefficients, scale, chunk=512):
    rows = features.shape[0]
    arrays = (features, residual, coefficients)
    vmem, hbm = pl.BlockSpec(memory_space=pltpu.VMEM), pl.BlockSpec(memory_space=pltpu.HBM)
    return pl.pallas_call(
        functools.partial(load_kernel, scale, chunk),
        in_specs=[hbm] * 3,
        out_specs=(vmem,) * 4,
        out_shape=(jax.ShapeDtypeStruct((1, rows), jnp.float32),)
        + tuple(pltpu.VMEM(value.shape, value.dtype) for value in arrays),
        scratch_shapes=[pltpu.SemaphoreType.DMA((rows // chunk,)), pltpu.SemaphoreType.DMA((2,))],
        compiler_params=pltpu.CompilerParams(vmem_limit_bytes=SMALL_LIMIT),
        cost_estimate=pl.CostEstimate(flops=3 * 10**9, bytes_accessed=8 * 1024 * 1024, transcendentals=0),
        name="load",
    )(*(pltpu.with_memory_space_constraint(value, pltpu.HBM) for value in arrays))


def slab_kernel(scale, chunk, *refs):
    refs = list(refs)
    ahead_ref, bnorm, grad = refs[-3], refs[-2], refs[-1]
    second = len(refs) > 10
    half_ref, feat_ref, norm_ref, res_ref, coef_ref = refs[:5]
    if second:
        core_ref, first_slab, first_grad, slab_ref, piece_ref, grads, cross = refs[5:12]
        cross[...] = jnp.zeros_like(cross)
    else:
        slab_ref = refs[5]
    scale2 = scale * LOG2E
    part = BLOCK // 2
    bnorm[...] = jnp.broadcast_to(scaled_norm(half_ref[...], scale2), bnorm.shape)
    grad[...] = jnp.zeros_like(grad)
    chunks = feat_ref.shape[0] // chunk
    rows_of = lambda i: pl.ds(pl.multiple_of(i * chunk, chunk), chunk)
    at_of = lambda p: slice(p * part, (p + 1) * part)

    def product(i, p):
        return lax.dot_general(half_ref[at_of(p)], feat_ref[rows_of(i), :], NT, preferred_element_type=jnp.float32)

    ahead_ref[...] = product(0, 0)

    def body(i, _):
        rows = rows_of(i)
        weighted = (res_ref[rows, :] - RIDGE * coef_ref[rows, :]).astype(jnp.bfloat16)
        norm_row = norm_ref[:, rows] * LOG2E
        dots = ahead_ref[...]
        for p in range(STEPS):
            ahead = product(i, p + 1) if p + 1 < STEPS else product(jnp.minimum(i + 1, chunks - 1), 0)
            norm_wide = jnp.concatenate([bnorm[at_of(p)]] * (chunk // bnorm.shape[1]), axis=1)
            slab = jnp.exp2(dots * (2.0 * scale2) - norm_wide - norm_row).astype(jnp.bfloat16)
            slab_ref[at_of(p), rows] = slab
            if p == 0:
                grad[...] += jnp.dot(slab, weighted, preferred_element_type=jnp.float32)
            dots = ahead
        ahead_ref[...] = dots
        if second:
            left = [first_slab[at_of(0), rows], slab_ref[at_of(0), rows], jnp.transpose(weighted)]
            right = [first_slab[at_of(1), rows], slab_ref[at_of(1), rows]]
            cross[...] += lax.dot_general(
                jnp.concatenate(left, axis=0), jnp.concatenate(right, axis=0), NT, preferred_element_type=jnp.float32
            )
        return 0

    lax.fori_loop(0, chunks, body, 0, unroll=4)
    if not second:
        refs[6][...] = grad[...]
        return
    grads[:, at_of(0)] = jnp.transpose(first_grad[...])
    grads[:, at_of(1)] = jnp.transpose(grad[...])
    grads[:, BLOCK:] = cross[BLOCK:]
    groups = piece_ref.shape[0]
    own, depth = grads.shape[0] // groups, BLOCK // groups
    exact = STEPS * own
    place = lambda h: ((1 - core_ref[0]) if h else core_ref[0]) * part
    lanes = lambda base, h: pl.ds(pl.multiple_of(base + place(h), part), part)
    for h in range(2):
        to = at_of(h)
        for s in range(STEPS):
            value = grads[:, lanes(s * BLOCK, h)]
            high = value.astype(jnp.bfloat16)
            low = (value - high.astype(jnp.float32)).astype(jnp.bfloat16)
            for d in range(groups):
                here = slice(d * own, (d + 1) * own)
                piece_ref[d, s * own : (s + 1) * own, to] = high[here]
                piece_ref[d, exact + s * own : exact + (s + 1) * own, to] = low[here]
        for d in range(groups):
            row = place(d * depth // part) + d * depth % part
            value = cross[pl.ds(pl.multiple_of(row, depth), depth), lanes(0, h)]
            piece_ref[d, 2 * exact :, to] = value.astype(jnp.bfloat16)


def in_vmem(value):
    return pltpu.with_memory_space_constraint(value, pltpu.VMEM)


def slabs(half, features, norms, residual, coefficients, scale, groups=0, core=None, first=(), chunk=512):
    rows, width = features.shape
    targets = residual.shape[1]
    vmem = pl.BlockSpec(memory_space=pltpu.VMEM)
    slab = pltpu.VMEM((BLOCK, rows), jnp.bfloat16)
    inputs = [half, in_vmem(features), norms, in_vmem(residual), in_vmem(coefficients)]
    in_specs = [vmem] * 5
    scratch = [
        pltpu.VMEM((BLOCK // 2, chunk), jnp.float32),
        pltpu.VMEM((BLOCK, 128), jnp.float32),
        pltpu.VMEM((BLOCK // 2, targets), jnp.float32),
    ]
    out = jax.ShapeDtypeStruct((BLOCK // 2, targets), jnp.float32)
    if first:
        piece = (groups, 2 * STEPS * targets // groups + BLOCK // groups, BLOCK)
        out = jax.ShapeDtypeStruct(piece, jnp.bfloat16)
        inputs += [core, in_vmem(first[0]), first[1]]
        in_specs += [pl.BlockSpec(memory_space=pltpu.SMEM), vmem, vmem]
        scratch = [
            pltpu.VMEM((targets, STEPS * BLOCK), jnp.float32),
            pltpu.VMEM((BLOCK + targets, BLOCK), jnp.float32),
        ] + scratch
    return pl.pallas_call(
        functools.partial(slab_kernel, scale, chunk),
        in_specs=in_specs,
        out_shape=(slab, out),
        scratch_shapes=scratch,
        compiler_params=pltpu.CompilerParams(vmem_limit_bytes=VMEM_LIMIT),
        cost_estimate=pl.CostEstimate(
            flops=2 * rows * BLOCK * (width + targets + (BLOCK if first else 0)),
            bytes_accessed=rows * (width * 2 + targets * 8 + BLOCK * 2),
            transcendentals=rows * BLOCK,
        ),
        name="slabs",
    )(*inputs)


def eliminate(tiles, t, lane, scaled_ref, waiting):
    start, shape = 8 * t, tiles[t].shape
    wide = lambda tile, k: jnp.broadcast_to(tile[:, start + k : start + k + 1], shape)
    rows = [jnp.broadcast_to(tiles[t][k : k + 1], shape) for k in range(8)]
    at = {(i, k): wide(rows[i], k) for i in range(8) for k in range(i, 8)}
    units = [jnp.where(lane == start + k, 1.0, 0.0) for k in range(8)]
    rows = [row + unit for row, unit in zip(rows, units)]
    total, lower = [None] * 8, {}
    waiting, share = list(waiting), -(-len(waiting) // 4)
    for r in range(0, 8, 2):
        p, m, q = at[r, r], at[r, r + 1], at[r + 1, r + 1]
        det = p * q - m * m
        guess = pl.reciprocal(det, approx=True)
        for _ in range(min(share, len(waiting))):
            waiting.pop(0)()
        refine = 2.0 - det * guess
        inverse = guess * refine
        for k in range(r + 2, 8):
            first = q * at[r, k] - m * at[r + 1, k]
            second = p * at[r + 1, k] - m * at[r, k]
            lower[r, k], lower[r + 1, k] = first * inverse, second * inverse
            for i in range(r + 2, k + 1):
                product = at[r, i] * first + at[r + 1, i] * second
                change = product * guess * refine if k < r + 4 else product * inverse
                at[i, k] = at[i, k] - change
            rows[k] = rows[k] - (first * rows[r] + second * rows[r + 1]) * inverse
        total[r] = (q * rows[r] - m * rows[r + 1]) * inverse
        total[r + 1] = (p * rows[r + 1] - m * rows[r]) * inverse
    for r in (4, 2, 0):
        for k in range(7, r + 1, -1):
            total[r] = total[r] - lower[r, k] * total[k]
            total[r + 1] = total[r + 1] - lower[r + 1, k] * total[k]
    for k in range(8):
        scaled_ref[start + k : start + k + 1] = total[k][:1] - units[k][:1]

    def update(u):
        parts = [wide(tiles[u], k) * total[k] for k in range(8)]
        while len(parts) > 1:
            parts = [x + y for x, y in zip(parts[::2], parts[1::2])]
        tiles[u] = tiles[u] - parts[0]

    if t + 1 < len(tiles):
        update(t + 1)
    return [functools.partial(update, u) for u in range(t + 2, len(tiles))]


def factor_kernel(index, copied, scale, *refs):
    refs = list(refs)
    rest_ref, _, _ = refs.pop(0), refs.pop(0), refs.pop(0)
    before_ref = refs.pop(0) if index else None
    scaled = refs.pop()
    if copied:
        sem = refs.pop()
        copy = pltpu.make_async_copy(refs.pop(0), refs.pop(), sem)
        copy.start()
    if index == 1:
        block_ref, cross_ref = refs.pop(0), refs.pop()
        cross_ref[...] = kernel_of(block_ref[:BLOCK], block_ref[BLOCK:], scale).astype(cross_ref.dtype)
    factor_ref = refs[0]
    here = slice(index * TILE, (index + 1) * TILE)
    dot = functools.partial(lax.dot_general, precision=HIGH, preferred_element_type=jnp.float32)
    plain = (((1,), (0,)), ((), ()))

    def updated(rows):
        if not index:
            return rest_ref[rows]
        then = slice((index - 1) * TILE, index * TILE)
        old = rest_ref[rows]
        inside = lax.broadcasted_iota(jnp.int32, old.shape, 1) // TILE == index - 1
        return jnp.where(inside, 0.0, old) - dot(rest_ref[rows, then], before_ref[TILE:], plain)

    first = TILE if index == 1 else 0
    factor_ref[:TILE] = updated(slice(first, first + TILE))
    row_ids = lax.broadcasted_iota(jnp.int32, (TILE, TILE), 0)
    col_ids = lax.broadcasted_iota(jnp.int32, (TILE, TILE), 1)
    lane = lax.broadcasted_iota(jnp.int32, (8, TILE), 1)
    tiles = [factor_ref[8 * t : 8 * t + 8, here] for t in range(TILE // 8)]
    if len(refs) > 1:
        refs[1][...] = updated(slice(first + TILE, rest_ref.shape[0]))
    waiting = []
    for t in range(TILE // 8):
        waiting = eliminate(tiles, t, lane, scaled, waiting)
    start = row_ids - row_ids % 8
    lower = jnp.where(col_ids < start, jnp.concatenate(tiles, axis=0), 0.0)
    lower = lower + jnp.where(col_ids == row_ids, 1.0, 0.0)
    right = jnp.where(col_ids < start + 8, scaled[...], 0.0)
    inv = dot(lower, right, (((0,), (0,)), ((), ())))
    panel = dot(inv, factor_ref[:TILE], plain)
    inside = lax.broadcasted_iota(jnp.int32, panel.shape, 1) // TILE == index
    factor_ref[TILE:] = jnp.where(inside, jnp.concatenate([inv] * (BLOCK // TILE), axis=1), panel)
    if copied:
        copy.wait()


def factor_step(rest, index, slab, before=None, copied=None, block=None, scale=None):
    left = BLOCK - (index + 1) * TILE
    vmem, hbm = pl.BlockSpec(memory_space=pltpu.VMEM), pl.BlockSpec(memory_space=pltpu.HBM)
    out = [jax.ShapeDtypeStruct((2 * TILE, BLOCK), jnp.float32)]
    inputs, scratch = [rest, *map(in_vmem, slab)], [pltpu.VMEM((TILE, TILE), jnp.float32)]
    if index:
        inputs.append(before)
        if left:
            out.append(jax.ShapeDtypeStruct((left, BLOCK), jnp.float32))
    if block is not None:
        inputs.append(block)
        out.append(jax.ShapeDtypeStruct((BLOCK, BLOCK), jnp.bfloat16))
    in_specs, out_specs = [vmem] * len(inputs), [vmem] * len(out)
    if copied is not None:
        inputs.append(in_vmem(copied))
        in_specs.append(vmem)
        out.append(pltpu.HBM(copied.shape, copied.dtype))
        out_specs.append(hbm)
        scratch.insert(0, pltpu.SemaphoreType.DMA)
    return pl.pallas_call(
        functools.partial(factor_kernel, index, copied is not None, scale),
        in_specs=in_specs,
        out_specs=tuple(out_specs),
        out_shape=tuple(out),
        scratch_shapes=scratch,
        compiler_params=pltpu.CompilerParams(vmem_limit_bytes=SMALL_LIMIT),
        cost_estimate=pl.CostEstimate(flops=6 * 10**9, bytes_accessed=4 * 1024 * 1024, transcendentals=0),
        name="factor",
    )(*inputs)


def apply_inverse(value, refs):
    upto = lambda k: slice(0, k * TILE)
    dot = functools.partial(lax.dot_general, precision=HIGH, preferred_element_type=jnp.float32)
    count = BLOCK // TILE
    middle = [dot(value[:, upto(k + 1)], refs[k][TILE:, upto(k + 1)], NT) for k in range(count)]
    added = {k: dot(middle[k], refs[k][:TILE, upto(k)], (((1,), (0,)), ((), ()))) for k in range(1, count)}
    out = []
    for j in range(count):
        total = middle[j]
        for k in range(j + 1, count):
            total = total + added[k][:, j * TILE : (j + 1) * TILE]
        out.append(total)
    return jnp.concatenate(out, axis=1)


def final_kernel(step_size, chunk, owner_ref, tiles_ref, me_ref, core_ref, packed_ref, gram_ref, slab0_ref, slab1_ref, res_ref, coef_ref, base_ref, *refs):
    factors, refs = refs[: 2 * (BLOCK // TILE)], refs[2 * (BLOCK // TILE) :]
    res_out, coef_out, upd_ref, wide_ref, part_ref, ahead_ref, res_buf, tile_buf, res_sems, tile_sems = refs
    rows, targets = res_ref.shape
    own = targets // packed_ref.shape[0]
    exact = STEPS * own
    count = BLOCK // TILE

    def gradient(s):
        high = packed_ref[:, s * own : (s + 1) * own].astype(jnp.float32)
        low = packed_ref[:, exact + s * own : exact + (s + 1) * own].astype(jnp.float32)
        return (high + low).reshape(targets, BLOCK)

    dot = functools.partial(jnp.dot, preferred_element_type=jnp.float32)
    first = apply_inverse(gradient(0), factors[:count]) * step_size
    high = first.astype(jnp.bfloat16)
    low = (first - high.astype(jnp.float32)).astype(jnp.bfloat16)
    half = BLOCK // 2
    upd_ref[...] = high
    mine, theirs = (pl.ds(pl.multiple_of(c * half, half), half) for c in (core_ref[0], 1 - core_ref[0]))
    mine_high, theirs_high = upd_ref[:, mine], upd_ref[:, theirs]
    for i in range(rows // chunk):
        at = slice(i * chunk, (i + 1) * chunk)
        part_ref[:, at] = dot(mine_high, slab0_ref[:half, at]) + dot(theirs_high, slab1_ref[:half, at])
    cross = packed_ref[:, 2 * exact :].reshape(BLOCK, BLOCK)
    block_part = dot(high, gram_ref[...]) + dot(low, gram_ref[...])
    again = gradient(1) - dot(high, cross) - RIDGE * block_part
    second = apply_inverse(again, factors[count:]) * step_size
    wide_ref[:, :BLOCK] = first
    wide_ref[:, BLOCK:] = second
    upd_ref[...] = second.astype(jnp.bfloat16)

    def change_of(s, k):
        at = s * BLOCK + k * TILE
        return jnp.transpose(wide_ref[:, at : at + TILE])

    def tile_rows(s, k):
        return pl.ds(pl.multiple_of(tiles_ref[s, k] * TILE, TILE), TILE)

    def tile_copy(s, k):
        return pltpu.make_async_copy(tile_buf.at[s, k], coef_out.at[tile_rows(s, k), :], tile_sems.at[s, k])

    owned = [owner_ref[s] == me_ref[0] for s in range(STEPS)]

    def writes(s, k):
        kept = owned[s]
        for later in range(s + 1, STEPS):
            for j in range(count):
                kept = kept & jnp.logical_not(owned[later] & (tiles_ref[later, j] == tiles_ref[s, k]))
        return kept

    for s in range(STEPS):
        for k in range(count):

            @pl.when(writes(s, k))
            def _():
                tile_buf[s, k] = coef_ref[tile_rows(s, k), :] + change_of(s, k)
                for earlier in range(s):
                    for j in range(count):

                        @pl.when(owned[earlier] & (tiles_ref[earlier, j] == tiles_ref[s, k]))
                        def _():
                            tile_buf[s, k] += change_of(earlier, j)

                tile_copy(s, k).start()

    chunks = rows // chunk
    rows_of = lambda i: pl.ds(pl.multiple_of(i * chunk, chunk), chunk)

    def res_copy(i):
        return pltpu.make_async_copy(res_buf.at[rows_of(i), :], res_out.at[rows_of(i), :], res_sems.at[i])

    def product(i):
        change = dot(upd_ref[:, mine], slab0_ref[half:, rows_of(i)])
        return part_ref[:, rows_of(i)] + change + dot(upd_ref[:, theirs], slab1_ref[half:, rows_of(i)])

    ahead_ref[...] = product(0)

    def body(i, _):
        change = ahead_ref[...]
        ahead = product(jnp.minimum(i + 1, chunks - 1))
        res_buf[rows_of(i), :] = res_ref[rows_of(i), :] - jnp.transpose(change)
        ahead_ref[...] = ahead
        res_copy(i).start()
        return 0

    lax.fori_loop(0, chunks, body, 0, unroll=4)
    for i in range(rows // chunk):
        res_copy(i).wait()
    for s in range(STEPS):
        for k in range(count):

            @pl.when(writes(s, k))
            def _():
                tile_copy(s, k).wait()


def finish(owner, tiles, me, core, packed, gram12, slab, residual, coefficients, base, factors, step_size, chunk=512):
    rows, targets = residual.shape
    both = STEPS * BLOCK
    count = BLOCK // TILE
    smem, vmem, hbm = (pl.BlockSpec(memory_space=space) for space in (pltpu.SMEM, pltpu.VMEM, pltpu.HBM))
    return pl.pallas_call(
        functools.partial(final_kernel, step_size, chunk),
        in_specs=[smem] * 4 + [vmem] * 6 + [hbm] + [vmem] * len(factors),
        out_specs=(hbm, hbm),
        out_shape=(
            pltpu.HBM(residual.shape, jnp.float32),
            pltpu.HBM(residual.shape, jnp.float32),
        ),
        scratch_shapes=[
            pltpu.VMEM((targets, BLOCK), jnp.bfloat16),
            pltpu.VMEM((targets, both), jnp.float32),
            pltpu.VMEM((targets, rows), jnp.float32),
            pltpu.VMEM((targets, chunk), jnp.float32),
            pltpu.VMEM((rows, targets), jnp.float32),
            pltpu.VMEM((STEPS, count, TILE, targets), jnp.float32),
            pltpu.SemaphoreType.DMA((rows // chunk,)),
            pltpu.SemaphoreType.DMA((STEPS, count)),
        ],
        input_output_aliases={10: 1},
        compiler_params=pltpu.CompilerParams(vmem_limit_bytes=VMEM_LIMIT),
        cost_estimate=pl.CostEstimate(
            flops=2 * rows * both * targets, bytes_accessed=rows * (both * 2 + targets * 16), transcendentals=0
        ),
        name="finish",
    )(owner, tiles, me, core, packed, gram12, *map(in_vmem, slab), in_vmem(residual), in_vmem(coefficients), base, *factors)


def local(features, residual, coefficients, block_owner, block_tiles):
    rows_dev, width = features.shape
    targets = residual.shape[1]
    sub_count = lax.axis_size("sub")
    devices = lax.axis_size("rows") * sub_count
    me = lax.axis_index(AXES).astype(jnp.int32)
    scale = 1.0 / width
    step_size = 1.0 / math.sqrt(rows_dev * devices)
    spread = Spread(AXES, sub_count) if devices <= 32 else Spread(("rows",), 1)
    groups = spread.count
    own = targets // groups

    loaded = load_all(features, residual, coefficients, scale)
    half, other, loaded = fetch_blocks(features, loaded, block_owner, block_tiles, me, devices, sub_count)
    norms, features, residual, coefficients = loaded
    core, on_core = bit_of(me, sub_count).reshape(1), (me & sub_count) != 0
    first = slabs(half, features, norms, residual, coefficients, scale)
    other, first = lax.optimization_barrier((other, first))
    last = slabs(other, features, norms, residual, coefficients, scale, groups, core, first)
    slab, pieces = (first[0], last[0]), last[1]
    block = both_halves(half, other, on_core)
    exact = STEPS * own
    if spread.axes != AXES:
        pieces = pack(lax.psum(unpack(pieces, exact), "sub"), exact)
    rest = gram(block, core, scale, slab)
    kept, sent, before, extra = [], [], None, []

    def beside(hop, indices):
        nonlocal before, rest, sent
        then, got = hop
        for index in indices:
            args = {0: {"copied": coefficients}, 1: {"block": block, "scale": scale}}.get(index, {})
            mine, *given = factor_step(rest, index, slab, before, **args)
            if args:
                extra.append(given.pop())
            if index == indices[-1]:
                got, mine, given, sent = lax.optimization_barrier((got, mine, given, sent))
            before, rest = mine, given[0] if given else rest
            sent = sent + [swap(mine, AXES, sub_count)]
            kept.append(mine)
        return then(got)

    value = spread.core_sum(pieces, exact)
    value = beside(spread.near_sum(value, exact), [0])
    value = beside(spread.far_sum(value, exact), [1, 2])
    packed = beside(spread.near_gather(pack(value, exact)), [3])
    base, gram12 = extra
    factors = [jnp.where(on_core, other, mine) for mine, other in zip(kept, sent)]
    factors += [jnp.where(on_core, mine, other) for mine, other in zip(kept, sent)]
    packed = spread.core_gather(packed)
    return finish(
        block_owner, block_tiles, me.reshape(1), core, packed, gram12, slab, residual, coefficients, base,
        factors, step_size,
    )


def solution(mesh):
    row_spec = P(AXES, None)
    return jax.shard_map(
        local,
        mesh=mesh,
        in_specs=(row_spec, row_spec, row_spec, P(), P()),
        out_specs=(row_spec, row_spec),
        check_vma=False,
    )
```
